256 devices in a mesh: wide: 16 (over z_hi, y), col: 16 (over x, z_lo, core).
Axes of the slice: x: 4, y: 4, z: 8 (z_hi: 4, z_lo: 2; z = z_hi * 2 + z_lo), core: 2. Of those that a mesh axis runs over, the one named last changes fastest.
Arguments:
- object_field: float32 [2, 8192, 8192], P(None, 'wide', 'col'), may hold values from -6 to 6
- probe_modes: float32 [2, 4, 128, 128], replicated, may hold values from -3 to 3
- amplitude: bfloat16 [16, 16, 32, 128, 128], P('wide', 'col'), may hold values from 0 to 4
- positions: int32 [16, 16, 32, 2], P('wide', 'col'), may hold values from 0 to 511
- slot_counts: int32 [16, 16], P('wide', 'col'), may hold values from 4 to 32, as said below
Outputs:
- new_object: float32 [2, 8192, 8192], P(None, 'wide', 'col')
- probe_direction: float32 [2, 4, 128, 128], replicated
The draws below stay inside these ranges and needn't reach their ends.
Inputs may be any that keep to these rules, and one draw needn't show every extreme that they name: `positions`: offsets lie inside the device's own tile. The live slots of a device are its first slot_counts[w, c] slots; at least one device has all 32 slots live.
All inputs are finite; a program needn't handle non-finite values.
Results may differ from the reference program's by a relative error of at most 0.0017.
The reference program's roundings to bfloat16 on the way (of `tables`, `exit_wave`, `half`, `residual_wave` and `half_back`) count: a program that leaves them out, or rounds other values in their place, can miss the bound.
Values sent between devices are 32-bit elements; how exact they have to be, the bound alone decides.
A program may use at most 128 MiB of HBM per device.

```python
import math
import jax
import jax.numpy as jnp
from jax import lax

PATCH = 128
MODES = 4
TILE = 512
SLOTS = 32
OBJ_ROWS = 8192
OBJ_COLS = 8192
N_WIDE = 16
N_COL = 16


def draw_slot_counts(key, part):
    key = jax.random.fold_in(key, 7)
    key_halve, key_full = jax.random.split(key)
    halvings = jax.random.randint(key_halve, (N_WIDE, N_COL), 0, 4)
    counted = SLOTS // jnp.power(2, halvings).astype(jnp.int32)
    fullest = jax.random.randint(key_full, (), 0, N_WIDE * N_COL)
    flat_counts = counted.reshape(-1).at[fullest].set(SLOTS)
    return flat_counts.reshape(N_WIDE, N_COL).astype(jnp.int32)


def set_ends(drawn, own_key, low, top_value):
    longest = drawn.shape.index(max(drawn.shape))
    spots = []
    for shift in (0, 1):
        where = [jax.random.randint(jax.random.fold_in(own_key, axis), (), 0, length) for axis, length in enumerate(drawn.shape)]
        where[longest] = (where[longest] + shift) % drawn.shape[longest]
        spots.append(tuple(where))
    return drawn.at[spots[0]].set(low).at[spots[1]].set(top_value)


def level_of(rng, dims, pieces, low, top_value):
    loudness, own = 1.0, jax.random.fold_in(rng, 6)
    for dim, shards_of in pieces:
        draws = jnp.exp(jax.random.uniform(jax.random.fold_in(own, dim), (shards_of,), jnp.float32, low / len(pieces), top_value / len(pieces)))
        loudness = loudness * jnp.repeat(draws, dims[dim] // shards_of).reshape([-1 if axis == dim else 1 for axis in range(len(dims))])
    return loudness


def bell_draw(own_key, extent, scale, limit, shards=(), held_as=jnp.bfloat16):
    result = scale * jax.random.normal(own_key, extent, jnp.float32)
    if shards:
        result = result * level_of(own_key, extent, shards, -0.22, 0.18)
    return jnp.clip(result, -limit, limit).astype(held_as)


def setup_inputs(seed: int = 0) -> dict:
    keys = jax.random.split(jax.random.key(seed), 6)
    object_field = bell_draw(keys[0], (2, OBJ_ROWS, OBJ_COLS), 1.0, 6.0, ((1, 16), (2, 16)), jnp.float32)
    probe_modes = bell_draw(keys[1], (2, MODES, PATCH, PATCH), 0.5, 3.0, (), jnp.float32)
    amplitude = jnp.clip(4.0 * jax.random.uniform(keys[2], (N_WIDE, N_COL, SLOTS, PATCH, PATCH), jnp.float32) ** level_of(keys[2], (N_WIDE, N_COL, SLOTS, PATCH, PATCH), ((0, 16), (1, 16)), -0.2, 0.2), 0.0, 4.0).astype(jnp.bfloat16)
    positions = set_ends(jax.random.randint(keys[3], (N_WIDE, N_COL, SLOTS, 2), 0, TILE), jax.random.fold_in(keys[3], 1), 0, TILE - 1).astype(jnp.int32)
    slot_counts = draw_slot_counts(jax.random.fold_in(keys[5], 71), 0)
    return dict(object_field=object_field, probe_modes=probe_modes, amplitude=amplitude, positions=positions, slot_counts=slot_counts)


def rounded(values):
    return lax.optimization_barrier(values.astype(jnp.bfloat16)).astype(jnp.float32)

def dft_tables(length, sign_value):
    indices = jnp.arange(length, dtype=jnp.int32)
    product = indices[:, None] * indices[None, :] % length
    angles = product.astype(jnp.float32) * (2.0 * math.pi / length)
    factor = 1.0 / math.sqrt(length)
    cosine = jnp.cos(angles) * factor
    sine = -sign_value * jnp.sin(angles) * factor
    left_table = jnp.stack([jnp.stack([cosine, -sine], 1), jnp.stack([sine, cosine], 1)], 0)
    right_table = jnp.transpose(left_table, (2, 3, 0, 1))
    return (rounded(left_table), rounded(right_table))

def patch_terms(patches, probe_modes, block_amps, valid, tables):
    fwd_left, fwd_right, inv_left, inv_right = tables
    probe_re = probe_modes[0][None]
    probe_im = probe_modes[1][None]
    patch_re = patches[:, 0][:, None]
    patch_im = patches[:, 1][:, None]
    exit_re = probe_re * patch_re - probe_im * patch_im
    exit_im = probe_re * patch_im + probe_im * patch_re
    exit_wave = rounded(jnp.stack([exit_re, exit_im], 2))
    half = rounded(jnp.einsum('cjdk,bmdkl->bmcjl', fwd_left, exit_wave))
    farfield = jnp.einsum('bmdjk,dkcl->bmcjl', half, fwd_right)
    intensity = lax.optimization_barrier(jnp.sum(farfield * farfield, axis=(1, 2)))
    factor = (block_amps.astype(jnp.float32) / jnp.sqrt(jnp.maximum(intensity, 1.0)) - 1.0) * valid[:, None, None]
    residual_wave = rounded(farfield * factor[:, None, None])
    half_back = rounded(jnp.einsum('cjdk,bmdkl->bmcjl', inv_left, residual_wave))
    update = jnp.einsum('bmdjk,dkcl->bmcjl', half_back, inv_right)
    update_re = update[:, :, 0]
    update_im = update[:, :, 1]
    grad_re = lax.optimization_barrier(jnp.sum(probe_re * update_re + probe_im * update_im, axis=1))
    grad_im = lax.optimization_barrier(jnp.sum(probe_re * update_im - probe_im * update_re, axis=1))
    patch_grad = jnp.stack([grad_re, grad_im], 1)
    patch_weight = valid[:, None, None] * lax.optimization_barrier(jnp.sum(probe_modes * probe_modes, axis=(0, 1)))[None]
    term_re = lax.optimization_barrier(jnp.sum(patch_re * update_re + patch_im * update_im, axis=0))
    term_im = lax.optimization_barrier(jnp.sum(patch_re * update_im - patch_im * update_re, axis=0))
    probe_term = jnp.stack([term_re, term_im], 0)
    illum_term = lax.optimization_barrier(jnp.sum(valid[:, None, None] * (patches[:, 0] * patches[:, 0] + patches[:, 1] * patches[:, 1]), axis=0))
    return (patch_grad, patch_weight, probe_term, illum_term)

def reference(object_field, probe_modes, amplitude, positions, slot_counts):
    fwd_left, fwd_right = dft_tables(PATCH, 1.0)
    inv_left, inv_right = dft_tables(PATCH, -1.0)
    tables = (fwd_left, fwd_right, inv_left, inv_right)
    padded = jnp.pad(object_field, ((0, 0), (0, PATCH), (0, PATCH)))
    device_count = N_WIDE * N_COL
    all_positions = positions.reshape(device_count, SLOTS, 2)
    all_amps = amplitude.reshape(device_count, SLOTS, PATCH, PATCH)
    all_live = slot_counts.reshape(device_count)
    device_ids = jnp.arange(device_count, dtype=jnp.int32)
    anchor_rows = device_ids // N_COL * TILE
    anchor_cols = device_ids % N_COL * TILE
    offsets = jnp.arange(PATCH, dtype=jnp.int32)
    slot_ids = jnp.arange(SLOTS, dtype=jnp.int32)

    def advance(totals, device_item):
        grad_total, weight_total, probe_total, illum_total = totals
        chosen, block_amps, live_slots, row_anchor, col_anchor = device_item
        row_index = (chosen[:, 0][:, None] + row_anchor + offsets[None])[:, :, None]
        col_index = (chosen[:, 1][:, None] + col_anchor + offsets[None])[:, None, :]
        patches = jnp.moveaxis(padded[:, row_index, col_index], 1, 0)
        valid = (slot_ids < live_slots).astype(jnp.float32)
        patch_grad, patch_weight, probe_term, illum_term = patch_terms(patches, probe_modes, block_amps, valid, tables)
        grad_total = grad_total.at[:, row_index, col_index].add(jnp.moveaxis(patch_grad, 1, 0))
        weight_total = weight_total.at[row_index, col_index].add(patch_weight)
        return ((grad_total, weight_total, probe_total + probe_term, illum_total + illum_term), None)
    initial = (jnp.zeros(padded.shape, jnp.float32), jnp.zeros(padded.shape[1:], jnp.float32), jnp.zeros(probe_modes.shape, jnp.float32), jnp.zeros((PATCH, PATCH), jnp.float32))
    totals, unused = lax.scan(advance, initial, (all_positions, all_amps, all_live, anchor_rows, anchor_cols))
    grad_total, weight_total, probe_total, illum_total = totals
    object_grad = grad_total[:, :OBJ_ROWS, :OBJ_COLS]
    object_weight = weight_total[:OBJ_ROWS, :OBJ_COLS]
    new_object = object_field + object_grad / (object_weight + 1.0)[None]
    probe_direction = probe_total / jnp.sqrt(illum_total + 1.0)[None, None]
    return (new_object, probe_direction)
```

```python
import functools
import math

import jax
import jax.numpy as jnp
import ml_dtypes
import numpy as np
from jax import lax
from jax.experimental import pallas as pl
from jax.experimental.pallas import tpu as pltpu
from jax.sharding import PartitionSpec as P

MESH = pl.DeviceIdType.MESH
F32 = jnp.float32
BF16 = jnp.bfloat16
PATCH = 128
TILE = 512
EXT = TILE + PATCH
MODES = 4
RING = 16
PLANES = 2 * MODES + 1
ROWS = PATCH // RING
PAIR = 2

VMEM_SPEC = pl.BlockSpec(memory_space=pltpu.VMEM)
SMEM_SPEC = pl.BlockSpec(memory_space=pltpu.SMEM)
ANY_SPEC = pl.BlockSpec(memory_space=pl.ANY)


def left_table():
    indices = np.arange(PATCH)
    angles = (indices[:, None] * indices[None, :] % PATCH) * (2.0 * math.pi / PATCH)
    cosine = np.cos(angles) / math.sqrt(PATCH)
    sine = -np.sin(angles) / math.sqrt(PATCH)
    whole = np.block([[cosine, -sine], [sine, cosine]])
    return whole.astype(np.float32).astype(ml_dtypes.bfloat16)


def halo_in_kernel(obj, right, lower, diag, sent, got):
    w = lax.axis_index("wide")
    c = lax.axis_index("col")
    above, below = lax.rem(w + 15, 16), lax.rem(w + 1, 16)
    before, after = lax.rem(c + 15, 16), lax.rem(c + 1, 16)
    barrier = pltpu.get_barrier_semaphore()
    for target in ((w, after), (below, c), (below, after)):
        pl.semaphore_signal(barrier, inc=1, device_id=target, device_id_type=MESH)
    pl.semaphore_wait(barrier, 3)
    copies = (
        (obj.at[:, pl.ds(0, PATCH), :], lower, (above, c), w > 0, w < 15),
        (obj.at[:, :, pl.ds(0, PATCH)], right, (w, before), c > 0, c < 15),
        (
            obj.at[:, pl.ds(0, PATCH), pl.ds(0, PATCH)],
            diag,
            (above, before),
            (w > 0) & (c > 0),
            (w < 15) & (c < 15),
        ),
    )
    made = []
    for k, (source, dest, target, sends, gets) in enumerate(copies):
        copy = pltpu.make_async_remote_copy(
            source, dest, sent.at[k], got.at[k], device_id=target, device_id_type=MESH
        )
        pl.when(sends)(copy.start)
        made.append((copy, sends, gets))
    for copy, sends, gets in made:
        pl.when(gets)(copy.wait_recv)
        pl.when(sends)(copy.wait_send)


def halo_in(obj):
    return pl.pallas_call(
        halo_in_kernel,
        out_shape=[
            jax.ShapeDtypeStruct((2, TILE, PATCH), F32),
            jax.ShapeDtypeStruct((2, PATCH, TILE), F32),
            jax.ShapeDtypeStruct((2, PATCH, PATCH), F32),
        ],
        in_specs=[ANY_SPEC],
        out_specs=[ANY_SPEC] * 3,
        scratch_shapes=[pltpu.SemaphoreType.DMA((3,)), pltpu.SemaphoreType.DMA((3,))],
        compiler_params=pltpu.CompilerParams(collective_id=1, has_side_effects=True),
        name="halo_in",
    )(obj)


def patches_kernel(
    pos_ref, cnt_ref, probe_ref, lt_ref, rt_ref, amp_ref, obj, right, lower, diag,
    gw_ref, pg_ref, ext, sems,
):
    copies = []

    def fetch(source, dest):
        copy = pltpu.make_async_copy(source, dest, sems.at[len(copies)])
        copy.start()
        copies.append(copy)

    for ct in range(4):
        lanes = pl.ds(PATCH * ct, PATCH)
        fetch(obj.at[:, :, lanes], ext.at[:, ct, pl.ds(0, TILE), :])
        fetch(lower.at[:, :, lanes], ext.at[:, ct, pl.ds(TILE, PATCH), :])
    fetch(right, ext.at[:, 4, pl.ds(0, TILE), :])
    fetch(diag, ext.at[:, 4, pl.ds(TILE, PATCH), :])
    gw_ref[...] = jnp.zeros(gw_ref.shape, F32)
    pg_ref[...] = jnp.zeros(pg_ref.shape, F32)
    for copy in copies:
        copy.wait()

    @pl.when(lax.axis_index("wide") == 15)
    def _():
        ext[:, :, TILE:, :] = jnp.zeros((2, 5, PATCH, PATCH), F32)

    @pl.when(lax.axis_index("col") == 15)
    def _():
        ext[:, 4, :, :] = jnp.zeros((2, EXT, PATCH), F32)

    lane = lax.broadcasted_iota(jnp.int32, (PATCH, PATCH), 1)
    count = cnt_ref[0, 0]
    lt = lt_ref[...]
    rt = rt_ref[...]
    power = jnp.sum(probe_ref[...] * probe_ref[...], axis=(0, 1))

    def scatter(plane, row, ct, shift, value):
        turned = pltpu.roll(value, shift, 1)
        first = lane >= shift
        zero = jnp.zeros_like(turned)
        rows = pl.ds(row, PATCH)
        gw_ref[plane, ct, rows, :] += jnp.where(first, turned, zero)
        gw_ref[plane, ct + 1, rows, :] += jnp.where(first, zero, turned)

    def both_sides(left, stacked, right_side):
        half = jnp.dot(left, stacked, preferred_element_type=F32).astype(BF16)
        lanes = [slice(PATCH * m, PATCH * (m + 1)) for m in range(MODES)]
        turned = jnp.concatenate(
            [jnp.concatenate([half[:PATCH, at], half[PATCH:, at]], 1) for at in lanes], 0
        )
        return jnp.dot(turned, right_side, preferred_element_type=F32)

    def stack(re, im):
        return jnp.concatenate([jnp.concatenate(re, 1), jnp.concatenate(im, 1)], 0)

    def parts(values, m):
        rows = slice(PATCH * m, PATCH * (m + 1))
        return values[rows, :PATCH], values[rows, PATCH:]

    def step(index, carry):
        slots = [index * PAIR + u for u in range(PAIR)]
        info, waves = [], []
        for s in slots:
            row, at = pos_ref[s, 0], pos_ref[s, 1]
            ct, shift = lax.shift_right_logical(at, 7), lax.bitwise_and(at, 127)
            back = lax.bitwise_and(PATCH - shift, 127)
            rows = pl.ds(row, PATCH)
            patch = []
            for p in range(2):
                joined = jnp.where(lane >= shift, ext[p, ct, rows, :], ext[p, ct + 1, rows, :])
                patch.append(pltpu.roll(joined, back, 1))
            live = (s < count).astype(F32)
            info.append((row, ct, shift, live, patch))
            re, im = [], []
            for m in range(MODES):
                pr, pi = probe_ref[0, m], probe_ref[1, m]
                re.append((pr * patch[0] - pi * patch[1]).astype(BF16))
                im.append((pr * patch[1] + pi * patch[0]).astype(BF16))
            waves.append(stack(re, im))
        fars = [both_sides(lt, wave, rt) for wave in waves]
        residuals = []
        for u, s in enumerate(slots):
            intensity = jnp.zeros((PATCH, PATCH), F32)
            for m in range(MODES):
                fr, fi = parts(fars[u], m)
                intensity = intensity + fr * fr + fi * fi
            measured = amp_ref[s].astype(F32)
            factor = (measured * lax.rsqrt(jnp.maximum(intensity, 1.0)) - 1.0) * info[u][3]
            re, im = [], []
            for m in range(MODES):
                fr, fi = parts(fars[u], m)
                re.append((fr * factor).astype(BF16))
                im.append((fi * factor).astype(BF16))
            residuals.append(stack(re, im))
        updates = [both_sides(rt, residual, lt) for residual in residuals]
        for m in range(MODES):
            sum_re, sum_im = pg_ref[m], pg_ref[MODES + m]
            for u in range(PAIR):
                patch = info[u][4]
                ur, ui = parts(updates[u], m)
                sum_re = sum_re + patch[0] * ur + patch[1] * ui
                sum_im = sum_im + patch[0] * ui - patch[1] * ur
            pg_ref[m] = sum_re
            pg_ref[MODES + m] = sum_im
        lit = pg_ref[2 * MODES]
        for u in range(PAIR):
            patch = info[u][4]
            lit = lit + info[u][3] * (patch[0] * patch[0] + patch[1] * patch[1])
        pg_ref[2 * MODES] = lit
        for u in range(PAIR):
            row, ct, shift, live, _ = info[u]
            grad_re = jnp.zeros((PATCH, PATCH), F32)
            grad_im = grad_re
            for m in range(MODES):
                pr, pi = probe_ref[0, m], probe_ref[1, m]
                ur, ui = parts(updates[u], m)
                grad_re = grad_re + pr * ur + pi * ui
                grad_im = grad_im + pr * ui - pi * ur
            scatter(0, row, ct, shift, grad_re)
            scatter(1, row, ct, shift, grad_im)
            scatter(2, row, ct, shift, power * live)
        return carry

    lax.fori_loop(0, (count + PAIR - 1) // PAIR, step, 0)


def patches(pos, count, probe, amp, obj, right, lower, diag):
    table = left_table()
    return pl.pallas_call(
        patches_kernel,
        out_shape=[
            jax.ShapeDtypeStruct((3, 5, EXT, PATCH), F32),
            jax.ShapeDtypeStruct((PLANES, PATCH, PATCH), F32),
        ],
        in_specs=[SMEM_SPEC] * 2 + [VMEM_SPEC] * 4 + [ANY_SPEC] * 4,
        out_specs=[VMEM_SPEC] * 2,
        scratch_shapes=[pltpu.VMEM((2, 5, EXT, PATCH), F32), pltpu.SemaphoreType.DMA((10,))],
        compiler_params=pltpu.CompilerParams(vmem_limit_bytes=56 * 2**20),
        name="patches",
    )(pos, count, probe, jnp.asarray(table), jnp.asarray(table.T), amp, obj, right, lower, diag)


def exchange_kernel(
    pg, gw, total, from_above, from_left, from_diag,
    buf1, red1, buf2, red2, own, s1, r1, s2, r2, s3, r3, s4, r4, sh, rh,
):
    w = lax.axis_index("wide")
    c = lax.axis_index("col")
    above, below = lax.rem(w + 15, 16), lax.rem(w + 1, 16)
    before, after = lax.rem(c + 15, 16), lax.rem(c + 1, 16)

    def remote(source, dest, sent, got, target):
        return pltpu.make_async_remote_copy(
            source, dest, sent, got, device_id=target, device_id_type=MESH
        )

    def chunk(index):
        return pl.ds(pl.multiple_of(index * ROWS, ROWS), ROWS)

    barrier = pltpu.get_barrier_semaphore()
    for d in range(1, RING):
        for target in ((w, lax.rem(c + d, 16)), (lax.rem(w + d, 16), c)):
            pl.semaphore_signal(barrier, inc=1, device_id=target, device_id_type=MESH)
    pl.semaphore_signal(barrier, inc=1, device_id=(above, before), device_id_type=MESH)
    pl.semaphore_wait(barrier, 31)

    first = []
    for d in range(1, RING):
        p = lax.rem(c + d, 16)
        copy = remote(pg.at[:, chunk(p), :], buf1.at[d], s1.at[d], r1.at[d], (w, p))
        copy.start()
        first.append(copy)
    halos = (
        (gw.at[:, pl.ds(0, 4), pl.ds(TILE, PATCH), :], from_above, (below, c), w < 15, w > 0),
        (gw.at[:, 4, pl.ds(0, TILE), :], from_left, (w, after), c < 15, c > 0),
        (
            gw.at[:, 4, pl.ds(TILE, PATCH), :],
            from_diag,
            (below, after),
            (w < 15) & (c < 15),
            (w > 0) & (c > 0),
        ),
    )
    strips = []
    for k, (source, dest, target, sends, gets) in enumerate(halos):
        copy = remote(source, dest, sh.at[k], rh.at[k], target)
        pl.when(sends)(copy.start)
        strips.append((copy, sends, gets))
    acc = pg[:, chunk(c), :]
    for d in range(1, RING):
        first[d - 1].wait_recv()
        acc = acc + buf1[d]
    red1[...] = acc

    def to_owner(j):
        return remote(red1.at[j], buf2.at[w], s2.at[j], r2.at[w], (jnp.int32(j), c))

    def at_owner(j):
        return remote(red1.at[0], buf2.at[j], s2.at[0], r2.at[j], (w, c))

    def from_owner(d):
        return remote(red2, own.at[w], s3.at[d], r3.at[w], (lax.rem(w + d, 16), c))

    def at_user(j):
        return remote(red2, own.at[j], s3.at[0], r3.at[j], (w, c))

    for j in range(PLANES):
        @pl.when(w != j)
        def _(j=j):
            to_owner(j).start()

    @pl.when(w < PLANES)
    def _():
        buf2[w] = red1[w]
        for j in range(RING):
            @pl.when(w != j)
            def _(j=j):
                at_owner(j).wait_recv()
        acc2 = buf2[0]
        for j in range(1, RING):
            acc2 = acc2 + buf2[j]
        red2[...] = acc2
        for d in range(1, RING):
            from_owner(d).start()
        own[w] = acc2

    for j in range(PLANES):
        @pl.when(w != j)
        def _(j=j):
            at_user(j).wait_recv()

    fourth = []
    for d in range(1, RING):
        copy = remote(own, total.at[:, chunk(c), :], s4.at[d], r4.at[d], (w, lax.rem(c + d, 16)))
        copy.start()
        fourth.append(copy)
    total[:, chunk(c), :] = own[...]
    for copy in first:
        copy.wait_send()
    for j in range(PLANES):
        @pl.when(w != j)
        def _(j=j):
            to_owner(j).wait_send()

    @pl.when(w < PLANES)
    def _():
        for d in range(1, RING):
            from_owner(d).wait_send()

    for d in range(1, RING):
        p = lax.rem(c + 16 - d, 16)
        remote(own, total.at[:, chunk(p), :], s4.at[d], r4.at[d], (w, p)).wait_recv()
    for copy in fourth:
        copy.wait_send()
    for copy, sends, gets in strips:
        pl.when(gets)(copy.wait_recv)
        pl.when(sends)(copy.wait_send)


def exchange(pg, gw):
    ring = pltpu.SemaphoreType.DMA((RING,))
    three = pltpu.SemaphoreType.DMA((3,))
    return pl.pallas_call(
        exchange_kernel,
        out_shape=[
            jax.ShapeDtypeStruct((PLANES, PATCH, PATCH), F32),
            jax.ShapeDtypeStruct((3, 4, PATCH, PATCH), F32),
            jax.ShapeDtypeStruct((3, TILE, PATCH), F32),
            jax.ShapeDtypeStruct((3, PATCH, PATCH), F32),
        ],
        in_specs=[VMEM_SPEC, ANY_SPEC],
        out_specs=[VMEM_SPEC] + [ANY_SPEC] * 3,
        scratch_shapes=[
            pltpu.VMEM((RING, PLANES, ROWS, PATCH), F32),
            pltpu.VMEM((PLANES, ROWS, PATCH), F32),
            pltpu.VMEM((RING, ROWS, PATCH), F32),
            pltpu.VMEM((ROWS, PATCH), F32),
            pltpu.VMEM((PLANES, ROWS, PATCH), F32),
        ]
        + [ring] * 8
        + [three] * 2,
        compiler_params=pltpu.CompilerParams(collective_id=2, has_side_effects=True),
        name="exchange",
    )(pg, gw)


def finish_kernel(obj, gw, total, from_above, from_left, from_diag, new, direction):
    block = pl.program_id(0)
    w = lax.axis_index("wide")
    c = lax.axis_index("col")
    got_above = (block == 0) & (w > 0)
    got_left = c > 0
    got_diag = got_above & got_left

    @pl.when(block == 0)
    def _():
        direction[...] = total[: 2 * MODES] / jnp.sqrt(total[2 * MODES :] + 1.0)

    for ct in range(4):
        lanes = slice(PATCH * ct, PATCH * (ct + 1))
        sums = gw[:, ct]
        sums = sums + jnp.where(got_above, from_above[:, ct], 0.0)
        if ct == 0:
            sums = sums + jnp.where(got_left, from_left[...], 0.0)
            sums = sums + jnp.where(got_diag, from_diag[...], 0.0)
        weight = sums[2] + 1.0
        for p in range(2):
            new[p, :, lanes] = obj[p, :, lanes] + sums[p] / weight


def finish(obj, gw, total, from_above, from_left, from_diag):
    return pl.pallas_call(
        finish_kernel,
        grid=(4,),
        out_shape=[
            jax.ShapeDtypeStruct((2, TILE, TILE), F32),
            jax.ShapeDtypeStruct((2 * MODES, PATCH, PATCH), F32),
        ],
        in_specs=[
            pl.BlockSpec((2, PATCH, TILE), lambda i: (0, i, 0)),
            pl.BlockSpec((3, 4, PATCH, PATCH), lambda i: (0, 0, i, 0)),
            pl.BlockSpec((PLANES, PATCH, PATCH), lambda i: (0, 0, 0)),
            pl.BlockSpec((3, 4, PATCH, PATCH), lambda i: (0, 0, 0, 0)),
            pl.BlockSpec((3, PATCH, PATCH), lambda i: (0, i, 0)),
            pl.BlockSpec((3, PATCH, PATCH), lambda i: (0, 0, 0)),
        ],
        out_specs=[
            pl.BlockSpec((2, PATCH, TILE), lambda i: (0, i, 0)),
            pl.BlockSpec((2 * MODES, PATCH, PATCH), lambda i: (0, 0, 0)),
        ],
        name="finish",
    )(obj, gw, total, from_above, from_left, from_diag)


def local(object_field, probe_modes, amplitude, positions, slot_counts):
    slots = positions.shape[2]
    right, lower, diag = halo_in(object_field)
    gw, pg = patches(
        positions.reshape(slots, 2),
        slot_counts,
        probe_modes,
        amplitude.reshape(slots, PATCH, PATCH),
        object_field,
        right,
        lower,
        diag,
    )
    total, from_above, from_left, from_diag = exchange(pg, gw)
    new_object, direction = finish(object_field, gw, total, from_above, from_left, from_diag)
    return new_object, direction.reshape(probe_modes.shape)


def solution(mesh):
    placed = (
        P(None, "wide", "col"),
        P(),
        P("wide", "col", None, None, None),
        P("wide", "col", None, None),
        P("wide", "col"),
    )
    return jax.shard_map(
        local, mesh=mesh, in_specs=placed, out_specs=(P(None, "wide", "col"), P()), check_vma=False
    )
```

```python
import functools
import math

import jax
import jax.numpy as jnp
import ml_dtypes
import numpy as np
from jax import lax
from jax.experimental import pallas as pl
from jax.experimental.pallas import tpu as pltpu
from jax.sharding import PartitionSpec as P

MESH = pl.DeviceIdType.MESH
F32 = jnp.float32
BF16 = jnp.bfloat16
PATCH = 128
TILE = 512
EXT = TILE + PATCH
MODES = 4
RING = 16
PLANES = 2 * MODES + 1
ROWS = PATCH // RING
PAIR = 2
CHUNKS = 4

VMEM_SPEC = pl.BlockSpec(memory_space=pltpu.VMEM)
SMEM_SPEC = pl.BlockSpec(memory_space=pltpu.SMEM)
ANY_SPEC = pl.BlockSpec(memory_space=pl.ANY)


def left_table():
    indices = np.arange(PATCH)
    angles = (indices[:, None] * indices[None, :] % PATCH) * (2.0 * math.pi / PATCH)
    cosine = np.cos(angles) / math.sqrt(PATCH)
    sine = -np.sin(angles) / math.sqrt(PATCH)
    whole = np.block([[cosine, -sine], [sine, cosine]])
    return whole.astype(np.float32).astype(ml_dtypes.bfloat16)


def remote(source, dest, sent, got, target):
    return pltpu.make_async_remote_copy(
        source, dest, sent, got, device_id=target, device_id_type=MESH
    )


def greet(barrier, target):
    pl.semaphore_signal(barrier, inc=1, device_id=target, device_id_type=MESH)


def halo_in_kernel(
    obj, meta, right, lower, diag, meta_above, meta_left, meta_diag, passing,
    sent, got, sent_relay, got_relay,
):
    w = lax.axis_index("wide")
    c = lax.axis_index("col")
    y, k = lax.rem(w, 4), lax.div(w, 4)
    above, below = lax.rem(w + 15, 16), lax.rem(w + 1, 16)
    before, after = lax.rem(c + 15, 16), lax.rem(c + 1, 16)
    far_send, far_get = (y == 0) & (k > 0), (y == 3) & (k < 3)
    relays = (y == 3) & (k > 0)
    relay_from, relay_at = lax.rem(w + 13, 16), lax.rem(w + 3, 16)
    relay_to, got_from = lax.rem(w + 12, 16), lax.rem(w + 4, 16)
    barrier = pltpu.get_barrier_semaphore()
    for target in (
        (w, after), (below, c), (below, after), (w, before), (above, c), (above, before)
    ):
        greet(barrier, target)
    pl.when(relays)(lambda: greet(barrier, (relay_from, c)))
    pl.when(far_get)(lambda: greet(barrier, (got_from, c)))
    pl.semaphore_wait(barrier, 6 + jnp.where(far_send | relays, 1, 0))
    top = pl.ds(0, PATCH)
    size = PATCH // CHUNKS
    cuts = [pl.ds(j * size, size) for j in range(CHUNKS)]
    to_relay = [
        remote(
            obj.at[1, cut, :], passing.at[cut, :], sent_relay.at[j], got_relay.at[j], (relay_at, c)
        )
        for j, cut in enumerate(cuts)
    ]
    from_relay = [
        remote(
            passing.at[cut, :], lower.at[1, cut, :],
            sent_relay.at[CHUNKS + j], got_relay.at[CHUNKS + j], (relay_to, c),
        )
        for j, cut in enumerate(cuts)
    ]

    @pl.when(far_send)
    def _():
        for copy in to_relay:
            copy.start()

    ups, downs = w > 0, w < 15
    lefts, rights = c > 0, c < 15
    near_send = ups & jnp.logical_not(far_send)
    near_get = downs & jnp.logical_not(far_get)
    plain = (
        (obj.at[0, top, :], lower.at[0], (above, c), ups, downs),
        (obj.at[1, top, :], lower.at[1], (above, c), near_send, near_get),
        (obj.at[:, :, top], right, (w, before), lefts, rights),
        (obj.at[:, top, top], diag, (above, before), ups & lefts, downs & rights),
        (meta, meta_above, (below, c), downs, ups),
        (meta, meta_left, (w, after), rights, lefts),
        (meta, meta_diag, (below, after), downs & rights, ups & lefts),
    )
    made = []
    for j, (source, dest, target, sends, gets) in enumerate(plain):
        copy = remote(source, dest, sent.at[j], got.at[j], target)
        pl.when(sends)(copy.start)
        made.append((copy, sends, gets))

    @pl.when(relays)
    def _():
        for arrived, onward in zip(to_relay, from_relay):
            arrived.wait_recv()
            onward.start()

    for copy, sends, gets in made:
        pl.when(gets)(copy.wait_recv)
        pl.when(sends)(copy.wait_send)

    @pl.when(far_get)
    def _():
        for copy in from_relay:
            copy.wait_recv()

    @pl.when(relays)
    def _():
        for copy in from_relay:
            copy.wait_send()

    @pl.when(far_send)
    def _():
        for copy in to_relay:
            copy.wait_send()


def halo_in(obj, meta):
    note = jax.ShapeDtypeStruct(meta.shape, meta.dtype)
    return pl.pallas_call(
        halo_in_kernel,
        out_shape=[
            jax.ShapeDtypeStruct((2, TILE, PATCH), F32),
            jax.ShapeDtypeStruct((2, PATCH, TILE), F32),
            jax.ShapeDtypeStruct((2, PATCH, PATCH), F32),
            note,
            note,
            note,
            jax.ShapeDtypeStruct((PATCH, TILE), F32),
        ],
        in_specs=[ANY_SPEC] * 2,
        out_specs=[ANY_SPEC] * 7,
        scratch_shapes=[pltpu.SemaphoreType.DMA((7,))] * 2
        + [pltpu.SemaphoreType.DMA((2 * CHUNKS,))] * 2,
        compiler_params=pltpu.CompilerParams(collective_id=1, has_side_effects=True),
        name="halo_in",
    )(obj, meta)[:6]


def patches_kernel(
    meta_ref, above_ref, left_ref, diag_ref, probe_ref, lt_ref, rt_ref, amp_ref,
    obj, right, lower, diag, grad_ref, weight_ref, pg_ref, ext, spread, sems,
):
    copies = []

    def fetch(source, dest):
        copy = pltpu.make_async_copy(source, dest, sems.at[len(copies)])
        copy.start()
        copies.append(copy)

    for ct in range(4):
        lanes = pl.ds(PATCH * ct, PATCH)
        fetch(obj.at[:, :, lanes], ext.at[:, ct, pl.ds(0, TILE), :])
        fetch(lower.at[:, :, lanes], ext.at[:, ct, pl.ds(TILE, PATCH), :])
    fetch(right, ext.at[:, 4, pl.ds(0, TILE), :])
    fetch(diag, ext.at[:, 4, pl.ds(TILE, PATCH), :])
    grad_ref[...] = jnp.zeros(grad_ref.shape, F32)
    spread[...] = jnp.zeros(spread.shape, F32)
    pg_ref[...] = jnp.zeros(pg_ref.shape, F32)
    w = lax.axis_index("wide")
    c = lax.axis_index("col")
    lane = lax.broadcasted_iota(jnp.int32, (PATCH, PATCH), 1)
    count = meta_ref[2, 0]
    power = jnp.sum(probe_ref[...] * probe_ref[...], axis=(0, 1))

    def scatter(ref, row, at, value):
        ct, shift = lax.shift_right_logical(at, 7), lax.bitwise_and(at, 127)
        turned = pltpu.roll(value, shift, 1)
        first = lane >= shift
        zero = jnp.zeros_like(turned)
        rows = pl.ds(row, PATCH)
        ref[ct, rows, :] += jnp.where(first, turned, zero)
        ref[ct + 1, rows, :] += jnp.where(first, zero, turned)

    for ref, there, down, side in (
        (meta_ref, None, 0, 0),
        (above_ref, w > 0, TILE, 0),
        (left_ref, c > 0, 0, TILE),
        (diag_ref, (w > 0) & (c > 0), TILE, TILE),
    ):
        live_there = ref[2, 0] if there is None else jnp.where(there, ref[2, 0], 0)

        def weigh(s, carry, ref=ref, down=down, side=side):
            row, at = ref[0, s] + (PATCH - down), ref[1, s] + (PATCH - side)
            touches = None
            if down:
                touches = row > 0
            if side:
                touches = at > 0 if touches is None else touches & (at > 0)
            if touches is None:
                scatter(spread, row, at, power)
            else:
                pl.when(touches)(lambda: scatter(spread, row, at, power))
            return carry

        lax.fori_loop(0, live_there, weigh, 0)
    weight_ref[...] = spread[1:5, PATCH : PATCH + TILE, :]
    for copy in copies:
        copy.wait()

    @pl.when(w == 15)
    def _():
        ext[:, :, TILE:, :] = jnp.zeros((2, 5, PATCH, PATCH), F32)

    @pl.when(c == 15)
    def _():
        ext[:, 4, :, :] = jnp.zeros((2, EXT, PATCH), F32)

    lt = lt_ref[...]
    rt = rt_ref[...]

    def both_sides(left, stacked, right_side):
        half = jnp.dot(left, stacked, preferred_element_type=F32).astype(BF16)
        lanes = [slice(PATCH * m, PATCH * (m + 1)) for m in range(MODES)]
        turned = jnp.concatenate(
            [jnp.concatenate([half[:PATCH, at], half[PATCH:, at]], 1) for at in lanes], 0
        )
        return jnp.dot(turned, right_side, preferred_element_type=F32)

    def stack(re, im):
        return jnp.concatenate([jnp.concatenate(re, 1), jnp.concatenate(im, 1)], 0)

    def parts(values, m):
        rows = slice(PATCH * m, PATCH * (m + 1))
        return values[rows, :PATCH], values[rows, PATCH:]

    def step(index, carry):
        slots = [index * PAIR + u for u in range(PAIR)]
        info, waves = [], []
        for s in slots:
            row, at = meta_ref[0, s], meta_ref[1, s]
            ct, shift = lax.shift_right_logical(at, 7), lax.bitwise_and(at, 127)
            back = lax.bitwise_and(PATCH - shift, 127)
            rows = pl.ds(row, PATCH)
            patch = []
            for p in range(2):
                joined = jnp.where(lane >= shift, ext[p, ct, rows, :], ext[p, ct + 1, rows, :])
                patch.append(pltpu.roll(joined, back, 1))
            live = (s < count).astype(F32)
            info.append((row, at, None, live, patch))
            re, im = [], []
            for m in range(MODES):
                pr, pi = probe_ref[0, m], probe_ref[1, m]
                re.append((pr * patch[0] - pi * patch[1]).astype(BF16))
                im.append((pr * patch[1] + pi * patch[0]).astype(BF16))
            waves.append(stack(re, im))
        fars = [both_sides(lt, wave, rt) for wave in waves]
        residuals = []
        for u, s in enumerate(slots):
            intensity = jnp.zeros((PATCH, PATCH), F32)
            for m in range(MODES):
                fr, fi = parts(fars[u], m)
                intensity = intensity + fr * fr + fi * fi
            measured = amp_ref[s].astype(F32)
            factor = (measured * lax.rsqrt(jnp.maximum(intensity, 1.0)) - 1.0) * info[u][3]
            re, im = [], []
            for m in range(MODES):
                fr, fi = parts(fars[u], m)
                re.append((fr * factor).astype(BF16))
                im.append((fi * factor).astype(BF16))
            residuals.append(stack(re, im))
        updates = [both_sides(rt, residual, lt) for residual in residuals]
        for m in range(MODES):
            sum_re, sum_im = pg_ref[m], pg_ref[MODES + m]
            for u in range(PAIR):
                patch = info[u][4]
                ur, ui = parts(updates[u], m)
                sum_re = sum_re + patch[0] * ur + patch[1] * ui
                sum_im = sum_im + patch[0] * ui - patch[1] * ur
            pg_ref[m] = sum_re
            pg_ref[MODES + m] = sum_im
        lit = pg_ref[2 * MODES]
        for u in range(PAIR):
            patch = info[u][4]
            lit = lit + info[u][3] * (patch[0] * patch[0] + patch[1] * patch[1])
        pg_ref[2 * MODES] = lit
        for u in range(PAIR):
            row, at, _, live, _ = info[u]
            grad_re = jnp.zeros((PATCH, PATCH), F32)
            grad_im = grad_re
            for m in range(MODES):
                pr, pi = probe_ref[0, m], probe_ref[1, m]
                ur, ui = parts(updates[u], m)
                grad_re = grad_re + pr * ur + pi * ui
                grad_im = grad_im + pr * ui - pi * ur
            scatter(grad_ref.at[0], row, at, grad_re)
            scatter(grad_ref.at[1], row, at, grad_im)
        return carry

    lax.fori_loop(0, (count + PAIR - 1) // PAIR, step, 0)


def patches(metas, probe, amp, obj, right, lower, diag):
    table = left_table()
    return pl.pallas_call(
        patches_kernel,
        out_shape=[
            jax.ShapeDtypeStruct((2, 5, EXT, PATCH), F32),
            jax.ShapeDtypeStruct((4, TILE, PATCH), F32),
            jax.ShapeDtypeStruct((PLANES, PATCH, PATCH), F32),
        ],
        in_specs=[SMEM_SPEC] * 4 + [VMEM_SPEC] * 4 + [ANY_SPEC] * 4,
        out_specs=[VMEM_SPEC] * 3,
        scratch_shapes=[
            pltpu.VMEM((2, 5, EXT, PATCH), F32),
            pltpu.VMEM((6, EXT + PATCH, PATCH), F32),
            pltpu.SemaphoreType.DMA((10,)),
        ],
        compiler_params=pltpu.CompilerParams(vmem_limit_bytes=56 * 2**20),
        name="patches",
    )(*metas, probe, jnp.asarray(table), jnp.asarray(table.T), amp, obj, right, lower, diag)


def exchange_kernel(
    pg, grad, total, from_above, from_left, from_diag, passing,
    buf0, red0, buf1, red1, buf2, red2, buf3, own, res,
    s0, r0, s1, r1, s2, r2, s3, r3, s4, r4, s5, r5, s6, r6, sh, rh, sr, rr,
):
    w = lax.axis_index("wide")
    c = lax.axis_index("col")
    y, k = lax.rem(w, 4), lax.div(w, 4)
    core, chip = lax.rem(c, 2), lax.div(c, 2)
    sibling = (w, 2 * chip + 1 - core)
    above, below = lax.rem(w + 15, 16), lax.rem(w + 1, 16)
    before, after = lax.rem(c + 15, 16), lax.rem(c + 1, 16)
    far_send, far_get = (y == 3) & (k < 3), (y == 0) & (k > 0)
    relays = (y == 0) & (k < 3)
    relay_from, relay_at = lax.rem(w + 3, 16), lax.rem(w + 13, 16)
    relay_to, got_from = lax.rem(w + 4, 16), lax.rem(w + 12, 16)

    def rows(index, half):
        return pl.ds(pl.multiple_of(index * ROWS + half * (PATCH // 2), ROWS), ROWS)

    def planes(index):
        return pl.ds(index * 3, 3)

    chips = [(w, lax.rem(chip + d, 8) * 2 + core) for d in range(1, 8)]
    along_y = [(k * 4 + lax.rem(y + d, 4), c) for d in range(1, 4)]
    along_z = [(lax.rem(w + 4 * d, 16), c) for d in range(1, 4)]
    barrier = pltpu.get_barrier_semaphore()
    for target in [sibling] + chips + along_y + along_z:
        greet(barrier, target)
    for target in ((w, before), (above, c), (above, before)):
        greet(barrier, target)
    pl.when(relays)(lambda: greet(barrier, (relay_from, c)))
    pl.when(far_get)(lambda: greet(barrier, (got_from, c)))
    pl.semaphore_wait(barrier, 17 + jnp.where(far_send | relays, 1, 0))

    zeroth = []
    for d in range(1, 9):
        p = lax.rem(chip + d, 8)
        copy = remote(pg.at[:, rows(p, 1 - core), :], buf0.at[d - 1], s0.at[d - 1], r0.at[d - 1], sibling)
        copy.start()
        zeroth.append(copy)

    low = pl.ds(TILE, PATCH)
    size = PATCH // CHUNKS
    to_relay, from_relay = [], []
    for j in range(CHUNKS):
        cut = pl.ds(j * size, size)
        to_relay.append(remote(
            grad.at[1, pl.ds(0, 4), pl.ds(TILE + j * size, size), :], passing.at[:, cut, :],
            sr.at[j], rr.at[j], (relay_at, c),
        ))
        from_relay.append(remote(
            passing.at[:, cut, :], from_above.at[1, :, cut, :],
            sr.at[CHUNKS + j], rr.at[CHUNKS + j], (relay_to, c),
        ))
    ups, downs = w > 0, w < 15
    lefts, rights = c > 0, c < 15
    near_send = downs & jnp.logical_not(far_send)
    near_get = ups & jnp.logical_not(far_get)
    halos = (
        (grad.at[0, pl.ds(0, 4), low, :], from_above.at[0], (below, c), downs, ups),
        (grad.at[1, pl.ds(0, 4), low, :], from_above.at[1], (below, c), near_send, near_get),
        (grad.at[:, 4, pl.ds(0, TILE), :], from_left, (w, after), rights, lefts),
        (grad.at[:, 4, low, :], from_diag, (below, after), downs & rights, ups & lefts),
    )

    @pl.when(far_send)
    def _():
        for copy in to_relay:
            copy.start()

    strips = []
    for j, (source, dest, target, sends, gets) in enumerate(halos):
        copy = remote(source, dest, sh.at[j], rh.at[j], target)
        pl.when(sends)(copy.start)
        strips.append((copy, sends, gets))

    first = []
    for d in range(1, 8):
        p = lax.rem(chip + d, 8)
        zeroth[d - 1].wait_recv()
        red0[d - 1] = pg[:, rows(p, core), :] + buf0[d - 1]
        copy = remote(red0.at[d - 1], buf1.at[d], s1.at[d], r1.at[d], chips[d - 1])
        copy.start()
        first.append(copy)
    zeroth[7].wait_recv()
    acc = pg[:, rows(chip, core), :] + buf0[7]

    @pl.when(relays)
    def _():
        for arrived, onward in zip(to_relay, from_relay):
            arrived.wait_recv()
            onward.start()

    for d in range(1, 8):
        first[d - 1].wait_recv()
        acc = acc + buf1[d]
    red1[pl.ds(0, PLANES)] = acc
    red1[pl.ds(PLANES, 3)] = jnp.zeros((3, ROWS, PATCH), F32)
    second = []
    for d in range(1, 4):
        copy = remote(
            red1.at[planes(lax.rem(y + d, 4))], buf2.at[d], s2.at[d], r2.at[d], along_y[d - 1]
        )
        copy.start()
        second.append(copy)
    acc = red1[planes(y)]
    for d in range(1, 4):
        second[d - 1].wait_recv()
        acc = acc + buf2[d]
    buf3[k] = acc
    third = []
    for d in range(1, 4):
        copy = remote(buf3.at[k], buf3.at[k], s3.at[d], r3.at[d], along_z[d - 1])
        copy.start()
        third.append(copy)
    for d in range(1, 4):
        p = lax.rem(k + 4 - d, 4)
        remote(buf3.at[p], buf3.at[p], s3.at[d], r3.at[d], along_z[d - 1]).wait_recv()
    own[planes(y)] = buf3[0] + buf3[1] + buf3[2] + buf3[3]
    fourth = []
    for d in range(1, 4):
        copy = remote(own.at[planes(y)], own.at[planes(y)], s4.at[d], r4.at[d], along_y[d - 1])
        copy.start()
        fourth.append(copy)
    for d in range(1, 4):
        p = planes(lax.rem(y + 4 - d, 4))
        remote(own.at[p], own.at[p], s4.at[d], r4.at[d], along_y[d - 1]).wait_recv()
    lit = own[2 * MODES]
    res[...] = own[pl.ds(0, 2 * MODES)] / jnp.sqrt(lit + 1.0)[None]

    mine = rows(chip, core)
    fifth, sixth = [], []
    for d in range(1, 8):
        copy = remote(res, total.at[:, mine, :], s5.at[d], r5.at[d], chips[d - 1])
        copy.start()
        fifth.append(copy)
    copy = remote(res, total.at[:, mine, :], s6.at[0], r6.at[0], sibling)
    copy.start()
    sixth.append(copy)
    total[:, mine, :] = res[...]
    for d in range(1, 8):
        at = rows(lax.rem(chip + 8 - d, 8), core)
        remote(res, total.at[:, at, :], s5.at[d], r5.at[d], chips[d - 1]).wait_recv()
        copy = remote(total.at[:, at, :], total.at[:, at, :], s6.at[d], r6.at[d], sibling)
        copy.start()
        sixth.append(copy)
    for copy in zeroth + first + second + third + fourth + fifth:
        copy.wait_send()
    for d in range(8):
        at = rows(lax.rem(chip + 8 - d, 8), 1 - core)
        remote(res, total.at[:, at, :], s6.at[d], r6.at[d], sibling).wait_recv()
    for copy in sixth:
        copy.wait_send()
    for copy, sends, gets in strips:
        pl.when(gets)(copy.wait_recv)
        pl.when(sends)(copy.wait_send)

    @pl.when(far_get)
    def _():
        for copy in from_relay:
            copy.wait_recv()

    @pl.when(relays)
    def _():
        for copy in from_relay:
            copy.wait_send()

    @pl.when(far_send)
    def _():
        for copy in to_relay:
            copy.wait_send()


def exchange(pg, grad):
    eight = pltpu.SemaphoreType.DMA((8,))
    four = pltpu.SemaphoreType.DMA((4,))
    relayed = pltpu.SemaphoreType.DMA((2 * CHUNKS,))
    return pl.pallas_call(
        exchange_kernel,
        out_shape=[
            jax.ShapeDtypeStruct((2 * MODES, PATCH, PATCH), F32),
            jax.ShapeDtypeStruct((2, 4, PATCH, PATCH), F32),
            jax.ShapeDtypeStruct((2, TILE, PATCH), F32),
            jax.ShapeDtypeStruct((2, PATCH, PATCH), F32),
            jax.ShapeDtypeStruct((4, PATCH, PATCH), F32),
        ],
        in_specs=[VMEM_SPEC, ANY_SPEC],
        out_specs=[VMEM_SPEC] + [ANY_SPEC] * 4,
        scratch_shapes=[
            pltpu.VMEM((8, PLANES, ROWS, PATCH), F32),
            pltpu.VMEM((8, PLANES, ROWS, PATCH), F32),
            pltpu.VMEM((8, PLANES, ROWS, PATCH), F32),
            pltpu.VMEM((12, ROWS, PATCH), F32),
            pltpu.VMEM((4, 3, ROWS, PATCH), F32),
            pltpu.VMEM((3, ROWS, PATCH), F32),
            pltpu.VMEM((4, 3, ROWS, PATCH), F32),
            pltpu.VMEM((12, ROWS, PATCH), F32),
            pltpu.VMEM((2 * MODES, ROWS, PATCH), F32),
        ]
        + [eight] * 4
        + [four] * 6
        + [eight] * 4
        + [four] * 2
        + [relayed] * 2,
        compiler_params=pltpu.CompilerParams(collective_id=2, has_side_effects=True),
        name="exchange",
    )(pg, grad)[:4]


def finish_kernel(obj, grad, weight, total, from_above, from_left, from_diag, new, direction):
    block = pl.program_id(0)
    w = lax.axis_index("wide")
    c = lax.axis_index("col")
    got_above = (block == 0) & (w > 0)
    got_left = c > 0
    got_diag = got_above & got_left

    @pl.when(block == 0)
    def _():
        direction[...] = total[...]

    for ct in range(4):
        lanes = slice(PATCH * ct, PATCH * (ct + 1))
        sums = grad[:, ct]
        sums = sums + jnp.where(got_above, from_above[:, ct], 0.0)
        if ct == 0:
            sums = sums + jnp.where(got_left, from_left[...], 0.0)
            sums = sums + jnp.where(got_diag, from_diag[...], 0.0)
        scale = weight[ct] + 1.0
        for p in range(2):
            new[p, :, lanes] = obj[p, :, lanes] + sums[p] / scale


def finish(obj, grad, weight, total, from_above, from_left, from_diag):
    return pl.pallas_call(
        finish_kernel,
        grid=(4,),
        out_shape=[
            jax.ShapeDtypeStruct((2, TILE, TILE), F32),
            jax.ShapeDtypeStruct((2 * MODES, PATCH, PATCH), F32),
        ],
        in_specs=[
            pl.BlockSpec((2, PATCH, TILE), lambda i: (0, i, 0)),
            pl.BlockSpec((2, 4, PATCH, PATCH), lambda i: (0, 0, i, 0)),
            pl.BlockSpec((4, PATCH, PATCH), lambda i: (0, i, 0)),
            pl.BlockSpec((2 * MODES, PATCH, PATCH), lambda i: (0, 0, 0)),
            pl.BlockSpec((2, 4, PATCH, PATCH), lambda i: (0, 0, 0, 0)),
            pl.BlockSpec((2, PATCH, PATCH), lambda i: (0, i, 0)),
            pl.BlockSpec((2, PATCH, PATCH), lambda i: (0, 0, 0)),
        ],
        out_specs=[
            pl.BlockSpec((2, PATCH, TILE), lambda i: (0, i, 0)),
            pl.BlockSpec((2 * MODES, PATCH, PATCH), lambda i: (0, 0, 0)),
        ],
        name="finish",
    )(obj, grad, weight, total, from_above, from_left, from_diag)


def local(object_field, probe_modes, amplitude, positions, slot_counts):
    slots = positions.shape[2]
    meta = jnp.concatenate(
        [
            jnp.pad(positions.reshape(slots, 2).T, ((0, 0), (0, PATCH - slots))),
            jnp.broadcast_to(slot_counts, (6, PATCH)),
        ],
        0,
    )
    right, lower, diag, *others = halo_in(object_field, meta)
    grad, weight, pg = patches(
        (meta, *others),
        probe_modes,
        amplitude.reshape(slots, PATCH, PATCH),
        object_field,
        right,
        lower,
        diag,
    )
    total, from_above, from_left, from_diag = exchange(pg, grad)
    new_object, direction = finish(
        object_field, grad, weight, total, from_above, from_left, from_diag
    )
    return new_object, direction.reshape(probe_modes.shape)


def solution(mesh):
    placed = (
        P(None, "wide", "col"),
        P(),
        P("wide", "col", None, None, None),
        P("wide", "col", None, None),
        P("wide", "col"),
    )
    return jax.shard_map(
        local, mesh=mesh, in_specs=placed, out_specs=(P(None, "wide", "col"), P()), check_vma=False
    )
```

```python
import functools
import math

import jax
import jax.numpy as jnp
import ml_dtypes
import numpy as np
from jax import lax
from jax.experimental import pallas as pl
from jax.experimental.pallas import tpu as pltpu
from jax.sharding import PartitionSpec as P

MESH = pl.DeviceIdType.MESH
F32 = jnp.float32
BF16 = jnp.bfloat16
PATCH = 128
TILE = 512
EXT = TILE + PATCH
MODES = 4
RING = 16
PLANES = 2 * MODES + 1
ROWS = PATCH // RING
PAIR = 2
CHUNKS = 4
EARLY = 16
INSIDE = TILE - PATCH

VMEM_SPEC = pl.BlockSpec(memory_space=pltpu.VMEM)
SMEM_SPEC = pl.BlockSpec(memory_space=pltpu.SMEM)
ANY_SPEC = pl.BlockSpec(memory_space=pl.ANY)


def left_table():
    indices = np.arange(PATCH)
    angles = (indices[:, None] * indices[None, :] % PATCH) * (2.0 * math.pi / PATCH)
    cosine = np.cos(angles) / math.sqrt(PATCH)
    sine = -np.sin(angles) / math.sqrt(PATCH)
    whole = np.block([[cosine, -sine], [sine, cosine]])
    return whole.astype(np.float32).astype(ml_dtypes.bfloat16)


def plan_kernel(pos_ref, count_ref, meta_ref):
    count = count_ref[0, 0]
    low, high = jnp.int32(0), count - 1
    for s in range(pos_ref.shape[1]):
        row, at = pos_ref[0, s], pos_ref[1, s]
        live = s < count
        inner = live & (row <= INSIDE) & (at <= INSIDE)
        place = jnp.where(inner, low, jnp.where(live, high, s))
        meta_ref[0, place] = row
        meta_ref[1, place] = at
        meta_ref[3, place] = s
        low = low + jnp.where(inner, 1, 0)
        high = high - jnp.where(live & jnp.logical_not(inner), 1, 0)
    for line in (0, 1, 3):
        meta_ref[line, pos_ref.shape[1]] = 0
    meta_ref[2, 0] = count
    meta_ref[2, 1] = low


def plan(positions, slot_counts):
    return pl.pallas_call(
        plan_kernel,
        out_shape=jax.ShapeDtypeStruct((8, PATCH), jnp.int32),
        in_specs=[SMEM_SPEC] * 2,
        out_specs=SMEM_SPEC,
        name="plan",
    )(positions, slot_counts)


def lanes_of():
    return lax.broadcasted_iota(jnp.int32, (PATCH, PATCH), 1)


def both_sides(left, stacked, right_side):
    half = jnp.dot(left, stacked, preferred_element_type=F32).astype(BF16)
    lanes = [slice(PATCH * m, PATCH * (m + 1)) for m in range(MODES)]
    turned = jnp.concatenate(
        [jnp.concatenate([half[:PATCH, at], half[PATCH:, at]], 1) for at in lanes], 0
    )
    return jnp.dot(turned, right_side, preferred_element_type=F32)


def stack(re, im):
    return jnp.concatenate([jnp.concatenate(re, 1), jnp.concatenate(im, 1)], 0)


def parts(values, m):
    rows = slice(PATCH * m, PATCH * (m + 1))
    return values[rows, :PATCH], values[rows, PATCH:]


def solve(slots, ext, last, probe_ref, lt, rt, amp_ref, pg_ref):
    lane = lanes_of()
    patches_of, waves = [], []
    for s, row, at, live in slots:
        ct, shift = lax.shift_right_logical(at, 7), lax.bitwise_and(at, 127)
        back = lax.bitwise_and(PATCH - shift, 127)
        beside = jnp.minimum(ct + 1, last)
        rows = pl.ds(row, PATCH)
        patch = []
        for p in range(2):
            joined = jnp.where(lane >= shift, ext[p, ct, rows, :], ext[p, beside, rows, :])
            patch.append(pltpu.roll(joined, back, 1))
        patches_of.append(patch)
        re, im = [], []
        for m in range(MODES):
            pr, pi = probe_ref[0, m], probe_ref[1, m]
            re.append((pr * patch[0] - pi * patch[1]).astype(BF16))
            im.append((pr * patch[1] + pi * patch[0]).astype(BF16))
        waves.append(stack(re, im))
    fars = [both_sides(lt, wave, rt) for wave in waves]
    residuals = []
    for (s, row, at, live), far in zip(slots, fars):
        intensity = jnp.zeros((PATCH, PATCH), F32)
        for m in range(MODES):
            fr, fi = parts(far, m)
            intensity = intensity + fr * fr + fi * fi
        measured = amp_ref[s].astype(F32)
        factor = (measured * lax.rsqrt(jnp.maximum(intensity, 1.0)) - 1.0) * live
        re, im = [], []
        for m in range(MODES):
            fr, fi = parts(far, m)
            re.append((fr * factor).astype(BF16))
            im.append((fi * factor).astype(BF16))
        residuals.append(stack(re, im))
    updates = [both_sides(rt, residual, lt) for residual in residuals]
    for m in range(MODES):
        sum_re, sum_im = pg_ref[m], pg_ref[MODES + m]
        for patch, update in zip(patches_of, updates):
            ur, ui = parts(update, m)
            sum_re = sum_re + patch[0] * ur + patch[1] * ui
            sum_im = sum_im + patch[0] * ui - patch[1] * ur
        pg_ref[m] = sum_re
        pg_ref[MODES + m] = sum_im
    lit = pg_ref[2 * MODES]
    for (s, row, at, live), patch in zip(slots, patches_of):
        lit = lit + live * (patch[0] * patch[0] + patch[1] * patch[1])
    pg_ref[2 * MODES] = lit
    grads = []
    for update in updates:
        grad_re = jnp.zeros((PATCH, PATCH), F32)
        grad_im = grad_re
        for m in range(MODES):
            pr, pi = probe_ref[0, m], probe_ref[1, m]
            ur, ui = parts(update, m)
            grad_re = grad_re + pr * ur + pi * ui
            grad_im = grad_im + pr * ui - pi * ur
        grads.append((grad_re, grad_im))
    return grads


def remote(source, dest, sent, got, target):
    return pltpu.make_async_remote_copy(
        source, dest, sent, got, device_id=target, device_id_type=MESH
    )


def greet(barrier, target):
    pl.semaphore_signal(barrier, inc=1, device_id=target, device_id_type=MESH)


def halo_in_kernel(
    obj, meta, meta_ref, probe_ref, lt_ref, rt_ref, amp_ref,
    right, lower, diag, meta_above, meta_left, meta_diag, passing, early_ref, pg_ref,
    ext, fetched, sent, got, sent_relay, got_relay,
):
    inward = []
    for ct in range(4):
        copy = pltpu.make_async_copy(
            obj.at[:, :, pl.ds(PATCH * ct, PATCH)], ext.at[:, ct], fetched.at[ct]
        )
        copy.start()
        inward.append(copy)
    w = lax.axis_index("wide")
    c = lax.axis_index("col")
    y, k = lax.rem(w, 4), lax.div(w, 4)
    above, below = lax.rem(w + 15, 16), lax.rem(w + 1, 16)
    before, after = lax.rem(c + 15, 16), lax.rem(c + 1, 16)
    far_send, far_get = (y == 0) & (k > 0), (y == 3) & (k < 3)
    relays = (y == 3) & (k > 0)
    relay_from, relay_at = lax.rem(w + 13, 16), lax.rem(w + 3, 16)
    relay_to, got_from = lax.rem(w + 12, 16), lax.rem(w + 4, 16)
    barrier = pltpu.get_barrier_semaphore()
    for target in (
        (w, after), (below, c), (below, after), (w, before), (above, c), (above, before)
    ):
        greet(barrier, target)
    pl.when(relays)(lambda: greet(barrier, (relay_from, c)))
    pl.when(far_get)(lambda: greet(barrier, (got_from, c)))
    pl.semaphore_wait(barrier, 6 + jnp.where(far_send | relays, 1, 0))
    top = pl.ds(0, PATCH)
    size = PATCH // CHUNKS
    cuts = [pl.ds(j * size, size) for j in range(CHUNKS)]
    to_relay = [
        remote(
            obj.at[1, cut, :], passing.at[cut, :], sent_relay.at[j], got_relay.at[j], (relay_at, c)
        )
        for j, cut in enumerate(cuts)
    ]
    from_relay = [
        remote(
            passing.at[cut, :], lower.at[1, cut, :],
            sent_relay.at[CHUNKS + j], got_relay.at[CHUNKS + j], (relay_to, c),
        )
        for j, cut in enumerate(cuts)
    ]

    @pl.when(far_send)
    def _():
        for copy in to_relay:
            copy.start()

    ups, downs = w > 0, w < 15
    lefts, rights = c > 0, c < 15
    near_send = ups & jnp.logical_not(far_send)
    near_get = downs & jnp.logical_not(far_get)
    plain = (
        (obj.at[0, top, :], lower.at[0], (above, c), ups, downs),
        (obj.at[1, top, :], lower.at[1], (above, c), near_send, near_get),
        (obj.at[:, :, top], right, (w, before), lefts, rights),
        (obj.at[:, top, top], diag, (above, before), ups & lefts, downs & rights),
        (meta, meta_above, (below, c), downs, ups),
        (meta, meta_left, (w, after), rights, lefts),
        (meta, meta_diag, (below, after), downs & rights, ups & lefts),
    )
    made = []
    for j, (source, dest, target, sends, gets) in enumerate(plain):
        copy = remote(source, dest, sent.at[j], got.at[j], target)
        pl.when(sends)(copy.start)
        made.append((copy, sends, gets))

    pg_ref[...] = jnp.zeros(pg_ref.shape, F32)
    lt = lt_ref[...]
    rt = rt_ref[...]
    inner = meta_ref[2, 1]
    for copy in inward:
        copy.wait()

    def step(index, carry):
        slots = []
        for u in range(PAIR):
            j = index * PAIR + u
            row, at = jnp.minimum(meta_ref[0, j], INSIDE), jnp.minimum(meta_ref[1, j], INSIDE)
            slots.append((meta_ref[3, j], row, at, (j < inner).astype(F32)))
        grads = solve(slots, ext, 3, probe_ref, lt, rt, amp_ref, pg_ref)
        for u, (grad_re, grad_im) in enumerate(grads):
            early_ref[index * PAIR + u, 0] = grad_re
            early_ref[index * PAIR + u, 1] = grad_im
        return carry

    steps = EARLY // PAIR
    lax.fori_loop(0, steps // 2, step, 0)

    @pl.when(relays)
    def _():
        for arrived, onward in zip(to_relay, from_relay):
            arrived.wait_recv()
            onward.start()

    lax.fori_loop(steps // 2, steps, step, 0)
    for copy, sends, gets in made:
        pl.when(gets)(copy.wait_recv)
        pl.when(sends)(copy.wait_send)

    @pl.when(far_get)
    def _():
        for copy in from_relay:
            copy.wait_recv()

    @pl.when(relays)
    def _():
        for copy in from_relay:
            copy.wait_send()

    @pl.when(far_send)
    def _():
        for copy in to_relay:
            copy.wait_send()


def halo_in(obj, meta, probe, tables, amp):
    note = jax.ShapeDtypeStruct(meta.shape, meta.dtype)
    made = pl.pallas_call(
        halo_in_kernel,
        out_shape=[
            jax.ShapeDtypeStruct((2, TILE, PATCH), F32),
            jax.ShapeDtypeStruct((2, PATCH, TILE), F32),
            jax.ShapeDtypeStruct((2, PATCH, PATCH), F32),
            note,
            note,
            note,
            jax.ShapeDtypeStruct((PATCH, TILE), F32),
            jax.ShapeDtypeStruct((EARLY, 2, PATCH, PATCH), F32),
            jax.ShapeDtypeStruct((PLANES, PATCH, PATCH), F32),
        ],
        in_specs=[ANY_SPEC] * 2 + [SMEM_SPEC] + [VMEM_SPEC] * 4,
        out_specs=[ANY_SPEC] * 7 + [VMEM_SPEC] * 2,
        scratch_shapes=[pltpu.VMEM((2, 4, TILE, PATCH), F32), pltpu.SemaphoreType.DMA((4,))]
        + [pltpu.SemaphoreType.DMA((7,))] * 2
        + [pltpu.SemaphoreType.DMA((2 * CHUNKS,))] * 2,
        compiler_params=pltpu.CompilerParams(
            collective_id=1, has_side_effects=True, vmem_limit_bytes=56 * 2**20
        ),
        name="halo_in",
    )(obj, meta, meta, probe, *tables, amp)
    return made[:6], made[7], made[8]


def patches_kernel(
    meta_ref, above_ref, left_ref, diag_ref, probe_ref, lt_ref, rt_ref, amp_ref,
    early_ref, early_pg, obj, right, lower, diag,
    grad_ref, weight_ref, pg_ref, ext, spread, sems,
):
    copies = []

    def fetch(source, dest):
        copy = pltpu.make_async_copy(source, dest, sems.at[len(copies)])
        copy.start()
        copies.append(copy)

    for ct in range(4):
        lanes = pl.ds(PATCH * ct, PATCH)
        fetch(obj.at[:, :, lanes], ext.at[:, ct, pl.ds(0, TILE), :])
        fetch(lower.at[:, :, lanes], ext.at[:, ct, pl.ds(TILE, PATCH), :])
    fetch(right, ext.at[:, 4, pl.ds(0, TILE), :])
    fetch(diag, ext.at[:, 4, pl.ds(TILE, PATCH), :])
    grad_ref[...] = jnp.zeros(grad_ref.shape, F32)
    spread[...] = jnp.zeros(spread.shape, F32)
    pg_ref[...] = early_pg[...]
    w = lax.axis_index("wide")
    c = lax.axis_index("col")
    lane = lanes_of()
    count = meta_ref[2, 0]
    done = jnp.minimum(meta_ref[2, 1], EARLY)
    power = jnp.sum(probe_ref[...] * probe_ref[...], axis=(0, 1))

    def scatter(ref, row, at, value):
        ct, shift = lax.shift_right_logical(at, 7), lax.bitwise_and(at, 127)
        turned = pltpu.roll(value, shift, 1)
        first = lane >= shift
        zero = jnp.zeros_like(turned)
        rows = pl.ds(row, PATCH)
        ref[ct, rows, :] += jnp.where(first, turned, zero)
        ref[ct + 1, rows, :] += jnp.where(first, zero, turned)

    for ref, there, down, side in (
        (meta_ref, None, 0, 0),
        (above_ref, w > 0, TILE, 0),
        (left_ref, c > 0, 0, TILE),
        (diag_ref, (w > 0) & (c > 0), TILE, TILE),
    ):
        live_there = ref[2, 0] if there is None else jnp.where(there, ref[2, 0], 0)

        def weigh(s, carry, ref=ref, down=down, side=side):
            row, at = ref[0, s] + (PATCH - down), ref[1, s] + (PATCH - side)
            touches = None
            if down:
                touches = row > 0
            if side:
                touches = at > 0 if touches is None else touches & (at > 0)
            if touches is None:
                scatter(spread, row, at, power)
            else:
                pl.when(touches)(lambda: scatter(spread, row, at, power))
            return carry

        lax.fori_loop(0, live_there, weigh, 0)
    weight_ref[...] = spread[1:5, PATCH : PATCH + TILE, :]

    def place(j, carry):
        for p in range(2):
            scatter(grad_ref.at[p], meta_ref[0, j], meta_ref[1, j], early_ref[j, p])
        return carry

    lax.fori_loop(0, done, place, 0)
    for copy in copies:
        copy.wait()

    @pl.when(w == 15)
    def _():
        ext[:, :, TILE:, :] = jnp.zeros((2, 5, PATCH, PATCH), F32)

    @pl.when(c == 15)
    def _():
        ext[:, 4, :, :] = jnp.zeros((2, EXT, PATCH), F32)

    lt = lt_ref[...]
    rt = rt_ref[...]

    def step(index, carry):
        slots = []
        for u in range(PAIR):
            j = done + index * PAIR + u
            slots.append((meta_ref[3, j], meta_ref[0, j], meta_ref[1, j], (j < count).astype(F32)))
        grads = solve(slots, ext, 4, probe_ref, lt, rt, amp_ref, pg_ref)
        for (s, row, at, live), (grad_re, grad_im) in zip(slots, grads):
            scatter(grad_ref.at[0], row, at, grad_re)
            scatter(grad_ref.at[1], row, at, grad_im)
        return carry

    lax.fori_loop(0, (count - done + PAIR - 1) // PAIR, step, 0)


def patches(metas, probe, tables, amp, early, early_pg, obj, right, lower, diag):
    return pl.pallas_call(
        patches_kernel,
        out_shape=[
            jax.ShapeDtypeStruct((2, 5, EXT, PATCH), F32),
            jax.ShapeDtypeStruct((4, TILE, PATCH), F32),
            jax.ShapeDtypeStruct((PLANES, PATCH, PATCH), F32),
        ],
        in_specs=[SMEM_SPEC] * 4 + [VMEM_SPEC] * 6 + [ANY_SPEC] * 4,
        out_specs=[VMEM_SPEC] * 3,
        scratch_shapes=[
            pltpu.VMEM((2, 5, EXT, PATCH), F32),
            pltpu.VMEM((6, EXT + PATCH, PATCH), F32),
            pltpu.SemaphoreType.DMA((10,)),
        ],
        compiler_params=pltpu.CompilerParams(vmem_limit_bytes=56 * 2**20),
        name="patches",
    )(*metas, probe, *tables, amp, early, early_pg, obj, right, lower, diag)


def exchange_kernel(
    pg, grad, total, from_above, from_left, from_diag, passing,
    buf0, red0, buf1, red1, buf2, red2, buf3, own, res,
    s0, r0, s1, r1, s2, r2, s3, r3, s4, r4, s5, r5, s6, r6, sh, rh, sr, rr,
):
    w = lax.axis_index("wide")
    c = lax.axis_index("col")
    y, k = lax.rem(w, 4), lax.div(w, 4)
    core, chip = lax.rem(c, 2), lax.div(c, 2)
    sibling = (w, 2 * chip + 1 - core)
    above, below = lax.rem(w + 15, 16), lax.rem(w + 1, 16)
    before, after = lax.rem(c + 15, 16), lax.rem(c + 1, 16)
    far_send, far_get = (y == 3) & (k < 3), (y == 0) & (k > 0)
    relays = (y == 0) & (k < 3)
    relay_from, relay_at = lax.rem(w + 3, 16), lax.rem(w + 13, 16)
    relay_to, got_from = lax.rem(w + 4, 16), lax.rem(w + 12, 16)

    def rows(index, half):
        return pl.ds(pl.multiple_of(index * ROWS + half * (PATCH // 2), ROWS), ROWS)

    def planes(index):
        return pl.ds(index * 3, 3)

    chips = [(w, lax.rem(chip + d, 8) * 2 + core) for d in range(1, 8)]
    along_y = [(k * 4 + lax.rem(y + d, 4), c) for d in range(1, 4)]
    along_z = [(lax.rem(w + 4 * d, 16), c) for d in range(1, 4)]
    barrier = pltpu.get_barrier_semaphore()
    for target in [sibling] + chips + along_y + along_z:
        greet(barrier, target)
    for target in ((w, before), (above, c), (above, before)):
        greet(barrier, target)
    pl.when(relays)(lambda: greet(barrier, (relay_from, c)))
    pl.when(far_get)(lambda: greet(barrier, (got_from, c)))
    pl.semaphore_wait(barrier, 17 + jnp.where(far_send | relays, 1, 0))

    zeroth = []
    for d in range(1, 9):
        p = lax.rem(chip + d, 8)
        copy = remote(pg.at[:, rows(p, 1 - core), :], buf0.at[d - 1], s0.at[d - 1], r0.at[d - 1], sibling)
        copy.start()
        zeroth.append(copy)

    low = pl.ds(TILE, PATCH)
    size = PATCH // CHUNKS
    to_relay, from_relay = [], []
    for j in range(CHUNKS):
        cut = pl.ds(j * size, size)
        to_relay.append(remote(
            grad.at[1, pl.ds(0, 4), pl.ds(TILE + j * size, size), :], passing.at[:, cut, :],
            sr.at[j], rr.at[j], (relay_at, c),
        ))
        from_relay.append(remote(
            passing.at[:, cut, :], from_above.at[1, :, cut, :],
            sr.at[CHUNKS + j], rr.at[CHUNKS + j], (relay_to, c),
        ))
    ups, downs = w > 0, w < 15
    lefts, rights = c > 0, c < 15
    near_send = downs & jnp.logical_not(far_send)
    near_get = ups & jnp.logical_not(far_get)
    halos = (
        (grad.at[0, pl.ds(0, 4), low, :], from_above.at[0], (below, c), downs, ups),
        (grad.at[1, pl.ds(0, 4), low, :], from_above.at[1], (below, c), near_send, near_get),
        (grad.at[:, 4, pl.ds(0, TILE), :], from_left, (w, after), rights, lefts),
        (grad.at[:, 4, low, :], from_diag, (below, after), downs & rights, ups & lefts),
    )

    @pl.when(far_send)
    def _():
        for copy in to_relay:
            copy.start()

    strips = []
    for j, (source, dest, target, sends, gets) in enumerate(halos):
        copy = remote(source, dest, sh.at[j], rh.at[j], target)
        pl.when(sends)(copy.start)
        strips.append((copy, sends, gets))

    first = []
    for d in range(1, 8):
        p = lax.rem(chip + d, 8)
        zeroth[d - 1].wait_recv()
        red0[d - 1] = pg[:, rows(p, core), :] + buf0[d - 1]
        copy = remote(red0.at[d - 1], buf1.at[d], s1.at[d], r1.at[d], chips[d - 1])
        copy.start()
        first.append(copy)
    zeroth[7].wait_recv()
    acc = pg[:, rows(chip, core), :] + buf0[7]

    @pl.when(relays)
    def _():
        for arrived, onward in zip(to_relay, from_relay):
            arrived.wait_recv()
            onward.start()

    for d in range(1, 8):
        first[d - 1].wait_recv()
        acc = acc + buf1[d]
    red1[pl.ds(0, PLANES)] = acc
    red1[pl.ds(PLANES, 3)] = jnp.zeros((3, ROWS, PATCH), F32)
    second = []
    for d in range(1, 4):
        copy = remote(
            red1.at[planes(lax.rem(y + d, 4))], buf2.at[d], s2.at[d], r2.at[d], along_y[d - 1]
        )
        copy.start()
        second.append(copy)
    acc = red1[planes(y)]
    for d in range(1, 4):
        second[d - 1].wait_recv()
        acc = acc + buf2[d]
    buf3[k] = acc
    third = []
    for d in range(1, 4):
        copy = remote(buf3.at[k], buf3.at[k], s3.at[d], r3.at[d], along_z[d - 1])
        copy.start()
        third.append(copy)
    for d in range(1, 4):
        p = lax.rem(k + 4 - d, 4)
        remote(buf3.at[p], buf3.at[p], s3.at[d], r3.at[d], along_z[d - 1]).wait_recv()
    own[planes(y)] = buf3[0] + buf3[1] + buf3[2] + buf3[3]
    fourth = []
    for d in range(1, 4):
        copy = remote(own.at[planes(y)], own.at[planes(y)], s4.at[d], r4.at[d], along_y[d - 1])
        copy.start()
        fourth.append(copy)
    for d in range(1, 4):
        p = planes(lax.rem(y + 4 - d, 4))
        remote(own.at[p], own.at[p], s4.at[d], r4.at[d], along_y[d - 1]).wait_recv()
    lit = own[2 * MODES]
    res[...] = own[pl.ds(0, 2 * MODES)] / jnp.sqrt(lit + 1.0)[None]

    mine = rows(chip, core)
    fifth, sixth = [], []
    for d in range(1, 8):
        copy = remote(res, total.at[:, mine, :], s5.at[d], r5.at[d], chips[d - 1])
        copy.start()
        fifth.append(copy)
    copy = remote(res, total.at[:, mine, :], s6.at[0], r6.at[0], sibling)
    copy.start()
    sixth.append(copy)
    total[:, mine, :] = res[...]
    for d in range(1, 8):
        at = rows(lax.rem(chip + 8 - d, 8), core)
        remote(res, total.at[:, at, :], s5.at[d], r5.at[d], chips[d - 1]).wait_recv()
        copy = remote(total.at[:, at, :], total.at[:, at, :], s6.at[d], r6.at[d], sibling)
        copy.start()
        sixth.append(copy)
    for copy in zeroth + first + second + third + fourth + fifth:
        copy.wait_send()
    for d in range(8):
        at = rows(lax.rem(chip + 8 - d, 8), 1 - core)
        remote(res, total.at[:, at, :], s6.at[d], r6.at[d], sibling).wait_recv()
    for copy in sixth:
        copy.wait_send()
    for copy, sends, gets in strips:
        pl.when(gets)(copy.wait_recv)
        pl.when(sends)(copy.wait_send)

    @pl.when(far_get)
    def _():
        for copy in from_relay:
            copy.wait_recv()

    @pl.when(relays)
    def _():
        for copy in from_relay:
            copy.wait_send()

    @pl.when(far_send)
    def _():
        for copy in to_relay:
            copy.wait_send()


def exchange(pg, grad):
    eight = pltpu.SemaphoreType.DMA((8,))
    four = pltpu.SemaphoreType.DMA((4,))
    relayed = pltpu.SemaphoreType.DMA((2 * CHUNKS,))
    return pl.pallas_call(
        exchange_kernel,
        out_shape=[
            jax.ShapeDtypeStruct((2 * MODES, PATCH, PATCH), F32),
            jax.ShapeDtypeStruct((2, 4, PATCH, PATCH), F32),
            jax.ShapeDtypeStruct((2, TILE, PATCH), F32),
            jax.ShapeDtypeStruct((2, PATCH, PATCH), F32),
            jax.ShapeDtypeStruct((4, PATCH, PATCH), F32),
        ],
        in_specs=[VMEM_SPEC, ANY_SPEC],
        out_specs=[VMEM_SPEC] + [ANY_SPEC] * 4,
        scratch_shapes=[
            pltpu.VMEM((8, PLANES, ROWS, PATCH), F32),
            pltpu.VMEM((8, PLANES, ROWS, PATCH), F32),
            pltpu.VMEM((8, PLANES, ROWS, PATCH), F32),
            pltpu.VMEM((12, ROWS, PATCH), F32),
            pltpu.VMEM((4, 3, ROWS, PATCH), F32),
            pltpu.VMEM((3, ROWS, PATCH), F32),
            pltpu.VMEM((4, 3, ROWS, PATCH), F32),
            pltpu.VMEM((12, ROWS, PATCH), F32),
            pltpu.VMEM((2 * MODES, ROWS, PATCH), F32),
        ]
        + [eight] * 4
        + [four] * 6
        + [eight] * 4
        + [four] * 2
        + [relayed] * 2,
        compiler_params=pltpu.CompilerParams(collective_id=2, has_side_effects=True),
        name="exchange",
    )(pg, grad)[:4]


def finish_kernel(obj, grad, weight, total, from_above, from_left, from_diag, new, direction):
    block = pl.program_id(0)
    w = lax.axis_index("wide")
    c = lax.axis_index("col")
    got_above = (block == 0) & (w > 0)
    got_left = c > 0
    got_diag = got_above & got_left

    @pl.when(block == 0)
    def _():
        direction[...] = total[...]

    for ct in range(4):
        lanes = slice(PATCH * ct, PATCH * (ct + 1))
        sums = grad[:, ct]
        sums = sums + jnp.where(got_above, from_above[:, ct], 0.0)
        if ct == 0:
            sums = sums + jnp.where(got_left, from_left[...], 0.0)
            sums = sums + jnp.where(got_diag, from_diag[...], 0.0)
        scale = weight[ct] + 1.0
        for p in range(2):
            new[p, :, lanes] = obj[p, :, lanes] + sums[p] / scale


def finish(obj, grad, weight, total, from_above, from_left, from_diag):
    return pl.pallas_call(
        finish_kernel,
        grid=(4,),
        out_shape=[
            jax.ShapeDtypeStruct((2, TILE, TILE), F32),
            jax.ShapeDtypeStruct((2 * MODES, PATCH, PATCH), F32),
        ],
        in_specs=[
            pl.BlockSpec((2, PATCH, TILE), lambda i: (0, i, 0)),
            pl.BlockSpec((2, 4, PATCH, PATCH), lambda i: (0, 0, i, 0)),
            pl.BlockSpec((4, PATCH, PATCH), lambda i: (0, i, 0)),
            pl.BlockSpec((2 * MODES, PATCH, PATCH), lambda i: (0, 0, 0)),
            pl.BlockSpec((2, 4, PATCH, PATCH), lambda i: (0, 0, 0, 0)),
            pl.BlockSpec((2, PATCH, PATCH), lambda i: (0, i, 0)),
            pl.BlockSpec((2, PATCH, PATCH), lambda i: (0, 0, 0)),
        ],
        out_specs=[
            pl.BlockSpec((2, PATCH, TILE), lambda i: (0, i, 0)),
            pl.BlockSpec((2 * MODES, PATCH, PATCH), lambda i: (0, 0, 0)),
        ],
        name="finish",
    )(obj, grad, weight, total, from_above, from_left, from_diag)


def local(object_field, probe_modes, amplitude, positions, slot_counts):
    slots = positions.shape[2]
    amp = amplitude.reshape(slots, PATCH, PATCH)
    table = left_table()
    tables = (jnp.asarray(table), jnp.asarray(table.T))
    meta = plan(positions.reshape(slots, 2).T, slot_counts)
    (right, lower, diag, *others), early, early_pg = halo_in(
        object_field, meta, probe_modes, tables, amp
    )
    grad, weight, pg = patches(
        (meta, *others), probe_modes, tables, amp, early, early_pg,
        object_field, right, lower, diag,
    )
    total, from_above, from_left, from_diag = exchange(pg, grad)
    new_object, direction = finish(
        object_field, grad, weight, total, from_above, from_left, from_diag
    )
    return new_object, direction.reshape(probe_modes.shape)


def solution(mesh):
    placed = (
        P(None, "wide", "col"),
        P(),
        P("wide", "col", None, None, None),
        P("wide", "col", None, None),
        P("wide", "col"),
    )
    return jax.shard_map(
        local, mesh=mesh, in_specs=placed, out_specs=(P(None, "wide", "col"), P()), check_vma=False
    )
```

```python
import functools
import math

import jax
import jax.numpy as jnp
import ml_dtypes
import numpy as np
from jax import lax
from jax.experimental import pallas as pl
from jax.experimental.pallas import tpu as pltpu
from jax.sharding import PartitionSpec as P

MESH = pl.DeviceIdType.MESH
F32 = jnp.float32
BF16 = jnp.bfloat16
PATCH = 128
TILE = 512
EXT = TILE + PATCH
MODES = 4
RING = 16
PLANES = 2 * MODES + 1
ROWS = PATCH // RING
PAIR = 2
CHUNKS = 5
DIRECT = PATCH - 2 * 8 * CHUNKS
EARLY = 16
INSIDE = TILE - PATCH

VMEM_SPEC = pl.BlockSpec(memory_space=pltpu.VMEM)
SMEM_SPEC = pl.BlockSpec(memory_space=pltpu.SMEM)
ANY_SPEC = pl.BlockSpec(memory_space=pl.ANY)


def left_table():
    indices = np.arange(PATCH)
    angles = (indices[:, None] * indices[None, :] % PATCH) * (2.0 * math.pi / PATCH)
    cosine = np.cos(angles) / math.sqrt(PATCH)
    sine = -np.sin(angles) / math.sqrt(PATCH)
    whole = np.block([[cosine, -sine], [sine, cosine]])
    return whole.astype(np.float32).astype(ml_dtypes.bfloat16)


def plan_kernel(pos_ref, count_ref, meta_ref):
    count = count_ref[0, 0]
    low, high = jnp.int32(0), count - 1
    for s in range(pos_ref.shape[1]):
        row, at = pos_ref[0, s], pos_ref[1, s]
        live = s < count
        inner = live & (row <= INSIDE) & (at <= INSIDE)
        place = jnp.where(inner, low, jnp.where(live, high, s))
        meta_ref[0, place] = row
        meta_ref[1, place] = at
        meta_ref[3, place] = s
        low = low + jnp.where(inner, 1, 0)
        high = high - jnp.where(live & jnp.logical_not(inner), 1, 0)
    for line in (0, 1, 3):
        meta_ref[line, pos_ref.shape[1]] = 0
    meta_ref[2, 0] = count
    meta_ref[2, 1] = low


def plan(positions, slot_counts):
    return pl.pallas_call(
        plan_kernel,
        out_shape=jax.ShapeDtypeStruct((8, PATCH), jnp.int32),
        in_specs=[SMEM_SPEC] * 2,
        out_specs=SMEM_SPEC,
        name="plan",
    )(positions, slot_counts)


def lanes_of():
    return lax.broadcasted_iota(jnp.int32, (PATCH, PATCH), 1)


def both_sides(left, stacked, right_side):
    half = jnp.dot(left, stacked, preferred_element_type=F32).astype(BF16)
    lanes = [slice(PATCH * m, PATCH * (m + 1)) for m in range(MODES)]
    turned = jnp.concatenate(
        [jnp.concatenate([half[:PATCH, at], half[PATCH:, at]], 1) for at in lanes], 0
    )
    return jnp.dot(turned, right_side, preferred_element_type=F32)


def stack(re, im):
    return jnp.concatenate([jnp.concatenate(re, 1), jnp.concatenate(im, 1)], 0)


def parts(values, m):
    rows = slice(PATCH * m, PATCH * (m + 1))
    return values[rows, :PATCH], values[rows, PATCH:]


def solve(slots, ext, last, probe_ref, lt, rt, amp_ref, pg_ref):
    lane = lanes_of()
    patches_of, waves = [], []
    for s, row, at, live in slots:
        ct, shift = lax.shift_right_logical(at, 7), lax.bitwise_and(at, 127)
        back = lax.bitwise_and(PATCH - shift, 127)
        beside = jnp.minimum(ct + 1, last)
        rows = pl.ds(row, PATCH)
        patch = []
        for p in range(2):
            joined = jnp.where(lane >= shift, ext[p, ct, rows, :], ext[p, beside, rows, :])
            patch.append(pltpu.roll(joined, back, 1))
        patches_of.append(patch)
        re, im = [], []
        for m in range(MODES):
            pr, pi = probe_ref[0, m], probe_ref[1, m]
            re.append((pr * patch[0] - pi * patch[1]).astype(BF16))
            im.append((pr * patch[1] + pi * patch[0]).astype(BF16))
        waves.append(stack(re, im))
    fars = [both_sides(lt, wave, rt) for wave in waves]
    residuals = []
    for (s, row, at, live), far in zip(slots, fars):
        intensity = jnp.zeros((PATCH, PATCH), F32)
        for m in range(MODES):
            fr, fi = parts(far, m)
            intensity = intensity + fr * fr + fi * fi
        measured = amp_ref[s].astype(F32)
        factor = (measured * lax.rsqrt(jnp.maximum(intensity, 1.0)) - 1.0) * live
        re, im = [], []
        for m in range(MODES):
            fr, fi = parts(far, m)
            re.append((fr * factor).astype(BF16))
            im.append((fi * factor).astype(BF16))
        residuals.append(stack(re, im))
    updates = [both_sides(rt, residual, lt) for residual in residuals]
    for m in range(MODES):
        sum_re, sum_im = pg_ref[m], pg_ref[MODES + m]
        for patch, update in zip(patches_of, updates):
            ur, ui = parts(update, m)
            sum_re = sum_re + patch[0] * ur + patch[1] * ui
            sum_im = sum_im + patch[0] * ui - patch[1] * ur
        pg_ref[m] = sum_re
        pg_ref[MODES + m] = sum_im
    lit = pg_ref[2 * MODES]
    for (s, row, at, live), patch in zip(slots, patches_of):
        lit = lit + live * (patch[0] * patch[0] + patch[1] * patch[1])
    pg_ref[2 * MODES] = lit
    grads = []
    for update in updates:
        grad_re = jnp.zeros((PATCH, PATCH), F32)
        grad_im = grad_re
        for m in range(MODES):
            pr, pi = probe_ref[0, m], probe_ref[1, m]
            ur, ui = parts(update, m)
            grad_re = grad_re + pr * ur + pi * ui
            grad_im = grad_im + pr * ui - pi * ur
        grads.append((grad_re, grad_im))
    return grads


def remote(source, dest, sent, got, target):
    return pltpu.make_async_remote_copy(
        source, dest, sent, got, device_id=target, device_id_type=MESH
    )


def greet(barrier, target):
    pl.semaphore_signal(barrier, inc=1, device_id=target, device_id_type=MESH)


def halo_in_kernel(
    obj, meta, meta_ref, probe_ref, lt_ref, rt_ref, amp,
    right, lower, diag, meta_above, meta_left, meta_diag, early, pg_ref,
    ext, amp_ref, early_ref, passing, fetched, stored, sent, got, sent_to, got_to, sent_on, got_on,
):
    w = lax.axis_index("wide")
    c = lax.axis_index("col")
    y, k = lax.rem(w, 4), lax.div(w, 4)
    above, below = lax.rem(w + 15, 16), lax.rem(w + 1, 16)
    before, after = lax.rem(c + 15, 16), lax.rem(c + 1, 16)
    far_send, far_get = (y == 0) & (k > 0), (y == 3) & (k < 3)
    relays = ((y == 3) | (y == 1)) & (k > 0)
    route = jnp.where(y == 1, 1, 0)
    onward_to = lax.rem(w + jnp.where(y == 1, 14, 12), 16)
    barrier = pltpu.get_barrier_semaphore()
    for target in (
        (w, after), (below, c), (below, after), (w, before), (above, c), (above, before)
    ):
        greet(barrier, target)
    pl.when(relays & (y == 3))(lambda: greet(barrier, (lax.rem(w + 13, 16), c)))

    @pl.when(far_get)
    def _():
        greet(barrier, (lax.rem(w + 4, 16), c))
        greet(barrier, (lax.rem(w + 2, 16), c))

    inward = [pltpu.make_async_copy(amp, amp_ref, fetched.at[4])]
    for ct in range(4):
        inward.append(pltpu.make_async_copy(
            obj.at[:, :, pl.ds(PATCH * ct, PATCH)], ext.at[:, ct], fetched.at[ct]
        ))
    for copy in inward:
        copy.start()
    pl.semaphore_wait(barrier, 6 + jnp.where(far_send | relays, 1, 0))

    def strip(first, rows):
        return pl.ds(first, rows)

    def to_relay(r, j):
        at = strip(DIRECT + 8 * (r * CHUNKS + j), 8)
        return remote(
            obj.at[:, at, :], passing.at[j], sent_to.at[r * CHUNKS + j], got_to.at[j],
            (lax.rem(w + (1 if r else 3), 16), c),
        )

    def onward(r, j):
        start = pl.multiple_of(DIRECT + 8 * (r * CHUNKS + j), 8)
        return remote(
            passing.at[j], lower.at[:, strip(start, 8), :],
            sent_on.at[j], got_on.at[r * CHUNKS + j], (onward_to, c),
        )

    @pl.when(far_send)
    def _():
        for j in range(CHUNKS):
            for r in range(2):
                to_relay(r, j).start()

    ups, downs = w > 0, w < 15
    lefts, rights = c > 0, c < 15
    near_send = ups & jnp.logical_not(far_send)
    near_get = downs & jnp.logical_not(far_get)
    top = pl.ds(0, PATCH)
    some, rest = strip(0, DIRECT), strip(DIRECT, PATCH - DIRECT)
    plain = (
        (meta, meta_above, (below, c), downs, ups),
        (meta, meta_left, (w, after), rights, lefts),
        (meta, meta_diag, (below, after), downs & rights, ups & lefts),
        (obj.at[:, some, :], lower.at[:, some, :], (above, c), ups, downs),
        (obj.at[:, rest, :], lower.at[:, rest, :], (above, c), near_send, near_get),
        (obj.at[:, top, top], diag, (above, before), ups & lefts, downs & rights),
        (obj.at[:, :, top], right, (w, before), lefts, rights),
    )
    made = []
    for j, (source, dest, target, sends, gets) in enumerate(plain):
        copy = remote(source, dest, sent.at[j], got.at[j], target)
        pl.when(sends)(copy.start)
        made.append((copy, sends, gets))

    pg_ref[...] = jnp.zeros(pg_ref.shape, F32)
    lt = lt_ref[...]
    rt = rt_ref[...]
    inner = meta_ref[2, 1]
    for copy in inward:
        copy.wait()

    def put(index):
        pair = pl.ds(index * PAIR, PAIR)
        return pltpu.make_async_copy(early_ref.at[pair], early.at[pair], stored.at[index])

    def step(index, carry):
        slots = []
        for u in range(PAIR):
            j = index * PAIR + u
            row, at = jnp.minimum(meta_ref[0, j], INSIDE), jnp.minimum(meta_ref[1, j], INSIDE)
            slots.append((meta_ref[3, j], row, at, (j < inner).astype(F32)))
        grads = solve(slots, ext, 3, probe_ref, lt, rt, amp_ref, pg_ref)
        for u, (grad_re, grad_im) in enumerate(grads):
            early_ref[index * PAIR + u, 0] = grad_re
            early_ref[index * PAIR + u, 1] = grad_im
        put(index).start()

        @pl.when(relays & (index > 0) & (index <= CHUNKS))
        def _():
            to_relay(0, index - 1).wait_recv()
            onward(route, index - 1).start()

        return carry

    lax.fori_loop(0, EARLY // PAIR, step, 0)
    for index in range(EARLY // PAIR):
        put(index).wait()
    for copy, sends, gets in made:
        pl.when(gets)(copy.wait_recv)
        pl.when(sends)(copy.wait_send)

    @pl.when(far_get)
    def _():
        for r in range(2):
            for j in range(CHUNKS):
                onward(r, j).wait_recv()

    @pl.when(relays)
    def _():
        for j in range(CHUNKS):
            onward(0, j).wait_send()

    @pl.when(far_send)
    def _():
        for r in range(2):
            for j in range(CHUNKS):
                to_relay(r, j).wait_send()


def halo_in(obj, meta, probe, tables, amp):
    note = jax.ShapeDtypeStruct(meta.shape, meta.dtype)
    made = pl.pallas_call(
        halo_in_kernel,
        out_shape=[
            jax.ShapeDtypeStruct((2, TILE, PATCH), F32),
            jax.ShapeDtypeStruct((2, PATCH, TILE), F32),
            jax.ShapeDtypeStruct((2, PATCH, PATCH), F32),
            note,
            note,
            note,
            jax.ShapeDtypeStruct((EARLY, 2, PATCH, PATCH), F32),
            jax.ShapeDtypeStruct((PLANES, PATCH, PATCH), F32),
        ],
        in_specs=[ANY_SPEC] * 2 + [SMEM_SPEC] + [VMEM_SPEC] * 3 + [ANY_SPEC],
        out_specs=[ANY_SPEC] * 7 + [VMEM_SPEC],
        scratch_shapes=[
            pltpu.VMEM((2, 4, TILE, PATCH), F32),
            pltpu.VMEM(amp.shape, amp.dtype),
            pltpu.VMEM((EARLY, 2, PATCH, PATCH), F32),
            pltpu.VMEM((CHUNKS, 2, 8, TILE), F32),
            pltpu.SemaphoreType.DMA((5,)),
            pltpu.SemaphoreType.DMA((EARLY // PAIR,)),
        ]
        + [pltpu.SemaphoreType.DMA((7,))] * 2
        + [pltpu.SemaphoreType.DMA((2 * CHUNKS,)), pltpu.SemaphoreType.DMA((CHUNKS,))]
        + [pltpu.SemaphoreType.DMA((CHUNKS,)), pltpu.SemaphoreType.DMA((2 * CHUNKS,))],
        compiler_params=pltpu.CompilerParams(
            collective_id=1, has_side_effects=True, vmem_limit_bytes=56 * 2**20
        ),
        name="halo_in",
    )(obj, meta, meta, probe, *tables, amp)
    return made[:6], made[6], made[7]


def patches_kernel(
    meta_ref, above_ref, left_ref, diag_ref, probe_ref, lt_ref, rt_ref,
    early_pg, amp, early, obj, right, lower, diag,
    grad_ref, weight, pg_ref, ext, spread, amp_ref, early_ref, sems, stored,
):
    copies = []

    def fetch(source, dest):
        copy = pltpu.make_async_copy(source, dest, sems.at[len(copies)])
        copy.start()
        copies.append(copy)

    fetch(early, early_ref)
    fetch(amp, amp_ref)
    for ct in range(4):
        lanes = pl.ds(PATCH * ct, PATCH)
        fetch(obj.at[:, :, lanes], ext.at[:, ct, pl.ds(0, TILE), :])
        fetch(lower.at[:, :, lanes], ext.at[:, ct, pl.ds(TILE, PATCH), :])
    fetch(right, ext.at[:, 4, pl.ds(0, TILE), :])
    fetch(diag, ext.at[:, 4, pl.ds(TILE, PATCH), :])
    grad_ref[...] = jnp.zeros(grad_ref.shape, F32)
    spread[...] = jnp.zeros(spread.shape, F32)
    pg_ref[...] = early_pg[...]
    w = lax.axis_index("wide")
    c = lax.axis_index("col")
    lane = lanes_of()
    count = meta_ref[2, 0]
    done = jnp.minimum(meta_ref[2, 1], EARLY)
    power = jnp.sum(probe_ref[...] * probe_ref[...], axis=(0, 1))

    def scatter(ref, row, at, value):
        ct, shift = lax.shift_right_logical(at, 7), lax.bitwise_and(at, 127)
        turned = pltpu.roll(value, shift, 1)
        first = lane >= shift
        zero = jnp.zeros_like(turned)
        rows = pl.ds(row, PATCH)
        ref[ct, rows, :] += jnp.where(first, turned, zero)
        ref[ct + 1, rows, :] += jnp.where(first, zero, turned)

    for ref, there, down, side in (
        (meta_ref, None, 0, 0),
        (above_ref, w > 0, TILE, 0),
        (left_ref, c > 0, 0, TILE),
        (diag_ref, (w > 0) & (c > 0), TILE, TILE),
    ):
        live_there = ref[2, 0] if there is None else jnp.where(there, ref[2, 0], 0)

        def weigh(s, carry, ref=ref, down=down, side=side):
            row, at = ref[0, s] + (PATCH - down), ref[1, s] + (PATCH - side)
            touches = None
            if down:
                touches = row > 0
            if side:
                touches = at > 0 if touches is None else touches & (at > 0)
            if touches is None:
                scatter(spread, row, at, power)
            else:
                pl.when(touches)(lambda: scatter(spread, row, at, power))
            return carry

        lax.fori_loop(0, live_there, weigh, 0)
    weights_out = pltpu.make_async_copy(
        spread.at[pl.ds(1, 4), pl.ds(PATCH, TILE), :], weight, stored.at[0]
    )
    weights_out.start()
    copies[0].wait()

    def place(j, carry):
        for p in range(2):
            scatter(grad_ref.at[p], meta_ref[0, j], meta_ref[1, j], early_ref[j, p])
        return carry

    lax.fori_loop(0, done, place, 0)
    for copy in copies[1:]:
        copy.wait()

    @pl.when(w == 15)
    def _():
        ext[:, :, TILE:, :] = jnp.zeros((2, 5, PATCH, PATCH), F32)

    @pl.when(c == 15)
    def _():
        ext[:, 4, :, :] = jnp.zeros((2, EXT, PATCH), F32)

    lt = lt_ref[...]
    rt = rt_ref[...]

    def step(index, carry):
        slots = []
        for u in range(PAIR):
            j = done + index * PAIR + u
            slots.append((meta_ref[3, j], meta_ref[0, j], meta_ref[1, j], (j < count).astype(F32)))
        grads = solve(slots, ext, 4, probe_ref, lt, rt, amp_ref, pg_ref)
        for (s, row, at, live), (grad_re, grad_im) in zip(slots, grads):
            scatter(grad_ref.at[0], row, at, grad_re)
            scatter(grad_ref.at[1], row, at, grad_im)
        return carry

    lax.fori_loop(0, (count - done + PAIR - 1) // PAIR, step, 0)
    weights_out.wait()


def patches(metas, probe, tables, amp, early, early_pg, obj, right, lower, diag):
    return pl.pallas_call(
        patches_kernel,
        out_shape=[
            jax.ShapeDtypeStruct((2, 5, EXT, PATCH), F32),
            jax.ShapeDtypeStruct((4, TILE, PATCH), F32),
            jax.ShapeDtypeStruct((PLANES, PATCH, PATCH), F32),
        ],
        in_specs=[SMEM_SPEC] * 4 + [VMEM_SPEC] * 4 + [ANY_SPEC] * 6,
        out_specs=[VMEM_SPEC, ANY_SPEC, VMEM_SPEC],
        scratch_shapes=[
            pltpu.VMEM((2, 5, EXT, PATCH), F32),
            pltpu.VMEM((6, EXT + PATCH, PATCH), F32),
            pltpu.VMEM(amp.shape, amp.dtype),
            pltpu.VMEM(early.shape, early.dtype),
            pltpu.SemaphoreType.DMA((12,)),
            pltpu.SemaphoreType.DMA((1,)),
        ],
        compiler_params=pltpu.CompilerParams(vmem_limit_bytes=56 * 2**20),
        name="patches",
    )(*metas, probe, *tables, early_pg, amp, early, obj, right, lower, diag)


def exchange_kernel(
    pg, grad, total, from_above, from_left, from_diag,
    buf0, red0, buf1, red1, buf2, buf3, own, res, passing,
    s0, r0, s1, r1, s2, r2, s3, r3, s4, r4, s5, r5, s6, r6, sh, rh, sent_to, got_to, sent_on, got_on,
):
    w = lax.axis_index("wide")
    c = lax.axis_index("col")
    y, k = lax.rem(w, 4), lax.div(w, 4)
    core, chip = lax.rem(c, 2), lax.div(c, 2)
    sibling = (w, 2 * chip + 1 - core)
    above, below = lax.rem(w + 15, 16), lax.rem(w + 1, 16)
    before, after = lax.rem(c + 15, 16), lax.rem(c + 1, 16)
    far_send, far_get = (y == 3) & (k < 3), (y == 0) & (k > 0)
    relays = ((y == 0) | (y == 2)) & (k < 3)
    route = jnp.where(y == 2, 1, 0)
    onward_to = lax.rem(w + jnp.where(y == 2, 2, 4), 16)

    def rows(index, half):
        return pl.ds(pl.multiple_of(index * ROWS + half * (PATCH // 2), ROWS), ROWS)

    def planes(index):
        return pl.ds(index * 3, 3)

    chips = [(w, lax.rem(chip + d, 8) * 2 + core) for d in range(1, 8)]
    along_y = [(k * 4 + lax.rem(y + d, 4), c) for d in range(1, 4)]
    along_z = [(lax.rem(w + 4 * d, 16), c) for d in range(1, 4)]
    barrier = pltpu.get_barrier_semaphore()
    for target in [sibling] + chips + along_y + along_z:
        greet(barrier, target)
    for target in ((w, before), (above, c), (above, before)):
        greet(barrier, target)

    @pl.when(far_get)
    def _():
        greet(barrier, (lax.rem(w + 12, 16), c))
        greet(barrier, (lax.rem(w + 14, 16), c))

    pl.semaphore_wait(barrier, 17 + jnp.where(relays, 1, 0))

    zeroth = []
    for d in range(1, 9):
        p = lax.rem(chip + d, 8)
        copy = remote(pg.at[:, rows(p, 1 - core), :], buf0.at[d - 1], s0.at[d - 1], r0.at[d - 1], sibling)
        copy.start()
        zeroth.append(copy)

    def to_relay(r, j):
        at = TILE + DIRECT + 8 * (r * CHUNKS + j)
        return remote(
            grad.at[:, pl.ds(0, 4), pl.ds(at, 8), :], passing.at[j],
            sent_to.at[r * CHUNKS + j], got_to.at[j], (lax.rem(w + (15 if r else 13), 16), c),
        )

    def onward(r, j):
        at = pl.multiple_of(DIRECT + 8 * (r * CHUNKS + j), 8)
        return remote(
            passing.at[j], from_above.at[:, :, pl.ds(at, 8), :],
            sent_on.at[j], got_on.at[r * CHUNKS + j], (onward_to, c),
        )

    def pass_on(chunks):
        @pl.when(relays)
        def _():
            for j in chunks:
                to_relay(0, j).wait_recv()
                onward(route, j).start()

    ups, downs = w > 0, w < 15
    lefts, rights = c > 0, c < 15
    near_send = downs & jnp.logical_not(far_send)
    near_get = ups & jnp.logical_not(far_get)
    strips = []

    def post(source, dest, target, sends, gets):
        copy = remote(source, dest, sh.at[len(strips)], rh.at[len(strips)], target)
        pl.when(sends)(copy.start)
        strips.append((copy, sends, gets))

    def post_rows(first, size, sends, gets):
        post(
            grad.at[:, pl.ds(0, 4), pl.ds(TILE + first, size), :],
            from_above.at[:, :, pl.ds(first, size), :], (below, c), sends, gets,
        )

    def post_columns(first, size):
        at = pl.ds(first, size)
        post(grad.at[:, 4, at, :], from_left.at[:, at, :], (w, after), rights, lefts)

    @pl.when(far_send)
    def _():
        for j in range(CHUNKS):
            for r in range(2):
                to_relay(r, j).start()

    post_rows(DIRECT, 40, near_send, near_get)
    first = []
    for d in range(1, 8):
        p = lax.rem(chip + d, 8)
        zeroth[d - 1].wait_recv()
        red0[d - 1] = pg[:, rows(p, core), :] + buf0[d - 1]
        copy = remote(red0.at[d - 1], buf1.at[d], s1.at[d], r1.at[d], chips[d - 1])
        copy.start()
        first.append(copy)
    zeroth[7].wait_recv()
    acc = pg[:, rows(chip, core), :] + buf0[7]

    post_rows(DIRECT + 40, 40, near_send, near_get)
    post(
        grad.at[:, 4, pl.ds(TILE, PATCH), :], from_diag, (below, after),
        downs & rights, ups & lefts,
    )
    pass_on(range(2))
    for d in range(1, 8):
        first[d - 1].wait_recv()
        acc = acc + buf1[d]
    red1[pl.ds(0, PLANES)] = acc
    red1[pl.ds(PLANES, 3)] = jnp.zeros((3, ROWS, PATCH), F32)
    second = []
    for d in range(1, 4):
        copy = remote(
            red1.at[planes(lax.rem(y + d, 4))], buf2.at[d], s2.at[d], r2.at[d], along_y[d - 1]
        )
        copy.start()
        second.append(copy)
    pass_on(range(2, CHUNKS))
    post_rows(0, 24, downs, ups)
    post_columns(0, 256)
    acc = red1[planes(y)]
    for d in range(1, 4):
        second[d - 1].wait_recv()
        acc = acc + buf2[d]
    buf3[k] = acc
    third = []
    for d in range(1, 4):
        copy = remote(buf3.at[k], buf3.at[k], s3.at[d], r3.at[d], along_z[d - 1])
        copy.start()
        third.append(copy)
    post_rows(24, 24, downs, ups)
    post_columns(256, 256)
    for d in range(1, 4):
        p = lax.rem(k + 4 - d, 4)
        remote(buf3.at[p], buf3.at[p], s3.at[d], r3.at[d], along_z[d - 1]).wait_recv()
    own[planes(y)] = buf3[0] + buf3[1] + buf3[2] + buf3[3]
    fourth = []
    for d in range(1, 4):
        copy = remote(own.at[planes(y)], own.at[planes(y)], s4.at[d], r4.at[d], along_y[d - 1])
        copy.start()
        fourth.append(copy)
    for d in range(1, 4):
        p = planes(lax.rem(y + 4 - d, 4))
        remote(own.at[p], own.at[p], s4.at[d], r4.at[d], along_y[d - 1]).wait_recv()
    lit = own[2 * MODES]
    res[...] = own[pl.ds(0, 2 * MODES)] / jnp.sqrt(lit + 1.0)[None]

    mine = rows(chip, core)
    fifth, sixth = [], []
    for d in range(1, 8):
        copy = remote(res, total.at[:, mine, :], s5.at[d], r5.at[d], chips[d - 1])
        copy.start()
        fifth.append(copy)
    copy = remote(res, total.at[:, mine, :], s6.at[0], r6.at[0], sibling)
    copy.start()
    sixth.append(copy)
    total[:, mine, :] = res[...]
    for d in range(1, 8):
        at = rows(lax.rem(chip + 8 - d, 8), core)
        remote(res, total.at[:, at, :], s5.at[d], r5.at[d], chips[d - 1]).wait_recv()
        copy = remote(total.at[:, at, :], total.at[:, at, :], s6.at[d], r6.at[d], sibling)
        copy.start()
        sixth.append(copy)
    for copy in zeroth + first + second + third + fourth + fifth:
        copy.wait_send()
    for d in range(8):
        at = rows(lax.rem(chip + 8 - d, 8), 1 - core)
        remote(res, total.at[:, at, :], s6.at[d], r6.at[d], sibling).wait_recv()
    for copy in sixth:
        copy.wait_send()
    for copy, sends, gets in strips:
        pl.when(gets)(copy.wait_recv)
        pl.when(sends)(copy.wait_send)

    @pl.when(far_get)
    def _():
        for r in range(2):
            for j in range(CHUNKS):
                onward(r, j).wait_recv()

    @pl.when(relays)
    def _():
        for j in range(CHUNKS):
            onward(0, j).wait_send()

    @pl.when(far_send)
    def _():
        for r in range(2):
            for j in range(CHUNKS):
                to_relay(r, j).wait_send()


def exchange(pg, grad):
    eight = pltpu.SemaphoreType.DMA((8,))
    four = pltpu.SemaphoreType.DMA((4,))
    ten = pltpu.SemaphoreType.DMA((2 * CHUNKS,))
    five = pltpu.SemaphoreType.DMA((CHUNKS,))
    return pl.pallas_call(
        exchange_kernel,
        out_shape=[
            jax.ShapeDtypeStruct((2 * MODES, PATCH, PATCH), F32),
            jax.ShapeDtypeStruct((2, 4, PATCH, PATCH), F32),
            jax.ShapeDtypeStruct((2, TILE, PATCH), F32),
            jax.ShapeDtypeStruct((2, PATCH, PATCH), F32),
        ],
        in_specs=[VMEM_SPEC, ANY_SPEC],
        out_specs=[VMEM_SPEC] + [ANY_SPEC] * 3,
        scratch_shapes=[
            pltpu.VMEM((8, PLANES, ROWS, PATCH), F32),
            pltpu.VMEM((8, PLANES, ROWS, PATCH), F32),
            pltpu.VMEM((8, PLANES, ROWS, PATCH), F32),
            pltpu.VMEM((12, ROWS, PATCH), F32),
            pltpu.VMEM((4, 3, ROWS, PATCH), F32),
            pltpu.VMEM((4, 3, ROWS, PATCH), F32),
            pltpu.VMEM((12, ROWS, PATCH), F32),
            pltpu.VMEM((2 * MODES, ROWS, PATCH), F32),
            pltpu.VMEM((CHUNKS, 2, 4, 8, PATCH), F32),
        ]
        + [eight] * 4
        + [four] * 6
        + [eight] * 4
        + [eight] * 2
        + [ten, five, five, ten],
        compiler_params=pltpu.CompilerParams(collective_id=2, has_side_effects=True),
        name="exchange",
    )(pg, grad)


def finish_kernel(obj, grad, weight, total, from_above, from_left, from_diag, new, direction):
    block = pl.program_id(0)
    w = lax.axis_index("wide")
    c = lax.axis_index("col")
    got_above = (block == 0) & (w > 0)
    got_left = c > 0
    got_diag = got_above & got_left

    @pl.when(block == 0)
    def _():
        direction[...] = total[...]

    for ct in range(4):
        lanes = slice(PATCH * ct, PATCH * (ct + 1))
        sums = grad[:, ct]
        sums = sums + jnp.where(got_above, from_above[:, ct], 0.0)
        if ct == 0:
            sums = sums + jnp.where(got_left, from_left[...], 0.0)
            sums = sums + jnp.where(got_diag, from_diag[...], 0.0)
        scale = weight[ct] + 1.0
        for p in range(2):
            new[p, :, lanes] = obj[p, :, lanes] + sums[p] / scale


def finish(obj, grad, weight, total, from_above, from_left, from_diag):
    return pl.pallas_call(
        finish_kernel,
        grid=(4,),
        out_shape=[
            jax.ShapeDtypeStruct((2, TILE, TILE), F32),
            jax.ShapeDtypeStruct((2 * MODES, PATCH, PATCH), F32),
        ],
        in_specs=[
            pl.BlockSpec((2, PATCH, TILE), lambda i: (0, i, 0)),
            pl.BlockSpec((2, 4, PATCH, PATCH), lambda i: (0, 0, i, 0)),
            pl.BlockSpec((4, PATCH, PATCH), lambda i: (0, i, 0)),
            pl.BlockSpec((2 * MODES, PATCH, PATCH), lambda i: (0, 0, 0)),
            pl.BlockSpec((2, 4, PATCH, PATCH), lambda i: (0, 0, 0, 0)),
            pl.BlockSpec((2, PATCH, PATCH), lambda i: (0, i, 0)),
            pl.BlockSpec((2, PATCH, PATCH), lambda i: (0, 0, 0)),
        ],
        out_specs=[
            pl.BlockSpec((2, PATCH, TILE), lambda i: (0, i, 0)),
            pl.BlockSpec((2 * MODES, PATCH, PATCH), lambda i: (0, 0, 0)),
        ],
        name="finish",
    )(obj, grad, weight, total, from_above, from_left, from_diag)


def local(object_field, probe_modes, amplitude, positions, slot_counts):
    slots = positions.shape[2]
    amp = amplitude.reshape(slots, PATCH, PATCH)
    table = left_table()
    tables = (jnp.asarray(table), jnp.asarray(table.T))
    meta = plan(positions.reshape(slots, 2).T, slot_counts)
    (right, lower, diag, *others), early, early_pg = halo_in(
        object_field, meta, probe_modes, tables, amp
    )
    grad, weight, pg = patches(
        (meta, *others), probe_modes, tables, amp, early, early_pg,
        object_field, right, lower, diag,
    )
    total, from_above, from_left, from_diag = exchange(pg, grad)
    new_object, direction = finish(
        object_field, grad, weight, total, from_above, from_left, from_diag
    )
    return new_object, direction.reshape(probe_modes.shape)


def solution(mesh):
    placed = (
        P(None, "wide", "col"),
        P(),
        P("wide", "col", None, None, None),
        P("wide", "col", None, None),
        P("wide", "col"),
    )
    return jax.shard_map(
        local, mesh=mesh, in_specs=placed, out_specs=(P(None, "wide", "col"), P()), check_vma=False
    )
```

```python
import functools
import math

import jax
import jax.numpy as jnp
import ml_dtypes
import numpy as np
from jax import lax
from jax.experimental import pallas as pl
from jax.experimental.pallas import tpu as pltpu
from jax.sharding import PartitionSpec as P

MESH = pl.DeviceIdType.MESH
F32 = jnp.float32
BF16 = jnp.bfloat16
PATCH = 128
TILE = 512
EXT = TILE + PATCH
MODES = 4
RING = 16
PLANES = 2 * MODES + 1
ROWS = PATCH // RING
PAIR = 2
CHUNKS = 5
ROUTES = 3
DIRECT = PATCH - ROUTES * 8 * CHUNKS
GROUP = 4
FIRST = 16
EARLY = 24
REST = TILE - PATCH
INSIDE = TILE - PATCH

VMEM_SPEC = pl.BlockSpec(memory_space=pltpu.VMEM)
SMEM_SPEC = pl.BlockSpec(memory_space=pltpu.SMEM)
ANY_SPEC = pl.BlockSpec(memory_space=pl.ANY)


def left_table():
    indices = np.arange(PATCH)
    angles = (indices[:, None] * indices[None, :] % PATCH) * (2.0 * math.pi / PATCH)
    cosine = np.cos(angles) / math.sqrt(PATCH)
    sine = -np.sin(angles) / math.sqrt(PATCH)
    whole = np.block([[cosine, -sine], [sine, cosine]])
    return whole.astype(np.float32).astype(ml_dtypes.bfloat16)


def plan_kernel(pos_ref, count_ref, meta_ref):
    count = count_ref[0, 0]
    slots = []
    inner_count, upper_count = jnp.int32(0), jnp.int32(0)
    for s in range(pos_ref.shape[1]):
        row, at = pos_ref[0, s], pos_ref[1, s]
        live = s < count
        upper = live & (row <= INSIDE)
        inner = upper & (at <= INSIDE)
        slots.append((row, at, live, upper, inner))
        inner_count = inner_count + jnp.where(inner, 1, 0)
        upper_count = upper_count + jnp.where(upper, 1, 0)
    low, middle, high = jnp.int32(0), inner_count, upper_count
    for s, (row, at, live, upper, inner) in enumerate(slots):
        outer = upper & jnp.logical_not(inner)
        place = jnp.where(inner, low, jnp.where(outer, middle, jnp.where(live, high, s)))
        meta_ref[0, place] = row
        meta_ref[1, place] = at
        meta_ref[3, place] = s
        low = low + jnp.where(inner, 1, 0)
        middle = middle + jnp.where(outer, 1, 0)
        high = high + jnp.where(live & jnp.logical_not(upper), 1, 0)
    for line in (0, 1, 3):
        for past in range(pos_ref.shape[1], pos_ref.shape[1] + EARLY):
            meta_ref[line, past] = 0
    meta_ref[2, 0] = count
    meta_ref[2, 1] = inner_count
    meta_ref[2, 2] = upper_count


def plan(positions, slot_counts):
    return pl.pallas_call(
        plan_kernel,
        out_shape=jax.ShapeDtypeStruct((8, PATCH), jnp.int32),
        in_specs=[SMEM_SPEC] * 2,
        out_specs=SMEM_SPEC,
        name="plan",
    )(positions, slot_counts)


def lanes_of():
    return lax.broadcasted_iota(jnp.int32, (PATCH, PATCH), 1)


def both_sides(left, stacked, right_side):
    half = jnp.dot(left, stacked, preferred_element_type=F32).astype(BF16)
    lanes = [slice(PATCH * m, PATCH * (m + 1)) for m in range(MODES)]
    turned = jnp.concatenate(
        [jnp.concatenate([half[:PATCH, at], half[PATCH:, at]], 1) for at in lanes], 0
    )
    return jnp.dot(turned, right_side, preferred_element_type=F32)


def stack(re, im):
    return jnp.concatenate([jnp.concatenate(re, 1), jnp.concatenate(im, 1)], 0)


def parts(values, m):
    rows = slice(PATCH * m, PATCH * (m + 1))
    return values[rows, :PATCH], values[rows, PATCH:]


def solve(slots, ext, last, probe_ref, lt, rt, amp_ref, pg_ref):
    lane = lanes_of()
    patches_of, waves = [], []
    for s, row, at, live in slots:
        ct, shift = lax.shift_right_logical(at, 7), lax.bitwise_and(at, 127)
        back = lax.bitwise_and(PATCH - shift, 127)
        beside = jnp.minimum(ct + 1, last)
        rows = pl.ds(row, PATCH)
        patch = []
        for p in range(2):
            joined = jnp.where(lane >= shift, ext[p, ct, rows, :], ext[p, beside, rows, :])
            patch.append(pltpu.roll(joined, back, 1))
        patches_of.append(patch)
        re, im = [], []
        for m in range(MODES):
            pr, pi = probe_ref[0, m], probe_ref[1, m]
            re.append((pr * patch[0] - pi * patch[1]).astype(BF16))
            im.append((pr * patch[1] + pi * patch[0]).astype(BF16))
        waves.append(stack(re, im))
    fars = [both_sides(lt, wave, rt) for wave in waves]
    residuals = []
    for (s, row, at, live), far in zip(slots, fars):
        intensity = jnp.zeros((PATCH, PATCH), F32)
        for m in range(MODES):
            fr, fi = parts(far, m)
            intensity = intensity + fr * fr + fi * fi
        measured = amp_ref[s].astype(F32)
        factor = (measured * lax.rsqrt(jnp.maximum(intensity, 1.0)) - 1.0) * live
        re, im = [], []
        for m in range(MODES):
            fr, fi = parts(far, m)
            re.append((fr * factor).astype(BF16))
            im.append((fi * factor).astype(BF16))
        residuals.append(stack(re, im))
    updates = [both_sides(rt, residual, lt) for residual in residuals]
    for m in range(MODES):
        sum_re, sum_im = pg_ref[m], pg_ref[MODES + m]
        for patch, update in zip(patches_of, updates):
            ur, ui = parts(update, m)
            sum_re = sum_re + patch[0] * ur + patch[1] * ui
            sum_im = sum_im + patch[0] * ui - patch[1] * ur
        pg_ref[m] = sum_re
        pg_ref[MODES + m] = sum_im
    lit = pg_ref[2 * MODES]
    for (s, row, at, live), patch in zip(slots, patches_of):
        lit = lit + live * (patch[0] * patch[0] + patch[1] * patch[1])
    pg_ref[2 * MODES] = lit
    grads = []
    for update in updates:
        grad_re = jnp.zeros((PATCH, PATCH), F32)
        grad_im = grad_re
        for m in range(MODES):
            pr, pi = probe_ref[0, m], probe_ref[1, m]
            ur, ui = parts(update, m)
            grad_re = grad_re + pr * ur + pi * ui
            grad_im = grad_im + pr * ui - pi * ur
        grads.append((grad_re, grad_im))
    return grads


def remote(source, dest, sent, got, target):
    return pltpu.make_async_remote_copy(
        source, dest, sent, got, device_id=target, device_id_type=MESH
    )


def greet(barrier, target):
    pl.semaphore_signal(barrier, inc=1, device_id=target, device_id_type=MESH)


def halo_in_kernel(
    obj, meta, meta_ref, probe, left_side, right_side, amp,
    right, lower, diag, meta_above, meta_left, meta_diag, early, pg_ref,
    ext, wide_ext, amp_ref, probe_ref, lt_ref, rt_ref, early_ref, passing, fetched, stored,
    sent, got, sent_to, got_to, sent_on, got_on,
):
    w = lax.axis_index("wide")
    c = lax.axis_index("col")
    y, k = lax.rem(w, 4), lax.div(w, 4)
    above, below = lax.rem(w + 15, 16), lax.rem(w + 1, 16)
    before, after = lax.rem(c + 15, 16), lax.rem(c + 1, 16)
    far_send, far_get = (y == 0) & (k > 0), (y == 3) & (k < 3)
    relays = (y > 0) & (k > 0)
    route = jnp.maximum(y - 1, 0)
    onward_to = lax.rem(w + 15 - y, 16)
    barrier = pltpu.get_barrier_semaphore()
    for target in (
        (w, after), (below, c), (below, after), (w, before), (above, c), (above, before)
    ):
        greet(barrier, target)
    pl.when(relays & (y > 1))(lambda: greet(barrier, (lax.rem(w + 16 - y, 16), c)))

    @pl.when(far_get)
    def _():
        for r in range(ROUTES):
            greet(barrier, (lax.rem(w + 2 + r, 16), c))

    inward = [
        pltpu.make_async_copy(source, dest, fetched.at[10 + j])
        for j, (source, dest) in enumerate(
            ((amp, amp_ref), (probe, probe_ref), (left_side, lt_ref), (right_side, rt_ref))
        )
    ]
    for ct in range(4):
        inward.append(pltpu.make_async_copy(
            obj.at[:, :, pl.ds(PATCH * ct, PATCH)], ext.at[:, ct], fetched.at[ct]
        ))
    beside = [
        pltpu.make_async_copy(
            obj.at[:, :, pl.ds(PATCH * ct, PATCH)], wide_ext.at[:, ct], fetched.at[5 + ct]
        )
        for ct in range(4)
    ]
    for copy in inward + beside:
        copy.start()
    pl.semaphore_wait(barrier, 6 + jnp.where(far_send, 2, jnp.where(relays, 1, 0)))

    def strip(first, rows):
        return pl.ds(first, rows)

    def to_relay(r, j):
        at = strip(DIRECT + 8 * (r * CHUNKS + j), 8)
        return remote(
            obj.at[:, at, :], passing.at[j], sent_to.at[r * CHUNKS + j], got_to.at[j],
            (lax.rem(w + r + 1, 16), c),
        )

    def onward(r, j):
        start = pl.multiple_of(DIRECT + 8 * (r * CHUNKS + j), 8)
        return remote(
            passing.at[j], lower.at[:, strip(start, 8), :],
            sent_on.at[j], got_on.at[r * CHUNKS + j], (onward_to, c),
        )

    @pl.when(far_send)
    def _():
        for j in range(CHUNKS):
            for r in reversed(range(ROUTES)):
                to_relay(r, j).start()

    ups, downs = w > 0, w < 15
    lefts, rights = c > 0, c < 15
    near_send = ups & jnp.logical_not(far_send)
    near_get = downs & jnp.logical_not(far_get)
    top = pl.ds(0, PATCH)
    some, rest = strip(0, DIRECT), strip(DIRECT, PATCH - DIRECT)
    plain = (
        (meta, meta_above, (below, c), downs, ups),
        (meta, meta_left, (w, after), rights, lefts),
        (meta, meta_diag, (below, after), downs & rights, ups & lefts),
        (obj.at[:, some, :], lower.at[:, some, :], (above, c), ups, downs),
        (obj.at[:, rest, :], lower.at[:, rest, :], (above, c), near_send, near_get),
        (obj.at[:, top, top], diag, (above, before), ups & lefts, downs & rights),
        (obj.at[:, :, top], wide_ext.at[:, 4], (w, before), lefts, rights),
    )
    made = []
    for j, (source, dest, target, sends, gets) in enumerate(plain):
        copy = remote(source, dest, sent.at[j], got.at[j], target)
        pl.when(sends)(copy.start)
        made.append((copy, sends, gets))

    pg_ref[...] = jnp.zeros(pg_ref.shape, F32)
    inner = meta_ref[2, 1]
    for copy in inward:
        copy.wait()
    lt = lt_ref[...]
    rt = rt_ref[...]

    def put(index):
        pair = pl.ds(index * GROUP, GROUP)
        return pltpu.make_async_copy(early_ref.at[pair], early.at[pair], stored.at[index])

    def solve_some(index, first_slot, live_slots, tiles, last, columns):
        slots = []
        for u in range(GROUP):
            j = first_slot + u
            row, at = jnp.minimum(meta_ref[0, j], INSIDE), jnp.minimum(meta_ref[1, j], columns)
            slots.append((meta_ref[3, j], row, at, (j < live_slots).astype(F32)))
        grads = solve(slots, tiles, last, probe_ref, lt, rt, amp_ref, pg_ref)
        for u, (grad_re, grad_im) in enumerate(grads):
            early_ref[index * GROUP + u, 0] = grad_re
            early_ref[index * GROUP + u, 1] = grad_im
        put(index).start()

        for half in range(2):
            @pl.when(relays & (index > 0) & (2 * index + half < CHUNKS + 2))
            def _(j=2 * index + half - 2):
                to_relay(0, j).wait_recv()
                onward(route, j).start()

    def first_step(index, carry):
        solve_some(index, index * GROUP, inner, ext, 3, INSIDE)
        return carry

    lax.fori_loop(0, FIRST // GROUP, first_step, 0)
    for copy in beside:
        copy.wait()
    pl.when(rights)(made[-1][0].wait_recv)

    @pl.when(c == 15)
    def _():
        wide_ext[:, 4] = jnp.zeros((2, TILE, PATCH), F32)

    keep = pltpu.make_async_copy(wide_ext.at[:, 4], right, fetched.at[9])
    keep.start()
    base = jnp.minimum(inner, FIRST)
    upper = meta_ref[2, 2]

    def next_step(index, carry):
        solve_some(index, base + index * GROUP - FIRST, upper, wide_ext, 4, TILE - 1)
        return carry

    lax.fori_loop(FIRST // GROUP, EARLY // GROUP, next_step, 0)
    keep.wait()
    for index in range(EARLY // GROUP):
        put(index).wait()
    for copy, sends, gets in made[:-1]:
        pl.when(gets)(copy.wait_recv)
        pl.when(sends)(copy.wait_send)
    pl.when(lefts)(made[-1][0].wait_send)

    @pl.when(far_get)
    def _():
        for r in range(ROUTES):
            for j in range(CHUNKS):
                onward(r, j).wait_recv()

    @pl.when(relays)
    def _():
        for j in range(CHUNKS):
            onward(0, j).wait_send()

    @pl.when(far_send)
    def _():
        for r in range(ROUTES):
            for j in range(CHUNKS):
                to_relay(r, j).wait_send()


def halo_in(obj, meta, probe, tables, amp):
    note = jax.ShapeDtypeStruct(meta.shape, meta.dtype)
    made = pl.pallas_call(
        halo_in_kernel,
        out_shape=[
            jax.ShapeDtypeStruct((2, TILE, PATCH), F32),
            jax.ShapeDtypeStruct((2, PATCH, TILE), F32),
            jax.ShapeDtypeStruct((2, PATCH, PATCH), F32),
            note,
            note,
            note,
            jax.ShapeDtypeStruct((EARLY, 2, PATCH, PATCH), F32),
            jax.ShapeDtypeStruct((PLANES, PATCH, PATCH), F32),
        ],
        in_specs=[ANY_SPEC] * 2 + [SMEM_SPEC] + [ANY_SPEC] * 4,
        out_specs=[ANY_SPEC] * 7 + [VMEM_SPEC],
        scratch_shapes=[
            pltpu.VMEM((2, 4, TILE, PATCH), F32),
            pltpu.VMEM((2, 5, TILE, PATCH), F32),
            pltpu.VMEM(amp.shape, amp.dtype),
            pltpu.VMEM(probe.shape, F32),
            pltpu.VMEM(tables[0].shape, BF16),
            pltpu.VMEM(tables[0].shape, BF16),
            pltpu.VMEM((EARLY, 2, PATCH, PATCH), F32),
            pltpu.VMEM((CHUNKS, 2, 8, TILE), F32),
            pltpu.SemaphoreType.DMA((14,)),
            pltpu.SemaphoreType.DMA((EARLY // GROUP,)),
        ]
        + [pltpu.SemaphoreType.DMA((7,))] * 2
        + [pltpu.SemaphoreType.DMA((ROUTES * CHUNKS,)), pltpu.SemaphoreType.DMA((CHUNKS,))]
        + [pltpu.SemaphoreType.DMA((CHUNKS,)), pltpu.SemaphoreType.DMA((ROUTES * CHUNKS,))],
        compiler_params=pltpu.CompilerParams(
            collective_id=1, has_side_effects=True, vmem_limit_bytes=56 * 2**20
        ),
        name="halo_in",
    )(obj, meta, meta, probe, *tables, amp)
    return made[:6], made[6], made[7]


def patches_kernel(
    meta, meta_above, meta_left, meta_diag, probe, left_side, right_side,
    early_pg, amp, early, obj, right, lower, diag,
    pre, grad, weight, pg,
    meta_ref, above_ref, left_ref, diag_ref, probe_ref, lt_ref, rt_ref, pg_ref, amp_ref, early_ref,
    ext, grad_ref, spread, inner_ref, sems, stored,
):
    copies = []

    def fetch(source, dest):
        copy = pltpu.make_async_copy(source, dest, sems.at[len(copies)])
        copy.start()
        copies.append(copy)

    fetch(probe, probe_ref)
    fetch(meta, meta_ref)
    fetch(meta_above, above_ref)
    fetch(meta_left, left_ref)
    fetch(meta_diag, diag_ref)
    at_first = len(copies)
    fetch(early, early_ref)
    fetch(left_side, lt_ref)
    fetch(right_side, rt_ref)
    fetch(early_pg, pg_ref)
    fetch(amp, amp_ref)
    for ct in range(4):
        lanes = pl.ds(PATCH * ct, PATCH)
        fetch(obj.at[:, :, lanes], ext.at[:, ct, pl.ds(0, TILE), :])
        fetch(lower.at[:, :, lanes], ext.at[:, ct, pl.ds(TILE, PATCH), :])
    fetch(right, ext.at[:, 4, pl.ds(0, TILE), :])
    fetch(diag, ext.at[:, 4, pl.ds(TILE, PATCH), :])
    grad_ref[...] = jnp.zeros(grad_ref.shape, F32)
    spread[...] = jnp.zeros(spread.shape, F32)
    for copy in copies[:at_first]:
        copy.wait()
    w = lax.axis_index("wide")
    c = lax.axis_index("col")
    lane = lanes_of()
    count = meta_ref[2, 0]
    base = jnp.minimum(meta_ref[2, 1], FIRST)
    done = jnp.minimum(meta_ref[2, 2], base + EARLY - FIRST)
    power = jnp.sum(probe_ref[...] * probe_ref[...], axis=(0, 1))

    def scatter(ref, row, at, value):
        ct, shift = lax.shift_right_logical(at, 7), lax.bitwise_and(at, 127)
        turned = pltpu.roll(value, shift, 1)
        first = lane >= shift
        zero = jnp.zeros_like(turned)
        rows = pl.ds(row, PATCH)
        ref[ct, rows, :] += jnp.where(first, turned, zero)
        ref[ct + 1, rows, :] += jnp.where(first, zero, turned)

    for ref, there, down, side in (
        (meta_ref, None, 0, 0),
        (above_ref, w > 0, TILE, 0),
        (left_ref, c > 0, 0, TILE),
        (diag_ref, (w > 0) & (c > 0), TILE, TILE),
    ):
        live_there = ref[2, 0] if there is None else jnp.where(there, ref[2, 0], 0)

        def weigh(s, carry, ref=ref, down=down, side=side):
            row, at = ref[0, s] + (PATCH - down), ref[1, s] + (PATCH - side)
            touches = None
            if down:
                touches = row > 0
            if side:
                touches = at > 0 if touches is None else touches & (at > 0)
            if touches is None:
                scatter(spread, row, at, power)
            else:
                pl.when(touches)(lambda: scatter(spread, row, at, power))
            return carry

        lax.fori_loop(0, live_there, weigh, 0)
    weights_out = pltpu.make_async_copy(
        spread.at[pl.ds(1, 4), pl.ds(PATCH, TILE), :], weight, stored.at[0]
    )
    weights_out.start()
    copies[at_first].wait()

    def place(j, carry):
        held = jnp.where(j < base, j, j - base + FIRST)
        for p in range(2):
            scatter(grad_ref.at[p], meta_ref[0, j], meta_ref[1, j], early_ref[held, p])
        return carry

    lax.fori_loop(0, done, place, 0)
    for copy in copies[at_first + 1 :]:
        copy.wait()

    @pl.when(w == 15)
    def _():
        ext[:, :, TILE:, :] = jnp.zeros((2, 5, PATCH, PATCH), F32)

    @pl.when(c == 15)
    def _():
        ext[:, 4, :, :] = jnp.zeros((2, EXT, PATCH), F32)

    lt = lt_ref[...]
    rt = rt_ref[...]

    def step(index, carry):
        slots = []
        for u in range(PAIR):
            j = done + index * PAIR + u
            slots.append((meta_ref[3, j], meta_ref[0, j], meta_ref[1, j], (j < count).astype(F32)))
        grads = solve(slots, ext, 4, probe_ref, lt, rt, amp_ref, pg_ref)
        for (s, row, at, live), (grad_re, grad_im) in zip(slots, grads):
            scatter(grad_ref.at[0], row, at, grad_re)
            scatter(grad_ref.at[1], row, at, grad_im)
        return carry

    lax.fori_loop(0, (count - done + PAIR - 1) // PAIR, step, 0)
    outward = [weights_out]
    low, top, between = pl.ds(TILE, PATCH), pl.ds(0, PATCH), pl.ds(PATCH, REST)
    for source, dest in (
        (pg_ref, pg),
        (grad_ref.at[:, :, low, :], grad.at[:, :, low, :]),
        (grad_ref.at[:, 4, pl.ds(0, TILE), :], grad.at[:, 4, pl.ds(0, TILE), :]),
        (grad_ref.at[:, pl.ds(0, 4), top, :], grad.at[:, pl.ds(0, 4), top, :]),
        (grad_ref.at[:, 0, between, :], grad.at[:, 0, between, :]),
    ):
        copy = pltpu.make_async_copy(source, dest, stored.at[len(outward)])
        copy.start()
        outward.append(copy)
    inside = slice(PATCH, TILE)
    for ct in range(1, 4):
        scale = spread[ct + 1, PATCH + PATCH : PATCH + TILE, :] + 1.0
        lanes = slice(PATCH * (ct - 1), PATCH * ct)
        for p in range(2):
            inner_ref[p, :, lanes] = ext[p, ct, inside, :] + grad_ref[p, ct, inside, :] / scale
    copy = pltpu.make_async_copy(
        inner_ref, pre.at[:, between, between], stored.at[len(outward)]
    )
    copy.start()
    for copy in outward + [copy]:
        copy.wait()


def patches(metas, probe, tables, amp, early, early_pg, obj, right, lower, diag):
    return pl.pallas_call(
        patches_kernel,
        out_shape=[
            jax.ShapeDtypeStruct((2, TILE, TILE), F32),
            jax.ShapeDtypeStruct((2, 5, EXT, PATCH), F32),
            jax.ShapeDtypeStruct((4, TILE, PATCH), F32),
            jax.ShapeDtypeStruct((PLANES, PATCH, PATCH), F32),
        ],
        in_specs=[ANY_SPEC] * 14,
        out_specs=[ANY_SPEC] * 4,
        scratch_shapes=[pltpu.SMEM(metas[0].shape, jnp.int32)] * 4
        + [
            pltpu.VMEM(probe.shape, F32),
            pltpu.VMEM(tables[0].shape, BF16),
            pltpu.VMEM(tables[0].shape, BF16),
            pltpu.VMEM((PLANES, PATCH, PATCH), F32),
            pltpu.VMEM(amp.shape, amp.dtype),
            pltpu.VMEM(early.shape, early.dtype),
            pltpu.VMEM((2, 5, EXT, PATCH), F32),
            pltpu.VMEM((2, 5, EXT, PATCH), F32),
            pltpu.VMEM((6, EXT + PATCH, PATCH), F32),
            pltpu.VMEM((2, REST, REST), F32),
            pltpu.SemaphoreType.DMA((20,)),
            pltpu.SemaphoreType.DMA((8,)),
        ],
        compiler_params=pltpu.CompilerParams(vmem_limit_bytes=56 * 2**20),
        name="patches",
    )(*metas, probe, *tables, early_pg, amp, early, obj, right, lower, diag)


def exchange_kernel(
    pg_far, grad, total, from_above, from_left, from_diag,
    pg, loaded, buf0, red0, buf1, red1, buf2, buf3, own, res, passing,
    s0, r0, s1, r1, s2, r2, s3, r3, s4, r4, s5, r5, s6, r6, sh, rh, sent_to, got_to, sent_on, got_on,
):
    w = lax.axis_index("wide")
    c = lax.axis_index("col")
    y, k = lax.rem(w, 4), lax.div(w, 4)
    core, chip = lax.rem(c, 2), lax.div(c, 2)
    sibling = (w, 2 * chip + 1 - core)
    above, below = lax.rem(w + 15, 16), lax.rem(w + 1, 16)
    before, after = lax.rem(c + 15, 16), lax.rem(c + 1, 16)
    far_send, far_get = (y == 3) & (k < 3), (y == 0) & (k > 0)
    relays = (y < 3) & (k < 3)
    route = jnp.maximum(2 - y, 0)
    onward_to = lax.rem(w + 4 - y, 16)

    def rows(index, half):
        return pl.ds(pl.multiple_of(index * ROWS + half * (PATCH // 2), ROWS), ROWS)

    def planes(index):
        return pl.ds(index * 3, 3)

    chips = [(w, lax.rem(chip + d, 8) * 2 + core) for d in range(1, 8)]
    along_y = [(k * 4 + lax.rem(y + d, 4), c) for d in range(1, 4)]
    along_z = [(lax.rem(w + 4 * d, 16), c) for d in range(1, 4)]
    barrier = pltpu.get_barrier_semaphore()
    for target in [sibling] + chips + along_y + along_z:
        greet(barrier, target)
    for target in ((w, before), (above, c), (above, before)):
        greet(barrier, target)

    @pl.when(far_get)
    def _():
        for r in range(ROUTES):
            greet(barrier, (lax.rem(w + 12 + r, 16), c))

    load = pltpu.make_async_copy(pg_far, pg, loaded)
    load.start()
    load.wait()
    pl.semaphore_wait(barrier, 17 + jnp.where(relays, 1, 0))

    zeroth = []
    for d in range(1, 9):
        p = lax.rem(chip + d, 8)
        copy = remote(pg.at[:, rows(p, 1 - core), :], buf0.at[d - 1], s0.at[d - 1], r0.at[d - 1], sibling)
        copy.start()
        zeroth.append(copy)

    def to_relay(r, j):
        at = TILE + DIRECT + 8 * (r * CHUNKS + j)
        return remote(
            grad.at[:, pl.ds(0, 4), pl.ds(at, 8), :], passing.at[j],
            sent_to.at[r * CHUNKS + j], got_to.at[j], (lax.rem(w + 15 - r, 16), c),
        )

    def onward(r, j):
        at = pl.multiple_of(DIRECT + 8 * (r * CHUNKS + j), 8)
        return remote(
            passing.at[j], from_above.at[:, :, pl.ds(at, 8), :],
            sent_on.at[j], got_on.at[r * CHUNKS + j], (onward_to, c),
        )

    def pass_on(chunks):
        @pl.when(relays)
        def _():
            for j in chunks:
                to_relay(0, j).wait_recv()
                onward(route, j).start()

    ups, downs = w > 0, w < 15
    lefts, rights = c > 0, c < 15
    near_send = downs & jnp.logical_not(far_send)
    near_get = ups & jnp.logical_not(far_get)
    strips = []

    def post(source, dest, target, sends, gets):
        copy = remote(source, dest, sh.at[len(strips)], rh.at[len(strips)], target)
        pl.when(sends)(copy.start)
        strips.append((copy, sends, gets))

    def post_rows(first, size, sends, gets):
        post(
            grad.at[:, pl.ds(0, 4), pl.ds(TILE + first, size), :],
            from_above.at[:, :, pl.ds(first, size), :], (below, c), sends, gets,
        )

    def post_columns(first, size):
        at = pl.ds(first, size)
        post(grad.at[:, 4, at, :], from_left.at[:, at, :], (w, after), rights, lefts)

    @pl.when(far_send)
    def _():
        for j in range(CHUNKS):
            for r in reversed(range(ROUTES)):
                to_relay(r, j).start()

    post_rows(DIRECT, 40, near_send, near_get)
    first = []
    for d in range(1, 8):
        p = lax.rem(chip + d, 8)
        zeroth[d - 1].wait_recv()
        red0[d - 1] = pg[:, rows(p, core), :] + buf0[d - 1]
        copy = remote(red0.at[d - 1], buf1.at[d], s1.at[d], r1.at[d], chips[d - 1])
        copy.start()
        first.append(copy)
    zeroth[7].wait_recv()
    acc = pg[:, rows(chip, core), :] + buf0[7]

    post_rows(DIRECT + 40, 40, near_send, near_get)
    post(
        grad.at[:, 4, pl.ds(TILE, PATCH), :], from_diag, (below, after),
        downs & rights, ups & lefts,
    )
    pass_on(range(2))
    for d in range(1, 8):
        first[d - 1].wait_recv()
        acc = acc + buf1[d]
    red1[pl.ds(0, PLANES)] = acc
    red1[pl.ds(PLANES, 3)] = jnp.zeros((3, ROWS, PATCH), F32)
    second = []
    for d in range(1, 4):
        copy = remote(
            red1.at[planes(lax.rem(y + d, 4))], buf2.at[d], s2.at[d], r2.at[d], along_y[d - 1]
        )
        copy.start()
        second.append(copy)
    pass_on(range(2, CHUNKS))
    post_rows(0, DIRECT, downs, ups)
    post_rows(DIRECT + 80, 40, near_send, near_get)
    post_columns(0, 256)
    acc = red1[planes(y)]
    for d in range(1, 4):
        second[d - 1].wait_recv()
        acc = acc + buf2[d]
    buf3[k] = acc
    third = []
    for d in range(1, 4):
        copy = remote(buf3.at[k], buf3.at[k], s3.at[d], r3.at[d], along_z[d - 1])
        copy.start()
        third.append(copy)
    post_columns(256, 256)
    for d in range(1, 4):
        p = lax.rem(k + 4 - d, 4)
        remote(buf3.at[p], buf3.at[p], s3.at[d], r3.at[d], along_z[d - 1]).wait_recv()
    own[planes(y)] = buf3[0] + buf3[1] + buf3[2] + buf3[3]
    fourth = []
    for d in range(1, 4):
        copy = remote(own.at[planes(y)], own.at[planes(y)], s4.at[d], r4.at[d], along_y[d - 1])
        copy.start()
        fourth.append(copy)
    for d in range(1, 4):
        p = planes(lax.rem(y + 4 - d, 4))
        remote(own.at[p], own.at[p], s4.at[d], r4.at[d], along_y[d - 1]).wait_recv()
    lit = own[2 * MODES]
    res[...] = own[pl.ds(0, 2 * MODES)] / jnp.sqrt(lit + 1.0)[None]

    mine = rows(chip, core)
    fifth, sixth = [], []
    for d in range(1, 8):
        copy = remote(res, total.at[:, mine, :], s5.at[d], r5.at[d], chips[d - 1])
        copy.start()
        fifth.append(copy)
    copy = remote(res, total.at[:, mine, :], s6.at[0], r6.at[0], sibling)
    copy.start()
    sixth.append(copy)
    total[:, mine, :] = res[...]
    for d in range(1, 8):
        at = rows(lax.rem(chip + 8 - d, 8), core)
        remote(res, total.at[:, at, :], s5.at[d], r5.at[d], chips[d - 1]).wait_recv()
        copy = remote(total.at[:, at, :], total.at[:, at, :], s6.at[d], r6.at[d], sibling)
        copy.start()
        sixth.append(copy)
    for copy in zeroth + first + second + third + fourth + fifth:
        copy.wait_send()
    for d in range(8):
        at = rows(lax.rem(chip + 8 - d, 8), 1 - core)
        remote(res, total.at[:, at, :], s6.at[d], r6.at[d], sibling).wait_recv()
    for copy in sixth:
        copy.wait_send()
    for copy, sends, gets in strips:
        pl.when(gets)(copy.wait_recv)
        pl.when(sends)(copy.wait_send)

    @pl.when(far_get)
    def _():
        for r in range(ROUTES):
            for j in range(CHUNKS):
                onward(r, j).wait_recv()

    @pl.when(relays)
    def _():
        for j in range(CHUNKS):
            onward(0, j).wait_send()

    @pl.when(far_send)
    def _():
        for r in range(ROUTES):
            for j in range(CHUNKS):
                to_relay(r, j).wait_send()


def exchange(pg, grad):
    eight = pltpu.SemaphoreType.DMA((8,))
    four = pltpu.SemaphoreType.DMA((4,))
    many = pltpu.SemaphoreType.DMA((ROUTES * CHUNKS,))
    few = pltpu.SemaphoreType.DMA((CHUNKS,))
    return pl.pallas_call(
        exchange_kernel,
        out_shape=[
            jax.ShapeDtypeStruct((2 * MODES, PATCH, PATCH), F32),
            jax.ShapeDtypeStruct((2, 4, PATCH, PATCH), F32),
            jax.ShapeDtypeStruct((2, TILE, PATCH), F32),
            jax.ShapeDtypeStruct((2, PATCH, PATCH), F32),
        ],
        in_specs=[ANY_SPEC] * 2,
        out_specs=[VMEM_SPEC] + [ANY_SPEC] * 3,
        scratch_shapes=[
            pltpu.VMEM((PLANES, PATCH, PATCH), F32),
            pltpu.SemaphoreType.DMA,
            pltpu.VMEM((8, PLANES, ROWS, PATCH), F32),
            pltpu.VMEM((8, PLANES, ROWS, PATCH), F32),
            pltpu.VMEM((8, PLANES, ROWS, PATCH), F32),
            pltpu.VMEM((12, ROWS, PATCH), F32),
            pltpu.VMEM((4, 3, ROWS, PATCH), F32),
            pltpu.VMEM((4, 3, ROWS, PATCH), F32),
            pltpu.VMEM((12, ROWS, PATCH), F32),
            pltpu.VMEM((2 * MODES, ROWS, PATCH), F32),
            pltpu.VMEM((CHUNKS, 2, 4, 8, PATCH), F32),
        ]
        + [eight] * 4
        + [four] * 6
        + [eight] * 4
        + [eight] * 2
        + [many, few, few, many],
        compiler_params=pltpu.CompilerParams(
            collective_id=2, has_side_effects=True, vmem_limit_bytes=56 * 2**20
        ),
        name="exchange",
    )(pg, grad)


def finish_kernel(
    pre, obj, grad, weight, total, from_above, from_left, from_diag, new, direction,
    obj_top, obj_left, grad_top, grad_left, weight_top, weight_left, above, left, corner,
    new_top, new_left, held, sems, stored,
):
    del pre
    top, between, tiles = pl.ds(0, PATCH), pl.ds(PATCH, REST), pl.ds(0, 4)
    copies = []
    for source, dest in (
        (obj.at[:, between, top], obj_left),
        (grad.at[:, 0, between, :], grad_left),
        (weight.at[0, between, :], weight_left),
        (from_left, left),
        (total, held),
        (obj.at[:, top, :], obj_top),
        (grad.at[:, tiles, top, :], grad_top),
        (weight.at[:, top, :], weight_top),
        (from_above, above),
        (from_diag, corner),
    ):
        copy = pltpu.make_async_copy(source, dest, sems.at[len(copies)])
        copy.start()
        copies.append(copy)
    got_above, got_left = lax.axis_index("wide") > 0, lax.axis_index("col") > 0
    for copy in copies[:4]:
        copy.wait()
    scale = weight_left[...] + 1.0
    for p in range(2):
        sums = grad_left[p] + jnp.where(got_left, left[p, PATCH:], 0.0)
        new_left[p] = obj_left[p] + sums / scale
    left_out = pltpu.make_async_copy(new_left, new.at[:, between, top], stored.at[1])
    left_out.start()
    copies[4].wait()
    whole = pltpu.make_async_copy(held, direction, stored.at[0])
    whole.start()
    for copy in copies[5:]:
        copy.wait()
    for ct in range(4):
        lanes = slice(PATCH * ct, PATCH * (ct + 1))
        scale = weight_top[ct] + 1.0
        for p in range(2):
            sums = grad_top[p, ct] + jnp.where(got_above, above[p, ct], 0.0)
            if ct == 0:
                sums = sums + jnp.where(got_left, left[p, :PATCH], 0.0)
                sums = sums + jnp.where(got_above & got_left, corner[p], 0.0)
            new_top[p, :, lanes] = obj_top[p, :, lanes] + sums / scale
    top_out = pltpu.make_async_copy(new_top, new.at[:, top, :], stored.at[2])
    top_out.start()
    for copy in (whole, left_out, top_out):
        copy.wait()


def finish(pre, obj, grad, weight, total, from_above, from_left, from_diag):
    return pl.pallas_call(
        finish_kernel,
        out_shape=[
            jax.ShapeDtypeStruct((2, TILE, TILE), F32),
            jax.ShapeDtypeStruct((2 * MODES, PATCH, PATCH), F32),
        ],
        in_specs=[ANY_SPEC] * 8,
        out_specs=[ANY_SPEC] * 2,
        input_output_aliases={0: 0},
        scratch_shapes=[
            pltpu.VMEM((2, PATCH, TILE), F32),
            pltpu.VMEM((2, REST, PATCH), F32),
            pltpu.VMEM((2, 4, PATCH, PATCH), F32),
            pltpu.VMEM((2, REST, PATCH), F32),
            pltpu.VMEM((4, PATCH, PATCH), F32),
            pltpu.VMEM((REST, PATCH), F32),
            pltpu.VMEM((2, 4, PATCH, PATCH), F32),
            pltpu.VMEM((2, TILE, PATCH), F32),
            pltpu.VMEM((2, PATCH, PATCH), F32),
            pltpu.VMEM((2, PATCH, TILE), F32),
            pltpu.VMEM((2, REST, PATCH), F32),
            pltpu.VMEM((2 * MODES, PATCH, PATCH), F32),
            pltpu.SemaphoreType.DMA((10,)),
            pltpu.SemaphoreType.DMA((3,)),
        ],
        compiler_params=pltpu.CompilerParams(vmem_limit_bytes=56 * 2**20),
        name="finish",
    )(pre, obj, grad, weight, total, from_above, from_left, from_diag)


def local(object_field, probe_modes, amplitude, positions, slot_counts):
    slots = positions.shape[2]
    amp = amplitude.reshape(slots, PATCH, PATCH)
    table = left_table()
    tables = (jnp.asarray(table), jnp.asarray(table.T))
    meta = plan(positions.reshape(slots, 2).T, slot_counts)
    (right, lower, diag, *others), early, early_pg = halo_in(
        object_field, meta, probe_modes, tables, amp
    )
    pre, grad, weight, pg = patches(
        (meta, *others), probe_modes, tables, amp, early, early_pg,
        object_field, right, lower, diag,
    )
    total, from_above, from_left, from_diag = exchange(pg, grad)
    new_object, direction = finish(
        pre, object_field, grad, weight, total, from_above, from_left, from_diag
    )
    return new_object, direction.reshape(probe_modes.shape)


def solution(mesh):
    placed = (
        P(None, "wide", "col"),
        P(),
        P("wide", "col", None, None, None),
        P("wide", "col", None, None),
        P("wide", "col"),
    )
    return jax.shard_map(
        local, mesh=mesh, in_specs=placed, out_specs=(P(None, "wide", "col"), P()), check_vma=False
    )
```

```python
import functools
import math

import jax
import jax.numpy as jnp
import ml_dtypes
import numpy as np
from jax import lax
from jax.experimental import pallas as pl
from jax.experimental.pallas import tpu as pltpu
from jax.sharding import PartitionSpec as P

MESH = pl.DeviceIdType.MESH
F32 = jnp.float32
BF16 = jnp.bfloat16
PATCH = 128
TILE = 512
EXT = TILE + PATCH
MODES = 4
RING = 16
PLANES = 2 * MODES + 1
ROWS = PATCH // RING
PAIR = 2
CHUNKS = 5
ROUTES = 3
DIRECT = PATCH - ROUTES * 8 * CHUNKS
GROUP = 4
FIRST = 16
EARLY = 24
REST = TILE - PATCH
INSIDE = TILE - PATCH

VMEM_SPEC = pl.BlockSpec(memory_space=pltpu.VMEM)
SMEM_SPEC = pl.BlockSpec(memory_space=pltpu.SMEM)
ANY_SPEC = pl.BlockSpec(memory_space=pl.ANY)


def left_table():
    indices = np.arange(PATCH)
    angles = (indices[:, None] * indices[None, :] % PATCH) * (2.0 * math.pi / PATCH)
    cosine = np.cos(angles) / math.sqrt(PATCH)
    sine = -np.sin(angles) / math.sqrt(PATCH)
    whole = np.block([[cosine, -sine], [sine, cosine]])
    return whole.astype(np.float32).astype(ml_dtypes.bfloat16)


def plan_kernel(pos_ref, count_ref, meta_ref):
    count = count_ref[0, 0]
    slots = []
    inner_count, upper_count = jnp.int32(0), jnp.int32(0)
    for s in range(pos_ref.shape[1]):
        row, at = pos_ref[0, s], pos_ref[1, s]
        live = s < count
        upper = live & (row <= INSIDE)
        inner = upper & (at <= INSIDE)
        slots.append((row, at, live, upper, inner))
        inner_count = inner_count + jnp.where(inner, 1, 0)
        upper_count = upper_count + jnp.where(upper, 1, 0)
    low, middle, high = jnp.int32(0), inner_count, upper_count
    for s, (row, at, live, upper, inner) in enumerate(slots):
        outer = upper & jnp.logical_not(inner)
        place = jnp.where(inner, low, jnp.where(outer, middle, jnp.where(live, high, s)))
        meta_ref[0, place] = row
        meta_ref[1, place] = at
        meta_ref[3, place] = s
        low = low + jnp.where(inner, 1, 0)
        middle = middle + jnp.where(outer, 1, 0)
        high = high + jnp.where(live & jnp.logical_not(upper), 1, 0)
    for line in (0, 1, 3):
        for past in range(pos_ref.shape[1], pos_ref.shape[1] + EARLY):
            meta_ref[line, past] = 0
    meta_ref[2, 0] = count
    meta_ref[2, 1] = inner_count
    meta_ref[2, 2] = upper_count


def plan(positions, slot_counts):
    return pl.pallas_call(
        plan_kernel,
        out_shape=jax.ShapeDtypeStruct((8, PATCH), jnp.int32),
        in_specs=[SMEM_SPEC] * 2,
        out_specs=SMEM_SPEC,
        name="plan",
    )(positions, slot_counts)


def lanes_of():
    return lax.broadcasted_iota(jnp.int32, (PATCH, PATCH), 1)


def both_sides(left, stacked, right_side):
    half = jnp.dot(left, stacked, preferred_element_type=F32).astype(BF16)
    lanes = [slice(PATCH * m, PATCH * (m + 1)) for m in range(MODES)]
    turned = jnp.concatenate(
        [jnp.concatenate([half[:PATCH, at], half[PATCH:, at]], 1) for at in lanes], 0
    )
    return jnp.dot(turned, right_side, preferred_element_type=F32)


def stack(re, im):
    return jnp.concatenate([jnp.concatenate(re, 1), jnp.concatenate(im, 1)], 0)


def parts(values, m):
    rows = slice(PATCH * m, PATCH * (m + 1))
    return values[rows, :PATCH], values[rows, PATCH:]


def solve(slots, ext, last, probe_ref, lt, rt, amp_ref, pg_ref):
    lane = lanes_of()
    patches_of, waves = [], []
    for s, row, at, live in slots:
        ct, shift = lax.shift_right_logical(at, 7), lax.bitwise_and(at, 127)
        back = lax.bitwise_and(PATCH - shift, 127)
        beside = jnp.minimum(ct + 1, last)
        rows = pl.ds(row, PATCH)
        patch = []
        for p in range(2):
            joined = jnp.where(lane >= shift, ext[p, ct, rows, :], ext[p, beside, rows, :])
            patch.append(pltpu.roll(joined, back, 1))
        patches_of.append(patch)
        re, im = [], []
        for m in range(MODES):
            pr, pi = probe_ref[0, m], probe_ref[1, m]
            re.append((pr * patch[0] - pi * patch[1]).astype(BF16))
            im.append((pr * patch[1] + pi * patch[0]).astype(BF16))
        waves.append(stack(re, im))
    fars = [both_sides(lt, wave, rt) for wave in waves]
    residuals = []
    for (s, row, at, live), far in zip(slots, fars):
        intensity = jnp.zeros((PATCH, PATCH), F32)
        for m in range(MODES):
            fr, fi = parts(far, m)
            intensity = intensity + fr * fr + fi * fi
        measured = amp_ref[s].astype(F32)
        factor = (measured * lax.rsqrt(jnp.maximum(intensity, 1.0)) - 1.0) * live
        re, im = [], []
        for m in range(MODES):
            fr, fi = parts(far, m)
            re.append((fr * factor).astype(BF16))
            im.append((fi * factor).astype(BF16))
        residuals.append(stack(re, im))
    updates = [both_sides(rt, residual, lt) for residual in residuals]
    for m in range(MODES):
        sum_re, sum_im = pg_ref[m], pg_ref[MODES + m]
        for patch, update in zip(patches_of, updates):
            ur, ui = parts(update, m)
            sum_re = sum_re + patch[0] * ur + patch[1] * ui
            sum_im = sum_im + patch[0] * ui - patch[1] * ur
        pg_ref[m] = sum_re
        pg_ref[MODES + m] = sum_im
    lit = pg_ref[2 * MODES]
    for (s, row, at, live), patch in zip(slots, patches_of):
        lit = lit + live * (patch[0] * patch[0] + patch[1] * patch[1])
    pg_ref[2 * MODES] = lit
    grads = []
    for update in updates:
        grad_re = jnp.zeros((PATCH, PATCH), F32)
        grad_im = grad_re
        for m in range(MODES):
            pr, pi = probe_ref[0, m], probe_ref[1, m]
            ur, ui = parts(update, m)
            grad_re = grad_re + pr * ur + pi * ui
            grad_im = grad_im + pr * ui - pi * ur
        grads.append((grad_re, grad_im))
    return grads


def remote(source, dest, sent, got, target):
    return pltpu.make_async_remote_copy(
        source, dest, sent, got, device_id=target, device_id_type=MESH
    )


def greet(barrier, target):
    pl.semaphore_signal(barrier, inc=1, device_id=target, device_id_type=MESH)


def halo_in_kernel(
    obj, meta, meta_ref, probe, left_side, right_side, amp,
    right, lower, diag, meta_above, meta_left, meta_diag, early, pg_ref,
    ext, wide_ext, amp_ref, probe_ref, lt_ref, rt_ref, early_ref, passing, fetched, stored,
    sent, got, sent_to, got_to, sent_on, got_on,
):
    w = lax.axis_index("wide")
    c = lax.axis_index("col")
    y, k = lax.rem(w, 4), lax.div(w, 4)
    above, below = lax.rem(w + 15, 16), lax.rem(w + 1, 16)
    before, after = lax.rem(c + 15, 16), lax.rem(c + 1, 16)
    far_send, far_get = (y == 0) & (k > 0), (y == 3) & (k < 3)
    relays = (y > 0) & (k > 0)
    route = jnp.maximum(y - 1, 0)
    onward_to = lax.rem(w + 15 - y, 16)
    barrier = pltpu.get_barrier_semaphore()
    for target in (
        (w, after), (below, c), (below, after), (w, before), (above, c), (above, before)
    ):
        greet(barrier, target)
    pl.when(relays & (y > 1))(lambda: greet(barrier, (lax.rem(w + 16 - y, 16), c)))

    @pl.when(far_get)
    def _():
        for r in range(ROUTES):
            greet(barrier, (lax.rem(w + 2 + r, 16), c))

    inward = [
        pltpu.make_async_copy(source, dest, fetched.at[10 + j])
        for j, (source, dest) in enumerate(
            ((amp, amp_ref), (probe, probe_ref), (left_side, lt_ref), (right_side, rt_ref))
        )
    ]
    for ct in range(4):
        inward.append(pltpu.make_async_copy(
            obj.at[:, :, pl.ds(PATCH * ct, PATCH)], ext.at[:, ct], fetched.at[ct]
        ))
    beside = [
        pltpu.make_async_copy(
            obj.at[:, :, pl.ds(PATCH * ct, PATCH)], wide_ext.at[:, ct], fetched.at[5 + ct]
        )
        for ct in range(4)
    ]
    for copy in inward + beside:
        copy.start()
    pl.semaphore_wait(barrier, 6 + jnp.where(far_send, 2, jnp.where(relays, 1, 0)))

    def strip(first, rows):
        return pl.ds(first, rows)

    def to_relay(r, j):
        at = strip(DIRECT + 8 * (r * CHUNKS + j), 8)
        return remote(
            obj.at[:, at, :], passing.at[j], sent_to.at[r * CHUNKS + j], got_to.at[j],
            (lax.rem(w + r + 1, 16), c),
        )

    def onward(r, j):
        start = pl.multiple_of(DIRECT + 8 * (r * CHUNKS + j), 8)
        return remote(
            passing.at[j], lower.at[:, strip(start, 8), :],
            sent_on.at[j], got_on.at[r * CHUNKS + j], (onward_to, c),
        )

    @pl.when(far_send)
    def _():
        for j in range(CHUNKS):
            for r in reversed(range(ROUTES)):
                to_relay(r, j).start()

    ups, downs = w > 0, w < 15
    lefts, rights = c > 0, c < 15
    near_send = ups & jnp.logical_not(far_send)
    near_get = downs & jnp.logical_not(far_get)
    top = pl.ds(0, PATCH)
    some, rest = strip(0, DIRECT), strip(DIRECT, PATCH - DIRECT)
    plain = (
        (meta, meta_above, (below, c), downs, ups),
        (meta, meta_left, (w, after), rights, lefts),
        (meta, meta_diag, (below, after), downs & rights, ups & lefts),
        (obj.at[:, some, :], lower.at[:, some, :], (above, c), ups, downs),
        (obj.at[:, rest, :], lower.at[:, rest, :], (above, c), near_send, near_get),
        (obj.at[:, top, top], diag, (above, before), ups & lefts, downs & rights),
        (obj.at[:, :, top], wide_ext.at[:, 4], (w, before), lefts, rights),
    )
    made = []
    for j, (source, dest, target, sends, gets) in enumerate(plain):
        copy = remote(source, dest, sent.at[j], got.at[j], target)
        pl.when(sends)(copy.start)
        made.append((copy, sends, gets))

    pg_ref[...] = jnp.zeros(pg_ref.shape, F32)
    inner = meta_ref[2, 1]
    for copy in inward:
        copy.wait()
    lt = lt_ref[...]
    rt = rt_ref[...]

    def put(index):
        pair = pl.ds(index * GROUP, GROUP)
        return pltpu.make_async_copy(early_ref.at[pair], early.at[pair], stored.at[index])

    def solve_some(index, first_slot, live_slots, tiles, last, columns):
        slots = []
        for u in range(GROUP):
            j = first_slot + u
            row, at = jnp.minimum(meta_ref[0, j], INSIDE), jnp.minimum(meta_ref[1, j], columns)
            slots.append((meta_ref[3, j], row, at, (j < live_slots).astype(F32)))
        grads = solve(slots, tiles, last, probe_ref, lt, rt, amp_ref, pg_ref)
        for u, (grad_re, grad_im) in enumerate(grads):
            early_ref[index * GROUP + u, 0] = grad_re
            early_ref[index * GROUP + u, 1] = grad_im
        put(index).start()

        for half in range(2):
            @pl.when(relays & (index > 0) & (2 * index + half < CHUNKS + 2))
            def _(j=2 * index + half - 2):
                to_relay(0, j).wait_recv()
                onward(route, j).start()

    def first_step(index, carry):
        solve_some(index, index * GROUP, inner, ext, 3, INSIDE)
        return carry

    lax.fori_loop(0, FIRST // GROUP, first_step, 0)
    for copy in beside:
        copy.wait()
    pl.when(rights)(made[-1][0].wait_recv)

    @pl.when(c == 15)
    def _():
        wide_ext[:, 4] = jnp.zeros((2, TILE, PATCH), F32)

    keep = pltpu.make_async_copy(wide_ext.at[:, 4], right, fetched.at[9])
    keep.start()
    base = jnp.minimum(inner, FIRST)
    upper = meta_ref[2, 2]

    def next_step(index, carry):
        solve_some(index, base + index * GROUP - FIRST, upper, wide_ext, 4, TILE - 1)
        return carry

    lax.fori_loop(FIRST // GROUP, EARLY // GROUP, next_step, 0)
    keep.wait()
    for index in range(EARLY // GROUP):
        put(index).wait()
    for copy, sends, gets in made[:-1]:
        pl.when(gets)(copy.wait_recv)
        pl.when(sends)(copy.wait_send)
    pl.when(lefts)(made[-1][0].wait_send)

    @pl.when(far_get)
    def _():
        for r in range(ROUTES):
            for j in range(CHUNKS):
                onward(r, j).wait_recv()

    @pl.when(relays)
    def _():
        for j in range(CHUNKS):
            onward(0, j).wait_send()

    @pl.when(far_send)
    def _():
        for r in range(ROUTES):
            for j in range(CHUNKS):
                to_relay(r, j).wait_send()


def halo_in(obj, meta, probe, tables, amp):
    note = jax.ShapeDtypeStruct(meta.shape, meta.dtype)
    made = pl.pallas_call(
        halo_in_kernel,
        out_shape=[
            jax.ShapeDtypeStruct((2, TILE, PATCH), F32),
            jax.ShapeDtypeStruct((2, PATCH, TILE), F32),
            jax.ShapeDtypeStruct((2, PATCH, PATCH), F32),
            note,
            note,
            note,
            jax.ShapeDtypeStruct((EARLY, 2, PATCH, PATCH), F32),
            jax.ShapeDtypeStruct((PLANES, PATCH, PATCH), F32),
        ],
        in_specs=[ANY_SPEC] * 2 + [SMEM_SPEC] + [ANY_SPEC] * 4,
        out_specs=[ANY_SPEC] * 7 + [VMEM_SPEC],
        scratch_shapes=[
            pltpu.VMEM((2, 4, TILE, PATCH), F32),
            pltpu.VMEM((2, 5, TILE, PATCH), F32),
            pltpu.VMEM(amp.shape, amp.dtype),
            pltpu.VMEM(probe.shape, F32),
            pltpu.VMEM(tables[0].shape, BF16),
            pltpu.VMEM(tables[0].shape, BF16),
            pltpu.VMEM((EARLY, 2, PATCH, PATCH), F32),
            pltpu.VMEM((CHUNKS, 2, 8, TILE), F32),
            pltpu.SemaphoreType.DMA((14,)),
            pltpu.SemaphoreType.DMA((EARLY // GROUP,)),
        ]
        + [pltpu.SemaphoreType.DMA((7,))] * 2
        + [pltpu.SemaphoreType.DMA((ROUTES * CHUNKS,)), pltpu.SemaphoreType.DMA((CHUNKS,))]
        + [pltpu.SemaphoreType.DMA((CHUNKS,)), pltpu.SemaphoreType.DMA((ROUTES * CHUNKS,))],
        compiler_params=pltpu.CompilerParams(
            collective_id=1, has_side_effects=True, vmem_limit_bytes=56 * 2**20
        ),
        name="halo_in",
    )(obj, meta, meta, probe, *tables, amp)
    return made[:6], made[6], made[7]


def patches_kernel(
    meta, meta_above, meta_left, meta_diag, probe, left_side, right_side,
    early_pg, amp, early, obj, right, lower, diag,
    pre, grad, weight, pg,
    meta_ref, above_ref, left_ref, diag_ref, probe_ref, lt_ref, rt_ref, pg_ref, amp_ref, early_ref,
    ext, grad_ref, spread, inner_ref, sems, stored,
):
    copies = []

    def fetch(source, dest):
        copy = pltpu.make_async_copy(source, dest, sems.at[len(copies)])
        copy.start()
        copies.append(copy)

    fetch(probe, probe_ref)
    fetch(meta, meta_ref)
    fetch(meta_above, above_ref)
    fetch(meta_left, left_ref)
    fetch(meta_diag, diag_ref)
    at_first = len(copies)
    fetch(early, early_ref)
    fetch(left_side, lt_ref)
    fetch(right_side, rt_ref)
    fetch(early_pg, pg_ref)
    fetch(amp, amp_ref)
    for ct in range(4):
        lanes = pl.ds(PATCH * ct, PATCH)
        fetch(obj.at[:, :, lanes], ext.at[:, ct, pl.ds(0, TILE), :])
        fetch(lower.at[:, :, lanes], ext.at[:, ct, pl.ds(TILE, PATCH), :])
    fetch(right, ext.at[:, 4, pl.ds(0, TILE), :])
    fetch(diag, ext.at[:, 4, pl.ds(TILE, PATCH), :])
    grad_ref[...] = jnp.zeros(grad_ref.shape, F32)
    spread[...] = jnp.zeros(spread.shape, F32)
    for copy in copies[:at_first]:
        copy.wait()
    w = lax.axis_index("wide")
    c = lax.axis_index("col")
    lane = lanes_of()
    count = meta_ref[2, 0]
    base = jnp.minimum(meta_ref[2, 1], FIRST)
    done = jnp.minimum(meta_ref[2, 2], base + EARLY - FIRST)
    power = jnp.sum(probe_ref[...] * probe_ref[...], axis=(0, 1))

    def scatter(ref, row, at, value):
        ct, shift = lax.shift_right_logical(at, 7), lax.bitwise_and(at, 127)
        turned = pltpu.roll(value, shift, 1)
        first = lane >= shift
        zero = jnp.zeros_like(turned)
        rows = pl.ds(row, PATCH)
        ref[ct, rows, :] += jnp.where(first, turned, zero)
        ref[ct + 1, rows, :] += jnp.where(first, zero, turned)

    for ref, there, down, side in (
        (meta_ref, None, 0, 0),
        (above_ref, w > 0, TILE, 0),
        (left_ref, c > 0, 0, TILE),
        (diag_ref, (w > 0) & (c > 0), TILE, TILE),
    ):
        live_there = ref[2, 0] if there is None else jnp.where(there, ref[2, 0], 0)

        def weigh(s, carry, ref=ref, down=down, side=side):
            row, at = ref[0, s] + (PATCH - down), ref[1, s] + (PATCH - side)
            touches = None
            if down:
                touches = row > 0
            if side:
                touches = at > 0 if touches is None else touches & (at > 0)
            if touches is None:
                scatter(spread, row, at, power)
            else:
                pl.when(touches)(lambda: scatter(spread, row, at, power))
            return carry

        lax.fori_loop(0, live_there, weigh, 0)
    weights_out = pltpu.make_async_copy(
        spread.at[pl.ds(1, 4), pl.ds(PATCH, TILE), :], weight, stored.at[0]
    )
    weights_out.start()
    copies[at_first].wait()

    def place(j, carry):
        held = jnp.where(j < base, j, j - base + FIRST)
        for p in range(2):
            scatter(grad_ref.at[p], meta_ref[0, j], meta_ref[1, j], early_ref[held, p])
        return carry

    lax.fori_loop(0, done, place, 0)
    for copy in copies[at_first + 1 :]:
        copy.wait()

    @pl.when(w == 15)
    def _():
        ext[:, :, TILE:, :] = jnp.zeros((2, 5, PATCH, PATCH), F32)

    @pl.when(c == 15)
    def _():
        ext[:, 4, :, :] = jnp.zeros((2, EXT, PATCH), F32)

    lt = lt_ref[...]
    rt = rt_ref[...]

    def steps(first_slot, size, number):
        def step(index, carry):
            slots = []
            for u in range(size):
                j = first_slot + index * size + u
                live = (j < count).astype(F32)
                slots.append((meta_ref[3, j], meta_ref[0, j], meta_ref[1, j], live))
            grads = solve(slots, ext, 4, probe_ref, lt, rt, amp_ref, pg_ref)
            for (s, row, at, live), (grad_re, grad_im) in zip(slots, grads):
                scatter(grad_ref.at[0], row, at, grad_re)
                scatter(grad_ref.at[1], row, at, grad_im)
            return carry

        lax.fori_loop(0, number, step, 0)

    whole = (count - done) // GROUP
    left_over = done + whole * GROUP
    steps(done, GROUP, whole)
    steps(left_over, PAIR, (count - left_over + PAIR - 1) // PAIR)
    outward = [weights_out]
    low, top, between = pl.ds(TILE, PATCH), pl.ds(0, PATCH), pl.ds(PATCH, REST)
    for source, dest in (
        (pg_ref, pg),
        (grad_ref.at[:, :, low, :], grad.at[:, :, low, :]),
        (grad_ref.at[:, 4, pl.ds(0, TILE), :], grad.at[:, 4, pl.ds(0, TILE), :]),
        (grad_ref.at[:, pl.ds(0, 4), top, :], grad.at[:, pl.ds(0, 4), top, :]),
        (grad_ref.at[:, 0, between, :], grad.at[:, 0, between, :]),
    ):
        copy = pltpu.make_async_copy(source, dest, stored.at[len(outward)])
        copy.start()
        outward.append(copy)
    inside = slice(PATCH, TILE)
    for ct in range(1, 4):
        scale = spread[ct + 1, PATCH + PATCH : PATCH + TILE, :] + 1.0
        lanes = slice(PATCH * (ct - 1), PATCH * ct)
        for p in range(2):
            inner_ref[p, :, lanes] = ext[p, ct, inside, :] + grad_ref[p, ct, inside, :] / scale
    copy = pltpu.make_async_copy(
        inner_ref, pre.at[:, between, between], stored.at[len(outward)]
    )
    copy.start()
    for copy in outward + [copy]:
        copy.wait()


def patches(metas, probe, tables, amp, early, early_pg, obj, right, lower, diag):
    return pl.pallas_call(
        patches_kernel,
        out_shape=[
            jax.ShapeDtypeStruct((2, TILE, TILE), F32),
            jax.ShapeDtypeStruct((2, 5, EXT, PATCH), F32),
            jax.ShapeDtypeStruct((4, TILE, PATCH), F32),
            jax.ShapeDtypeStruct((PLANES, PATCH, PATCH), F32),
        ],
        in_specs=[ANY_SPEC] * 14,
        out_specs=[ANY_SPEC] * 4,
        scratch_shapes=[pltpu.SMEM(metas[0].shape, jnp.int32)] * 4
        + [
            pltpu.VMEM(probe.shape, F32),
            pltpu.VMEM(tables[0].shape, BF16),
            pltpu.VMEM(tables[0].shape, BF16),
            pltpu.VMEM((PLANES, PATCH, PATCH), F32),
            pltpu.VMEM(amp.shape, amp.dtype),
            pltpu.VMEM(early.shape, early.dtype),
            pltpu.VMEM((2, 5, EXT, PATCH), F32),
            pltpu.VMEM((2, 5, EXT, PATCH), F32),
            pltpu.VMEM((6, EXT + PATCH, PATCH), F32),
            pltpu.VMEM((2, REST, REST), F32),
            pltpu.SemaphoreType.DMA((20,)),
            pltpu.SemaphoreType.DMA((8,)),
        ],
        compiler_params=pltpu.CompilerParams(vmem_limit_bytes=56 * 2**20),
        name="patches",
    )(*metas, probe, *tables, early_pg, amp, early, obj, right, lower, diag)


def exchange_kernel(
    pg_far, grad, total, from_above, from_left, from_diag,
    pg, loaded, buf0, red0, buf1, red1, buf2, buf3, own, res, passing,
    s0, r0, s1, r1, s2, r2, s3, r3, s4, r4, s5, r5, s6, r6, sh, rh, sent_to, got_to, sent_on, got_on,
):
    w = lax.axis_index("wide")
    c = lax.axis_index("col")
    y, k = lax.rem(w, 4), lax.div(w, 4)
    core, chip = lax.rem(c, 2), lax.div(c, 2)
    sibling = (w, 2 * chip + 1 - core)
    above, below = lax.rem(w + 15, 16), lax.rem(w + 1, 16)
    before, after = lax.rem(c + 15, 16), lax.rem(c + 1, 16)
    far_send, far_get = (y == 3) & (k < 3), (y == 0) & (k > 0)
    relays = (y < 3) & (k < 3)
    route = jnp.maximum(2 - y, 0)
    onward_to = lax.rem(w + 4 - y, 16)

    def rows(index, half):
        return pl.ds(pl.multiple_of(index * ROWS + half * (PATCH // 2), ROWS), ROWS)

    def planes(index):
        return pl.ds(index * 3, 3)

    chips = [(w, lax.rem(chip + d, 8) * 2 + core) for d in range(1, 8)]
    along_y = [(k * 4 + lax.rem(y + d, 4), c) for d in range(1, 4)]
    along_z = [(lax.rem(w + 4 * d, 16), c) for d in range(1, 4)]
    barrier = pltpu.get_barrier_semaphore()
    for target in [sibling] + chips + along_y + along_z:
        greet(barrier, target)
    for target in ((w, before), (above, c), (above, before)):
        greet(barrier, target)

    @pl.when(far_get)
    def _():
        for r in range(ROUTES):
            greet(barrier, (lax.rem(w + 12 + r, 16), c))

    load = pltpu.make_async_copy(pg_far, pg, loaded)
    load.start()
    pl.semaphore_wait(barrier, 17 + jnp.where(relays, 1, 0))

    zeroth = []
    for d in range(1, 9):
        p = lax.rem(chip + d, 8)
        copy = remote(pg_far.at[:, rows(p, 1 - core), :], buf0.at[d - 1], s0.at[d - 1], r0.at[d - 1], sibling)
        copy.start()
        zeroth.append(copy)

    def to_relay(r, j):
        at = TILE + DIRECT + 8 * (r * CHUNKS + j)
        return remote(
            grad.at[:, pl.ds(0, 4), pl.ds(at, 8), :], passing.at[j],
            sent_to.at[r * CHUNKS + j], got_to.at[j], (lax.rem(w + 15 - r, 16), c),
        )

    def onward(r, j):
        at = pl.multiple_of(DIRECT + 8 * (r * CHUNKS + j), 8)
        return remote(
            passing.at[j], from_above.at[:, :, pl.ds(at, 8), :],
            sent_on.at[j], got_on.at[r * CHUNKS + j], (onward_to, c),
        )

    def pass_on(chunks):
        @pl.when(relays)
        def _():
            for j in chunks:
                to_relay(0, j).wait_recv()
                onward(route, j).start()

    ups, downs = w > 0, w < 15
    lefts, rights = c > 0, c < 15
    near_send = downs & jnp.logical_not(far_send)
    near_get = ups & jnp.logical_not(far_get)
    strips = []

    def post(source, dest, target, sends, gets):
        copy = remote(source, dest, sh.at[len(strips)], rh.at[len(strips)], target)
        pl.when(sends)(copy.start)
        strips.append((copy, sends, gets))

    def post_rows(first, size, sends, gets):
        post(
            grad.at[:, pl.ds(0, 4), pl.ds(TILE + first, size), :],
            from_above.at[:, :, pl.ds(first, size), :], (below, c), sends, gets,
        )

    def post_columns(first, size):
        at = pl.ds(first, size)
        post(grad.at[:, 4, at, :], from_left.at[:, at, :], (w, after), rights, lefts)

    @pl.when(far_send)
    def _():
        for j in range(CHUNKS):
            for r in reversed(range(ROUTES)):
                to_relay(r, j).start()

    post_rows(DIRECT, 16, near_send, near_get)
    load.wait()
    first = []
    for d in range(1, 8):
        p = lax.rem(chip + d, 8)
        zeroth[d - 1].wait_recv()
        red0[d - 1] = pg[:, rows(p, core), :] + buf0[d - 1]
        copy = remote(red0.at[d - 1], buf1.at[d], s1.at[d], r1.at[d], chips[d - 1])
        copy.start()
        first.append(copy)
    zeroth[7].wait_recv()
    acc = pg[:, rows(chip, core), :] + buf0[7]

    post_rows(DIRECT + 16, 32, near_send, near_get)
    post(
        grad.at[:, 4, pl.ds(TILE, PATCH), :], from_diag, (below, after),
        downs & rights, ups & lefts,
    )
    pass_on(range(2))
    for d in range(1, 8):
        first[d - 1].wait_recv()
        acc = acc + buf1[d]
    red1[pl.ds(0, PLANES)] = acc
    red1[pl.ds(PLANES, 3)] = jnp.zeros((3, ROWS, PATCH), F32)
    second = []
    for d in range(1, 4):
        copy = remote(
            red1.at[planes(lax.rem(y + d, 4))], buf2.at[d], s2.at[d], r2.at[d], along_y[d - 1]
        )
        copy.start()
        second.append(copy)
    pass_on(range(2, CHUNKS))
    post_columns(0, 256)
    acc = red1[planes(y)]
    for d in range(1, 4):
        second[d - 1].wait_recv()
        acc = acc + buf2[d]
    buf3[k] = acc
    third = []
    for d in range(1, 4):
        copy = remote(buf3.at[k], buf3.at[k], s3.at[d], r3.at[d], along_z[d - 1])
        copy.start()
        third.append(copy)
    post_columns(256, 256)
    for d in range(1, 4):
        p = lax.rem(k + 4 - d, 4)
        remote(buf3.at[p], buf3.at[p], s3.at[d], r3.at[d], along_z[d - 1]).wait_recv()
    own[planes(y)] = buf3[0] + buf3[1] + buf3[2] + buf3[3]
    fourth = []
    for d in range(1, 4):
        copy = remote(own.at[planes(y)], own.at[planes(y)], s4.at[d], r4.at[d], along_y[d - 1])
        copy.start()
        fourth.append(copy)
    for d in range(1, 4):
        p = planes(lax.rem(y + 4 - d, 4))
        remote(own.at[p], own.at[p], s4.at[d], r4.at[d], along_y[d - 1]).wait_recv()
    lit = own[2 * MODES]
    res[...] = own[pl.ds(0, 2 * MODES)] / jnp.sqrt(lit + 1.0)[None]

    mine = rows(chip, core)
    fifth, sixth = [], []
    for d in range(1, 8):
        copy = remote(res, total.at[:, mine, :], s5.at[d], r5.at[d], chips[d - 1])
        copy.start()
        fifth.append(copy)
    copy = remote(res, total.at[:, mine, :], s6.at[0], r6.at[0], sibling)
    copy.start()
    sixth.append(copy)
    total[:, mine, :] = res[...]
    post_rows(DIRECT + 48, 72, near_send, near_get)
    post_rows(0, DIRECT, downs, ups)
    for d in range(1, 8):
        at = rows(lax.rem(chip + 8 - d, 8), core)
        remote(res, total.at[:, at, :], s5.at[d], r5.at[d], chips[d - 1]).wait_recv()
        copy = remote(total.at[:, at, :], total.at[:, at, :], s6.at[d], r6.at[d], sibling)
        copy.start()
        sixth.append(copy)
    for copy in zeroth + first + second + third + fourth + fifth:
        copy.wait_send()
    for d in range(8):
        at = rows(lax.rem(chip + 8 - d, 8), 1 - core)
        remote(res, total.at[:, at, :], s6.at[d], r6.at[d], sibling).wait_recv()
    for copy in sixth:
        copy.wait_send()
    for copy, sends, gets in strips:
        pl.when(gets)(copy.wait_recv)
        pl.when(sends)(copy.wait_send)

    @pl.when(far_get)
    def _():
        for r in range(ROUTES):
            for j in range(CHUNKS):
                onward(r, j).wait_recv()

    @pl.when(relays)
    def _():
        for j in range(CHUNKS):
            onward(0, j).wait_send()

    @pl.when(far_send)
    def _():
        for r in range(ROUTES):
            for j in range(CHUNKS):
                to_relay(r, j).wait_send()


def exchange(pg, grad):
    eight = pltpu.SemaphoreType.DMA((8,))
    four = pltpu.SemaphoreType.DMA((4,))
    many = pltpu.SemaphoreType.DMA((ROUTES * CHUNKS,))
    few = pltpu.SemaphoreType.DMA((CHUNKS,))
    return pl.pallas_call(
        exchange_kernel,
        out_shape=[
            jax.ShapeDtypeStruct((2 * MODES, PATCH, PATCH), F32),
            jax.ShapeDtypeStruct((2, 4, PATCH, PATCH), F32),
            jax.ShapeDtypeStruct((2, TILE, PATCH), F32),
            jax.ShapeDtypeStruct((2, PATCH, PATCH), F32),
        ],
        in_specs=[ANY_SPEC] * 2,
        out_specs=[VMEM_SPEC] + [ANY_SPEC] * 3,
        scratch_shapes=[
            pltpu.VMEM((PLANES, PATCH, PATCH), F32),
            pltpu.SemaphoreType.DMA,
            pltpu.VMEM((8, PLANES, ROWS, PATCH), F32),
            pltpu.VMEM((8, PLANES, ROWS, PATCH), F32),
            pltpu.VMEM((8, PLANES, ROWS, PATCH), F32),
            pltpu.VMEM((12, ROWS, PATCH), F32),
            pltpu.VMEM((4, 3, ROWS, PATCH), F32),
            pltpu.VMEM((4, 3, ROWS, PATCH), F32),
            pltpu.VMEM((12, ROWS, PATCH), F32),
            pltpu.VMEM((2 * MODES, ROWS, PATCH), F32),
            pltpu.VMEM((CHUNKS, 2, 4, 8, PATCH), F32),
        ]
        + [eight] * 4
        + [four] * 6
        + [eight] * 4
        + [eight] * 2
        + [many, few, few, many],
        compiler_params=pltpu.CompilerParams(
            collective_id=2, has_side_effects=True, vmem_limit_bytes=56 * 2**20
        ),
        name="exchange",
    )(pg, grad)


def finish_kernel(
    pre, obj, grad, weight, total, from_above, from_left, from_diag, new, direction,
    obj_top, obj_left, grad_top, grad_left, weight_top, weight_left, above, left, corner,
    new_top, new_left, held, sems, stored,
):
    del pre
    top, between, tiles = pl.ds(0, PATCH), pl.ds(PATCH, REST), pl.ds(0, 4)
    copies = []
    for source, dest in (
        (obj.at[:, between, top], obj_left),
        (grad.at[:, 0, between, :], grad_left),
        (weight.at[0, between, :], weight_left),
        (from_left, left),
        (total, held),
        (obj.at[:, top, :], obj_top),
        (grad.at[:, tiles, top, :], grad_top),
        (weight.at[:, top, :], weight_top),
        (from_above, above),
        (from_diag, corner),
    ):
        copy = pltpu.make_async_copy(source, dest, sems.at[len(copies)])
        copy.start()
        copies.append(copy)
    got_above, got_left = lax.axis_index("wide") > 0, lax.axis_index("col") > 0
    for copy in copies[:4]:
        copy.wait()
    scale = weight_left[...] + 1.0
    for p in range(2):
        sums = grad_left[p] + jnp.where(got_left, left[p, PATCH:], 0.0)
        new_left[p] = obj_left[p] + sums / scale
    left_out = pltpu.make_async_copy(new_left, new.at[:, between, top], stored.at[1])
    left_out.start()
    copies[4].wait()
    whole = pltpu.make_async_copy(held, direction, stored.at[0])
    whole.start()
    for copy in copies[5:]:
        copy.wait()
    for ct in range(4):
        lanes = slice(PATCH * ct, PATCH * (ct + 1))
        scale = weight_top[ct] + 1.0
        for p in range(2):
            sums = grad_top[p, ct] + jnp.where(got_above, above[p, ct], 0.0)
            if ct == 0:
                sums = sums + jnp.where(got_left, left[p, :PATCH], 0.0)
                sums = sums + jnp.where(got_above & got_left, corner[p], 0.0)
            new_top[p, :, lanes] = obj_top[p, :, lanes] + sums / scale
    top_out = pltpu.make_async_copy(new_top, new.at[:, top, :], stored.at[2])
    top_out.start()
    for copy in (whole, left_out, top_out):
        copy.wait()


def finish(pre, obj, grad, weight, total, from_above, from_left, from_diag):
    return pl.pallas_call(
        finish_kernel,
        out_shape=[
            jax.ShapeDtypeStruct((2, TILE, TILE), F32),
            jax.ShapeDtypeStruct((2 * MODES, PATCH, PATCH), F32),
        ],
        in_specs=[ANY_SPEC] * 8,
        out_specs=[ANY_SPEC] * 2,
        input_output_aliases={0: 0},
        scratch_shapes=[
            pltpu.VMEM((2, PATCH, TILE), F32),
            pltpu.VMEM((2, REST, PATCH), F32),
            pltpu.VMEM((2, 4, PATCH, PATCH), F32),
            pltpu.VMEM((2, REST, PATCH), F32),
            pltpu.VMEM((4, PATCH, PATCH), F32),
            pltpu.VMEM((REST, PATCH), F32),
            pltpu.VMEM((2, 4, PATCH, PATCH), F32),
            pltpu.VMEM((2, TILE, PATCH), F32),
            pltpu.VMEM((2, PATCH, PATCH), F32),
            pltpu.VMEM((2, PATCH, TILE), F32),
            pltpu.VMEM((2, REST, PATCH), F32),
            pltpu.VMEM((2 * MODES, PATCH, PATCH), F32),
            pltpu.SemaphoreType.DMA((10,)),
            pltpu.SemaphoreType.DMA((3,)),
        ],
        compiler_params=pltpu.CompilerParams(vmem_limit_bytes=56 * 2**20),
        name="finish",
    )(pre, obj, grad, weight, total, from_above, from_left, from_diag)


def local(object_field, probe_modes, amplitude, positions, slot_counts):
    slots = positions.shape[2]
    amp = amplitude.reshape(slots, PATCH, PATCH)
    table = left_table()
    tables = (jnp.asarray(table), jnp.asarray(table.T))
    meta = plan(positions.reshape(slots, 2).T, slot_counts)
    (right, lower, diag, *others), early, early_pg = halo_in(
        object_field, meta, probe_modes, tables, amp
    )
    pre, grad, weight, pg = patches(
        (meta, *others), probe_modes, tables, amp, early, early_pg,
        object_field, right, lower, diag,
    )
    total, from_above, from_left, from_diag = exchange(pg, grad)
    new_object, direction = finish(
        pre, object_field, grad, weight, total, from_above, from_left, from_diag
    )
    return new_object, direction.reshape(probe_modes.shape)


def solution(mesh):
    placed = (
        P(None, "wide", "col"),
        P(),
        P("wide", "col", None, None, None),
        P("wide", "col", None, None),
        P("wide", "col"),
    )
    return jax.shard_map(
        local, mesh=mesh, in_specs=placed, out_specs=(P(None, "wide", "col"), P()), check_vma=False
    )
```

```python
import functools
import math

import jax
import jax.numpy as jnp
import ml_dtypes
import numpy as np
from jax import lax
from jax.experimental import pallas as pl
from jax.experimental.pallas import tpu as pltpu
from jax.sharding import PartitionSpec as P

MESH = pl.DeviceIdType.MESH
F32 = jnp.float32
BF16 = jnp.bfloat16
PATCH = 128
TILE = 512
EXT = TILE + PATCH
MODES = 4
RING = 16
PLANES = 2 * MODES + 1
ROWS = PATCH // RING
PAIR = 2
CHUNKS = 5
ROUTES = 3
DIRECT = PATCH - ROUTES * 8 * CHUNKS
GROUP = 4
FIRST = 16
EARLY = 24
REST = TILE - PATCH
INSIDE = TILE - PATCH

VMEM_SPEC = pl.BlockSpec(memory_space=pltpu.VMEM)
SMEM_SPEC = pl.BlockSpec(memory_space=pltpu.SMEM)
ANY_SPEC = pl.BlockSpec(memory_space=pl.ANY)


def left_table():
    indices = np.arange(PATCH)
    angles = (indices[:, None] * indices[None, :] % PATCH) * (2.0 * math.pi / PATCH)
    cosine = np.cos(angles) / math.sqrt(PATCH)
    sine = -np.sin(angles) / math.sqrt(PATCH)
    whole = np.block([[cosine, -sine], [sine, cosine]])
    return whole.astype(np.float32).astype(ml_dtypes.bfloat16)


def plan_kernel(pos_ref, count_ref, meta_ref):
    count = count_ref[0, 0]
    slots = []
    inner_count, upper_count = jnp.int32(0), jnp.int32(0)
    for s in range(pos_ref.shape[1]):
        row, at = pos_ref[0, s], pos_ref[1, s]
        live = s < count
        upper = live & (row <= INSIDE)
        inner = upper & (at <= INSIDE)
        slots.append((row, at, live, upper, inner))
        inner_count = inner_count + jnp.where(inner, 1, 0)
        upper_count = upper_count + jnp.where(upper, 1, 0)
    low, middle, high = jnp.int32(0), inner_count, upper_count
    for s, (row, at, live, upper, inner) in enumerate(slots):
        outer = upper & jnp.logical_not(inner)
        place = jnp.where(inner, low, jnp.where(outer, middle, jnp.where(live, high, s)))
        meta_ref[0, place] = row
        meta_ref[1, place] = at
        meta_ref[3, place] = s
        low = low + jnp.where(inner, 1, 0)
        middle = middle + jnp.where(outer, 1, 0)
        high = high + jnp.where(live & jnp.logical_not(upper), 1, 0)
    for line in (0, 1, 3):
        meta_ref[line, pos_ref.shape[1]] = 0
    meta_ref[2, 0] = count
    meta_ref[2, 1] = inner_count
    meta_ref[2, 2] = upper_count


def plan(positions, slot_counts):
    return pl.pallas_call(
        plan_kernel,
        out_shape=jax.ShapeDtypeStruct((8, PATCH), jnp.int32),
        in_specs=[SMEM_SPEC] * 2,
        out_specs=SMEM_SPEC,
        name="plan",
    )(positions, slot_counts)


def lanes_of():
    return lax.broadcasted_iota(jnp.int32, (PATCH, PATCH), 1)


def both_sides(left, stacked, right_side):
    half = jnp.dot(left, stacked, preferred_element_type=F32).astype(BF16)
    lanes = [slice(PATCH * m, PATCH * (m + 1)) for m in range(MODES)]
    turned = jnp.concatenate(
        [jnp.concatenate([half[:PATCH, at], half[PATCH:, at]], 1) for at in lanes], 0
    )
    return jnp.dot(turned, right_side, preferred_element_type=F32)


def stack(re, im):
    return jnp.concatenate([jnp.concatenate(re, 1), jnp.concatenate(im, 1)], 0)


def parts(values, m):
    rows = slice(PATCH * m, PATCH * (m + 1))
    return values[rows, :PATCH], values[rows, PATCH:]


def solve(slots, ext, last, probe_ref, lt, rt, amp_ref, pg_ref):
    lane = lanes_of()
    patches_of, waves = [], []
    for s, row, at, live in slots:
        ct, shift = lax.shift_right_logical(at, 7), lax.bitwise_and(at, 127)
        back = lax.bitwise_and(PATCH - shift, 127)
        beside = jnp.minimum(ct + 1, last)
        rows = pl.ds(row, PATCH)
        patch = []
        for p in range(2):
            joined = jnp.where(lane >= shift, ext[p, ct, rows, :], ext[p, beside, rows, :])
            patch.append(pltpu.roll(joined, back, 1))
        patches_of.append(patch)
        re, im = [], []
        for m in range(MODES):
            pr, pi = probe_ref[0, m], probe_ref[1, m]
            re.append((pr * patch[0] - pi * patch[1]).astype(BF16))
            im.append((pr * patch[1] + pi * patch[0]).astype(BF16))
        waves.append(stack(re, im))
    fars = [both_sides(lt, wave, rt) for wave in waves]
    residuals = []
    for (s, row, at, live), far in zip(slots, fars):
        intensity = jnp.zeros((PATCH, PATCH), F32)
        for m in range(MODES):
            fr, fi = parts(far, m)
            intensity = intensity + fr * fr + fi * fi
        measured = amp_ref[s].astype(F32)
        factor = (measured * lax.rsqrt(jnp.maximum(intensity, 1.0)) - 1.0) * live
        re, im = [], []
        for m in range(MODES):
            fr, fi = parts(far, m)
            re.append((fr * factor).astype(BF16))
            im.append((fi * factor).astype(BF16))
        residuals.append(stack(re, im))
    updates = [both_sides(rt, residual, lt) for residual in residuals]
    for m in range(MODES):
        sum_re, sum_im = pg_ref[m], pg_ref[MODES + m]
        for patch, update in zip(patches_of, updates):
            ur, ui = parts(update, m)
            sum_re = sum_re + patch[0] * ur + patch[1] * ui
            sum_im = sum_im + patch[0] * ui - patch[1] * ur
        pg_ref[m] = sum_re
        pg_ref[MODES + m] = sum_im
    lit = pg_ref[2 * MODES]
    for (s, row, at, live), patch in zip(slots, patches_of):
        lit = lit + live * (patch[0] * patch[0] + patch[1] * patch[1])
    pg_ref[2 * MODES] = lit
    grads = []
    for update in updates:
        grad_re = jnp.zeros((PATCH, PATCH), F32)
        grad_im = grad_re
        for m in range(MODES):
            pr, pi = probe_ref[0, m], probe_ref[1, m]
            ur, ui = parts(update, m)
            grad_re = grad_re + pr * ur + pi * ui
            grad_im = grad_im + pr * ui - pi * ur
        grads.append((grad_re, grad_im))
    return grads


def remote(source, dest, sent, got, target):
    return pltpu.make_async_remote_copy(
        source, dest, sent, got, device_id=target, device_id_type=MESH
    )


def greet(barrier, target):
    pl.semaphore_signal(barrier, inc=1, device_id=target, device_id_type=MESH)


def halo_in_kernel(
    obj, meta, meta_ref, probe, left_side, right_side, amp,
    right, lower, diag, meta_above, meta_left, meta_diag, early, pg_ref,
    ext, wide_ext, amp_ref, probe_ref, lt_ref, rt_ref, early_ref, passing, fetched, stored,
    sent, got, sent_to, got_to, sent_on, got_on,
):
    w = lax.axis_index("wide")
    c = lax.axis_index("col")
    y, k = lax.rem(w, 4), lax.div(w, 4)
    above, below = lax.rem(w + 15, 16), lax.rem(w + 1, 16)
    before, after = lax.rem(c + 15, 16), lax.rem(c + 1, 16)
    far_send, far_get = (y == 0) & (k > 0), (y == 3) & (k < 3)
    relays = (y > 0) & (k > 0)
    route = jnp.maximum(y - 1, 0)
    onward_to = lax.rem(w + 15 - y, 16)
    barrier = pltpu.get_barrier_semaphore()
    for target in (
        (w, after), (below, c), (below, after), (w, before), (above, c), (above, before)
    ):
        greet(barrier, target)
    pl.when(relays & (y > 1))(lambda: greet(barrier, (lax.rem(w + 16 - y, 16), c)))

    @pl.when(far_get)
    def _():
        for r in range(ROUTES):
            greet(barrier, (lax.rem(w + 2 + r, 16), c))

    inward = [
        pltpu.make_async_copy(source, dest, fetched.at[10 + j])
        for j, (source, dest) in enumerate(
            ((amp, amp_ref), (probe, probe_ref), (left_side, lt_ref), (right_side, rt_ref))
        )
    ]
    for ct in range(4):
        inward.append(pltpu.make_async_copy(
            obj.at[:, :, pl.ds(PATCH * ct, PATCH)], ext.at[:, ct], fetched.at[ct]
        ))
    beside = [
        pltpu.make_async_copy(
            obj.at[:, :, pl.ds(PATCH * ct, PATCH)], wide_ext.at[:, ct], fetched.at[5 + ct]
        )
        for ct in range(4)
    ]
    for copy in inward + beside:
        copy.start()
    pl.semaphore_wait(barrier, 6 + jnp.where(far_send, 2, jnp.where(relays, 1, 0)))

    def strip(first, rows):
        return pl.ds(first, rows)

    def to_relay(r, j):
        at = strip(DIRECT + 8 * (r * CHUNKS + j), 8)
        return remote(
            obj.at[:, at, :], passing.at[j], sent_to.at[r * CHUNKS + j], got_to.at[j],
            (lax.rem(w + r + 1, 16), c),
        )

    def onward(r, j):
        start = pl.multiple_of(DIRECT + 8 * (r * CHUNKS + j), 8)
        return remote(
            passing.at[j], lower.at[:, strip(start, 8), :],
            sent_on.at[j], got_on.at[r * CHUNKS + j], (onward_to, c),
        )

    @pl.when(far_send)
    def _():
        for j in range(CHUNKS):
            for r in reversed(range(ROUTES)):
                to_relay(r, j).start()

    ups, downs = w > 0, w < 15
    lefts, rights = c > 0, c < 15
    near_send = ups & jnp.logical_not(far_send)
    near_get = downs & jnp.logical_not(far_get)
    top = pl.ds(0, PATCH)
    some, rest = strip(0, DIRECT), strip(DIRECT, PATCH - DIRECT)
    plain = (
        (meta, meta_above, (below, c), downs, ups),
        (meta, meta_left, (w, after), rights, lefts),
        (meta, meta_diag, (below, after), downs & rights, ups & lefts),
        (obj.at[:, some, :], lower.at[:, some, :], (above, c), ups, downs),
        (obj.at[:, rest, :], lower.at[:, rest, :], (above, c), near_send, near_get),
        (obj.at[:, top, top], diag, (above, before), ups & lefts, downs & rights),
        (obj.at[:, :, top], wide_ext.at[:, 4], (w, before), lefts, rights),
    )
    made = []
    for j, (source, dest, target, sends, gets) in enumerate(plain):
        copy = remote(source, dest, sent.at[j], got.at[j], target)
        pl.when(sends)(copy.start)
        made.append((copy, sends, gets))

    pg_ref[...] = jnp.zeros(pg_ref.shape, F32)
    inner = meta_ref[2, 1]
    for copy in inward:
        copy.wait()
    lt = lt_ref[...]
    rt = rt_ref[...]

    def put(index):
        pair = pl.ds(index * GROUP, GROUP)
        return pltpu.make_async_copy(early_ref.at[pair], early.at[pair], stored.at[index])

    def solve_some(index, first_slot, live_slots, tiles, last, columns):
        slots = []
        for u in range(GROUP):
            j = first_slot + u
            row, at = jnp.minimum(meta_ref[0, j], INSIDE), jnp.minimum(meta_ref[1, j], columns)
            slots.append((meta_ref[3, j], row, at, (j < live_slots).astype(F32)))
        grads = solve(slots, tiles, last, probe_ref, lt, rt, amp_ref, pg_ref)
        for u, (grad_re, grad_im) in enumerate(grads):
            early_ref[index * GROUP + u, 0] = grad_re
            early_ref[index * GROUP + u, 1] = grad_im
        put(index).start()

        for half in range(2):
            @pl.when(relays & (2 * index + half < CHUNKS))
            def _(j=2 * index + half):
                to_relay(0, j).wait_recv()
                onward(route, j).start()

    def first_step(index, carry):
        solve_some(index, index * GROUP, inner, ext, 3, INSIDE)
        return carry

    lax.fori_loop(0, FIRST // GROUP, first_step, 0)
    for copy in beside:
        copy.wait()
    pl.when(rights)(made[-1][0].wait_recv)

    @pl.when(c == 15)
    def _():
        wide_ext[:, 4] = jnp.zeros((2, TILE, PATCH), F32)

    keep = pltpu.make_async_copy(wide_ext.at[:, 4], right, fetched.at[9])
    keep.start()
    base = jnp.minimum(inner, FIRST)
    upper = meta_ref[2, 2]

    def next_step(index, carry):
        solve_some(index, base + index * GROUP - FIRST, upper, wide_ext, 4, TILE - 1)
        return carry

    lax.fori_loop(FIRST // GROUP, EARLY // GROUP, next_step, 0)
    keep.wait()
    for index in range(EARLY // GROUP):
        put(index).wait()
    for copy, sends, gets in made[:-1]:
        pl.when(gets)(copy.wait_recv)
        pl.when(sends)(copy.wait_send)
    pl.when(lefts)(made[-1][0].wait_send)

    @pl.when(far_get)
    def _():
        for r in range(ROUTES):
            for j in range(CHUNKS):
                onward(r, j).wait_recv()

    @pl.when(relays)
    def _():
        for j in range(CHUNKS):
            onward(0, j).wait_send()

    @pl.when(far_send)
    def _():
        for r in range(ROUTES):
            for j in range(CHUNKS):
                to_relay(r, j).wait_send()


def halo_in(obj, meta, probe, tables, amp):
    note = jax.ShapeDtypeStruct(meta.shape, meta.dtype)
    made = pl.pallas_call(
        halo_in_kernel,
        out_shape=[
            jax.ShapeDtypeStruct((2, TILE, PATCH), F32),
            jax.ShapeDtypeStruct((2, PATCH, TILE), F32),
            jax.ShapeDtypeStruct((2, PATCH, PATCH), F32),
            note,
            note,
            note,
            jax.ShapeDtypeStruct((EARLY, 2, PATCH, PATCH), F32),
            jax.ShapeDtypeStruct((PLANES, PATCH, PATCH), F32),
        ],
        in_specs=[ANY_SPEC] * 2 + [SMEM_SPEC] + [ANY_SPEC] * 4,
        out_specs=[ANY_SPEC] * 7 + [VMEM_SPEC],
        scratch_shapes=[
            pltpu.VMEM((2, 4, TILE, PATCH), F32),
            pltpu.VMEM((2, 5, TILE, PATCH), F32),
            pltpu.VMEM(amp.shape, amp.dtype),
            pltpu.VMEM(probe.shape, F32),
            pltpu.VMEM(tables[0].shape, BF16),
            pltpu.VMEM(tables[0].shape, BF16),
            pltpu.VMEM((EARLY, 2, PATCH, PATCH), F32),
            pltpu.VMEM((CHUNKS, 2, 8, TILE), F32),
            pltpu.SemaphoreType.DMA((14,)),
            pltpu.SemaphoreType.DMA((EARLY // GROUP,)),
        ]
        + [pltpu.SemaphoreType.DMA((7,))] * 2
        + [pltpu.SemaphoreType.DMA((ROUTES * CHUNKS,)), pltpu.SemaphoreType.DMA((CHUNKS,))]
        + [pltpu.SemaphoreType.DMA((CHUNKS,)), pltpu.SemaphoreType.DMA((ROUTES * CHUNKS,))],
        compiler_params=pltpu.CompilerParams(
            collective_id=1, has_side_effects=True, vmem_limit_bytes=56 * 2**20
        ),
        name="halo_in",
    )(obj, meta, meta, probe, *tables, amp)
    return made[:6], made[6], made[7]


def patches_kernel(
    meta, meta_above, meta_left, meta_diag, probe, left_side, right_side,
    early_pg, amp, early, obj, right, lower, diag,
    pre, grad, weight, pg,
    meta_ref, above_ref, left_ref, diag_ref, probe_ref, lt_ref, rt_ref, pg_ref, amp_ref, early_ref,
    ext, grad_ref, spread, inner_ref, sems, stored,
):
    copies = []

    def fetch(source, dest):
        copy = pltpu.make_async_copy(source, dest, sems.at[len(copies)])
        copy.start()
        copies.append(copy)

    fetch(probe, probe_ref)
    fetch(meta, meta_ref)
    fetch(meta_above, above_ref)
    fetch(meta_left, left_ref)
    fetch(meta_diag, diag_ref)
    at_first = len(copies)
    fetch(early, early_ref)
    fetch(left_side, lt_ref)
    fetch(right_side, rt_ref)
    fetch(early_pg, pg_ref)
    fetch(amp, amp_ref)
    for ct in range(4):
        lanes = pl.ds(PATCH * ct, PATCH)
        fetch(obj.at[:, :, lanes], ext.at[:, ct, pl.ds(0, TILE), :])
        fetch(lower.at[:, :, lanes], ext.at[:, ct, pl.ds(TILE, PATCH), :])
    fetch(right, ext.at[:, 4, pl.ds(0, TILE), :])
    fetch(diag, ext.at[:, 4, pl.ds(TILE, PATCH), :])
    grad_ref[...] = jnp.zeros(grad_ref.shape, F32)
    spread[...] = jnp.zeros(spread.shape, F32)
    for copy in copies[:at_first]:
        copy.wait()
    w = lax.axis_index("wide")
    c = lax.axis_index("col")
    lane = lanes_of()
    count = meta_ref[2, 0]
    base = jnp.minimum(meta_ref[2, 1], FIRST)
    done = jnp.minimum(meta_ref[2, 2], base + EARLY - FIRST)
    power = jnp.sum(probe_ref[...] * probe_ref[...], axis=(0, 1))

    def scatter(ref, row, at, value):
        ct, shift = lax.shift_right_logical(at, 7), lax.bitwise_and(at, 127)
        turned = pltpu.roll(value, shift, 1)
        first = lane >= shift
        zero = jnp.zeros_like(turned)
        rows = pl.ds(row, PATCH)
        ref[ct, rows, :] += jnp.where(first, turned, zero)
        ref[ct + 1, rows, :] += jnp.where(first, zero, turned)

    for ref, there, down, side in (
        (meta_ref, None, 0, 0),
        (above_ref, w > 0, TILE, 0),
        (left_ref, c > 0, 0, TILE),
        (diag_ref, (w > 0) & (c > 0), TILE, TILE),
    ):
        live_there = ref[2, 0] if there is None else jnp.where(there, ref[2, 0], 0)

        def weigh(index, carry, ref=ref, down=down, side=side, live_there=live_there):
            for s in (2 * index, 2 * index + 1):
                row, at = ref[0, s] + (PATCH - down), ref[1, s] + (PATCH - side)
                live = s < live_there
                if down or side:
                    touches = live
                    if down:
                        touches = touches & (row > 0)
                    if side:
                        touches = touches & (at > 0)
                    pl.when(touches)(functools.partial(scatter, spread, row, at, power))
                else:
                    scatter(spread, row, at, power * live.astype(F32))
            return carry

        lax.fori_loop(0, (live_there + 1) // 2, weigh, 0)
    weights_out = pltpu.make_async_copy(
        spread.at[pl.ds(1, 4), pl.ds(PATCH, TILE), :], weight, stored.at[0]
    )
    weights_out.start()
    copies[at_first].wait()

    def place(index, carry):
        for j in (2 * index, 2 * index + 1):
            held = jnp.minimum(jnp.where(j < base, j, j - base + FIRST), EARLY - 1)
            for p in range(2):
                value = jnp.where(j < done, early_ref[held, p], 0.0)
                scatter(grad_ref.at[p], meta_ref[0, j], meta_ref[1, j], value)
        return carry

    lax.fori_loop(0, (done + 1) // 2, place, 0)
    for copy in copies[at_first + 1 :]:
        copy.wait()

    @pl.when(w == 15)
    def _():
        ext[:, :, TILE:, :] = jnp.zeros((2, 5, PATCH, PATCH), F32)

    @pl.when(c == 15)
    def _():
        ext[:, 4, :, :] = jnp.zeros((2, EXT, PATCH), F32)

    lt = lt_ref[...]
    rt = rt_ref[...]

    def steps(first_slot, size, number):
        def step(index, carry):
            slots = []
            for u in range(size):
                j = first_slot + index * size + u
                live = (j < count).astype(F32)
                slots.append((meta_ref[3, j], meta_ref[0, j], meta_ref[1, j], live))
            grads = solve(slots, ext, 4, probe_ref, lt, rt, amp_ref, pg_ref)
            for (s, row, at, live), (grad_re, grad_im) in zip(slots, grads):
                scatter(grad_ref.at[0], row, at, grad_re)
                scatter(grad_ref.at[1], row, at, grad_im)
            return carry

        lax.fori_loop(0, number, step, 0)

    whole = (count - done) // GROUP
    left_over = done + whole * GROUP
    steps(done, GROUP, whole)
    steps(left_over, PAIR, (count - left_over + PAIR - 1) // PAIR)
    outward = [weights_out]
    low, top, between = pl.ds(TILE, PATCH), pl.ds(0, PATCH), pl.ds(PATCH, REST)
    for source, dest in (
        (pg_ref, pg),
        (grad_ref.at[:, :, low, :], grad.at[:, :, low, :]),
        (grad_ref.at[:, 4, pl.ds(0, TILE), :], grad.at[:, 4, pl.ds(0, TILE), :]),
        (grad_ref.at[:, pl.ds(0, 4), top, :], grad.at[:, pl.ds(0, 4), top, :]),
        (grad_ref.at[:, 0, between, :], grad.at[:, 0, between, :]),
    ):
        copy = pltpu.make_async_copy(source, dest, stored.at[len(outward)])
        copy.start()
        outward.append(copy)
    inside = slice(PATCH, TILE)
    for ct in range(1, 4):
        scale = spread[ct + 1, PATCH + PATCH : PATCH + TILE, :] + 1.0
        lanes = slice(PATCH * (ct - 1), PATCH * ct)
        for p in range(2):
            inner_ref[p, :, lanes] = ext[p, ct, inside, :] + grad_ref[p, ct, inside, :] / scale
    copy = pltpu.make_async_copy(
        inner_ref, pre.at[:, between, between], stored.at[len(outward)]
    )
    copy.start()
    for copy in outward + [copy]:
        copy.wait()


def patches(metas, probe, tables, amp, early, early_pg, obj, right, lower, diag):
    return pl.pallas_call(
        patches_kernel,
        out_shape=[
            jax.ShapeDtypeStruct((2, TILE, TILE), F32),
            jax.ShapeDtypeStruct((2, 5, EXT, PATCH), F32),
            jax.ShapeDtypeStruct((4, TILE, PATCH), F32),
            jax.ShapeDtypeStruct((PLANES, PATCH, PATCH), F32),
        ],
        in_specs=[ANY_SPEC] * 14,
        out_specs=[ANY_SPEC] * 4,
        scratch_shapes=[pltpu.SMEM(metas[0].shape, jnp.int32)] * 4
        + [
            pltpu.VMEM(probe.shape, F32),
            pltpu.VMEM(tables[0].shape, BF16),
            pltpu.VMEM(tables[0].shape, BF16),
            pltpu.VMEM((PLANES, PATCH, PATCH), F32),
            pltpu.VMEM(amp.shape, amp.dtype),
            pltpu.VMEM(early.shape, early.dtype),
            pltpu.VMEM((2, 5, EXT, PATCH), F32),
            pltpu.VMEM((2, 5, EXT, PATCH), F32),
            pltpu.VMEM((6, EXT + PATCH, PATCH), F32),
            pltpu.VMEM((2, REST, REST), F32),
            pltpu.SemaphoreType.DMA((20,)),
            pltpu.SemaphoreType.DMA((8,)),
        ],
        compiler_params=pltpu.CompilerParams(vmem_limit_bytes=56 * 2**20),
        name="patches",
    )(*metas, probe, *tables, early_pg, amp, early, obj, right, lower, diag)


def exchange_kernel(
    pg_far, grad, total, from_above, from_left, from_diag,
    pg, loaded, buf0, red0, buf1, red1, buf2, buf3, own, res, passing,
    s0, r0, s1, r1, s2, r2, s3, r3, s4, r4, s5, r5, s6, r6, sh, rh, sent_to, got_to, sent_on, got_on,
):
    w = lax.axis_index("wide")
    c = lax.axis_index("col")
    y, k = lax.rem(w, 4), lax.div(w, 4)
    core, chip = lax.rem(c, 2), lax.div(c, 2)
    sibling = (w, 2 * chip + 1 - core)
    above, below = lax.rem(w + 15, 16), lax.rem(w + 1, 16)
    before, after = lax.rem(c + 15, 16), lax.rem(c + 1, 16)
    far_send, far_get = (y == 3) & (k < 3), (y == 0) & (k > 0)
    relays = (y < 3) & (k < 3)
    route = jnp.maximum(2 - y, 0)
    onward_to = lax.rem(w + 4 - y, 16)

    def rows(index, half):
        return pl.ds(pl.multiple_of(index * ROWS + half * (PATCH // 2), ROWS), ROWS)

    def planes(index):
        return pl.ds(index * 3, 3)

    chips = [(w, lax.rem(chip + d, 8) * 2 + core) for d in range(1, 8)]
    along_y = [(k * 4 + lax.rem(y + d, 4), c) for d in range(1, 4)]
    along_z = [(lax.rem(w + 4 * d, 16), c) for d in range(1, 4)]
    barrier = pltpu.get_barrier_semaphore()
    for target in [sibling] + chips + along_y + along_z:
        greet(barrier, target)
    for target in ((w, before), (above, c), (above, before)):
        greet(barrier, target)

    @pl.when(far_get)
    def _():
        for r in range(ROUTES):
            greet(barrier, (lax.rem(w + 12 + r, 16), c))

    load = pltpu.make_async_copy(pg_far, pg, loaded)
    load.start()
    pl.semaphore_wait(barrier, 17 + jnp.where(relays, 1, 0))

    zeroth = []
    for d in range(1, 9):
        p = lax.rem(chip + d, 8)
        copy = remote(pg_far.at[:, rows(p, 1 - core), :], buf0.at[d - 1], s0.at[d - 1], r0.at[d - 1], sibling)
        copy.start()
        zeroth.append(copy)

    def to_relay(r, j):
        at = TILE + DIRECT + 8 * (r * CHUNKS + j)
        return remote(
            grad.at[:, pl.ds(0, 4), pl.ds(at, 8), :], passing.at[j],
            sent_to.at[r * CHUNKS + j], got_to.at[j], (lax.rem(w + 15 - r, 16), c),
        )

    def onward(r, j):
        at = pl.multiple_of(DIRECT + 8 * (r * CHUNKS + j), 8)
        return remote(
            passing.at[j], from_above.at[:, :, pl.ds(at, 8), :],
            sent_on.at[j], got_on.at[r * CHUNKS + j], (onward_to, c),
        )

    def pass_on(chunks):
        @pl.when(relays)
        def _():
            for j in chunks:
                to_relay(0, j).wait_recv()
                onward(route, j).start()

    ups, downs = w > 0, w < 15
    lefts, rights = c > 0, c < 15
    near_send = downs & jnp.logical_not(far_send)
    near_get = ups & jnp.logical_not(far_get)
    strips = []

    def post(source, dest, target, sends, gets):
        copy = remote(source, dest, sh.at[len(strips)], rh.at[len(strips)], target)
        pl.when(sends)(copy.start)
        strips.append((copy, sends, gets))

    def post_rows(first, size, sends, gets):
        post(
            grad.at[:, pl.ds(0, 4), pl.ds(TILE + first, size), :],
            from_above.at[:, :, pl.ds(first, size), :], (below, c), sends, gets,
        )

    def post_columns(first, size):
        at = pl.ds(first, size)
        post(grad.at[:, 4, at, :], from_left.at[:, at, :], (w, after), rights, lefts)

    @pl.when(far_send)
    def _():
        for j in range(CHUNKS):
            for r in reversed(range(ROUTES)):
                to_relay(r, j).start()

    post_rows(DIRECT, 16, near_send, near_get)
    load.wait()
    first = []
    for d in range(1, 8):
        p = lax.rem(chip + d, 8)
        zeroth[d - 1].wait_recv()
        red0[d - 1] = pg[:, rows(p, core), :] + buf0[d - 1]
        copy = remote(red0.at[d - 1], buf1.at[d], s1.at[d], r1.at[d], chips[d - 1])
        copy.start()
        first.append(copy)
    zeroth[7].wait_recv()
    acc = pg[:, rows(chip, core), :] + buf0[7]

    post_rows(DIRECT + 16, 32, near_send, near_get)
    post(
        grad.at[:, 4, pl.ds(TILE, PATCH), :], from_diag, (below, after),
        downs & rights, ups & lefts,
    )
    pass_on(range(2))
    for d in range(1, 8):
        first[d - 1].wait_recv()
        acc = acc + buf1[d]
    red1[pl.ds(0, PLANES)] = acc
    red1[pl.ds(PLANES, 3)] = jnp.zeros((3, ROWS, PATCH), F32)
    second = []
    for d in range(1, 4):
        copy = remote(
            red1.at[planes(lax.rem(y + d, 4))], buf2.at[d], s2.at[d], r2.at[d], along_y[d - 1]
        )
        copy.start()
        second.append(copy)
    pass_on(range(2, CHUNKS))
    post_columns(0, 256)
    acc = red1[planes(y)]
    for d in range(1, 4):
        second[d - 1].wait_recv()
        acc = acc + buf2[d]
    buf3[k] = acc
    third = []
    for d in range(1, 4):
        copy = remote(buf3.at[k], buf3.at[k], s3.at[d], r3.at[d], along_z[d - 1])
        copy.start()
        third.append(copy)
    post_columns(256, 256)
    for d in range(1, 4):
        p = lax.rem(k + 4 - d, 4)
        remote(buf3.at[p], buf3.at[p], s3.at[d], r3.at[d], along_z[d - 1]).wait_recv()
    own[planes(y)] = buf3[0] + buf3[1] + buf3[2] + buf3[3]
    fourth = []
    for d in range(1, 4):
        copy = remote(own.at[planes(y)], own.at[planes(y)], s4.at[d], r4.at[d], along_y[d - 1])
        copy.start()
        fourth.append(copy)
    for d in range(1, 4):
        p = planes(lax.rem(y + 4 - d, 4))
        remote(own.at[p], own.at[p], s4.at[d], r4.at[d], along_y[d - 1]).wait_recv()
    lit = own[2 * MODES]
    res[...] = own[pl.ds(0, 2 * MODES)] / jnp.sqrt(lit + 1.0)[None]

    mine = rows(chip, core)
    fifth, sixth = [], []
    for d in range(1, 8):
        copy = remote(res, total.at[:, mine, :], s5.at[d], r5.at[d], chips[d - 1])
        copy.start()
        fifth.append(copy)
    copy = remote(res, total.at[:, mine, :], s6.at[0], r6.at[0], sibling)
    copy.start()
    sixth.append(copy)
    total[:, mine, :] = res[...]
    post_rows(DIRECT + 48, 72, near_send, near_get)
    post_rows(0, DIRECT, downs, ups)
    for d in range(1, 8):
        at = rows(lax.rem(chip + 8 - d, 8), core)
        remote(res, total.at[:, at, :], s5.at[d], r5.at[d], chips[d - 1]).wait_recv()
        copy = remote(total.at[:, at, :], total.at[:, at, :], s6.at[d], r6.at[d], sibling)
        copy.start()
        sixth.append(copy)
    for copy in zeroth + first + second + third + fourth + fifth:
        copy.wait_send()
    for d in range(8):
        at = rows(lax.rem(chip + 8 - d, 8), 1 - core)
        remote(res, total.at[:, at, :], s6.at[d], r6.at[d], sibling).wait_recv()
    for copy in sixth:
        copy.wait_send()
    for copy, sends, gets in strips:
        pl.when(gets)(copy.wait_recv)
        pl.when(sends)(copy.wait_send)

    @pl.when(far_get)
    def _():
        for r in range(ROUTES):
            for j in range(CHUNKS):
                onward(r, j).wait_recv()

    @pl.when(relays)
    def _():
        for j in range(CHUNKS):
            onward(0, j).wait_send()

    @pl.when(far_send)
    def _():
        for r in range(ROUTES):
            for j in range(CHUNKS):
                to_relay(r, j).wait_send()


def exchange(pg, grad):
    eight = pltpu.SemaphoreType.DMA((8,))
    four = pltpu.SemaphoreType.DMA((4,))
    many = pltpu.SemaphoreType.DMA((ROUTES * CHUNKS,))
    few = pltpu.SemaphoreType.DMA((CHUNKS,))
    return pl.pallas_call(
        exchange_kernel,
        out_shape=[
            jax.ShapeDtypeStruct((2 * MODES, PATCH, PATCH), F32),
            jax.ShapeDtypeStruct((2, 4, PATCH, PATCH), F32),
            jax.ShapeDtypeStruct((2, TILE, PATCH), F32),
            jax.ShapeDtypeStruct((2, PATCH, PATCH), F32),
        ],
        in_specs=[ANY_SPEC] * 2,
        out_specs=[VMEM_SPEC] + [ANY_SPEC] * 3,
        scratch_shapes=[
            pltpu.VMEM((PLANES, PATCH, PATCH), F32),
            pltpu.SemaphoreType.DMA,
            pltpu.VMEM((8, PLANES, ROWS, PATCH), F32),
            pltpu.VMEM((8, PLANES, ROWS, PATCH), F32),
            pltpu.VMEM((8, PLANES, ROWS, PATCH), F32),
            pltpu.VMEM((12, ROWS, PATCH), F32),
            pltpu.VMEM((4, 3, ROWS, PATCH), F32),
            pltpu.VMEM((4, 3, ROWS, PATCH), F32),
            pltpu.VMEM((12, ROWS, PATCH), F32),
            pltpu.VMEM((2 * MODES, ROWS, PATCH), F32),
            pltpu.VMEM((CHUNKS, 2, 4, 8, PATCH), F32),
        ]
        + [eight] * 4
        + [four] * 6
        + [eight] * 4
        + [eight] * 2
        + [many, few, few, many],
        compiler_params=pltpu.CompilerParams(
            collective_id=2, has_side_effects=True, vmem_limit_bytes=56 * 2**20
        ),
        name="exchange",
    )(pg, grad)


def finish_kernel(
    pre, obj, grad, weight, total, from_above, from_left, from_diag, new, direction,
    obj_top, obj_left, grad_top, grad_left, weight_top, weight_left, above, left, corner,
    new_top, new_left, held, sems, stored,
):
    del pre
    top, between, tiles = pl.ds(0, PATCH), pl.ds(PATCH, REST), pl.ds(0, 4)
    copies = []
    for source, dest in (
        (obj.at[:, between, top], obj_left),
        (grad.at[:, 0, between, :], grad_left),
        (weight.at[0, between, :], weight_left),
        (from_left, left),
        (total, held),
        (obj.at[:, top, :], obj_top),
        (grad.at[:, tiles, top, :], grad_top),
        (weight.at[:, top, :], weight_top),
        (from_above, above),
        (from_diag, corner),
    ):
        copy = pltpu.make_async_copy(source, dest, sems.at[len(copies)])
        copy.start()
        copies.append(copy)
    got_above, got_left = lax.axis_index("wide") > 0, lax.axis_index("col") > 0
    for copy in copies[:4]:
        copy.wait()
    scale = weight_left[...] + 1.0
    for p in range(2):
        sums = grad_left[p] + jnp.where(got_left, left[p, PATCH:], 0.0)
        new_left[p] = obj_left[p] + sums / scale
    left_out = pltpu.make_async_copy(new_left, new.at[:, between, top], stored.at[1])
    left_out.start()
    copies[4].wait()
    whole = pltpu.make_async_copy(held, direction, stored.at[0])
    whole.start()
    for copy in copies[5:]:
        copy.wait()
    for ct in range(4):
        lanes = slice(PATCH * ct, PATCH * (ct + 1))
        scale = weight_top[ct] + 1.0
        for p in range(2):
            sums = grad_top[p, ct] + jnp.where(got_above, above[p, ct], 0.0)
            if ct == 0:
                sums = sums + jnp.where(got_left, left[p, :PATCH], 0.0)
                sums = sums + jnp.where(got_above & got_left, corner[p], 0.0)
            new_top[p, :, lanes] = obj_top[p, :, lanes] + sums / scale
    top_out = pltpu.make_async_copy(new_top, new.at[:, top, :], stored.at[2])
    top_out.start()
    for copy in (whole, left_out, top_out):
        copy.wait()


def finish(pre, obj, grad, weight, total, from_above, from_left, from_diag):
    return pl.pallas_call(
        finish_kernel,
        out_shape=[
            jax.ShapeDtypeStruct((2, TILE, TILE), F32),
            jax.ShapeDtypeStruct((2 * MODES, PATCH, PATCH), F32),
        ],
        in_specs=[ANY_SPEC] * 8,
        out_specs=[ANY_SPEC] * 2,
        input_output_aliases={0: 0},
        scratch_shapes=[
            pltpu.VMEM((2, PATCH, TILE), F32),
            pltpu.VMEM((2, REST, PATCH), F32),
            pltpu.VMEM((2, 4, PATCH, PATCH), F32),
            pltpu.VMEM((2, REST, PATCH), F32),
            pltpu.VMEM((4, PATCH, PATCH), F32),
            pltpu.VMEM((REST, PATCH), F32),
            pltpu.VMEM((2, 4, PATCH, PATCH), F32),
            pltpu.VMEM((2, TILE, PATCH), F32),
            pltpu.VMEM((2, PATCH, PATCH), F32),
            pltpu.VMEM((2, PATCH, TILE), F32),
            pltpu.VMEM((2, REST, PATCH), F32),
            pltpu.VMEM((2 * MODES, PATCH, PATCH), F32),
            pltpu.SemaphoreType.DMA((10,)),
            pltpu.SemaphoreType.DMA((3,)),
        ],
        compiler_params=pltpu.CompilerParams(vmem_limit_bytes=56 * 2**20),
        name="finish",
    )(pre, obj, grad, weight, total, from_above, from_left, from_diag)


def local(object_field, probe_modes, amplitude, positions, slot_counts):
    slots = positions.shape[2]
    amp = amplitude.reshape(slots, PATCH, PATCH)
    table = left_table()
    tables = (jnp.asarray(table), jnp.asarray(table.T))
    meta = plan(positions.reshape(slots, 2).T, slot_counts)
    (right, lower, diag, *others), early, early_pg = halo_in(
        object_field, meta, probe_modes, tables, amp
    )
    pre, grad, weight, pg = patches(
        (meta, *others), probe_modes, tables, amp, early, early_pg,
        object_field, right, lower, diag,
    )
    total, from_above, from_left, from_diag = exchange(pg, grad)
    new_object, direction = finish(
        pre, object_field, grad, weight, total, from_above, from_left, from_diag
    )
    return new_object, direction.reshape(probe_modes.shape)


def solution(mesh):
    placed = (
        P(None, "wide", "col"),
        P(),
        P("wide", "col", None, None, None),
        P("wide", "col", None, None),
        P("wide", "col"),
    )
    return jax.shard_map(
        local, mesh=mesh, in_specs=placed, out_specs=(P(None, "wide", "col"), P()), check_vma=False
    )
```

```python
import functools
import math

import jax
import jax.numpy as jnp
import ml_dtypes
import numpy as np
from jax import lax
from jax.experimental import pallas as pl
from jax.experimental.pallas import tpu as pltpu
from jax.sharding import PartitionSpec as P

MESH = pl.DeviceIdType.MESH
F32 = jnp.float32
BF16 = jnp.bfloat16
PATCH = 128
TILE = 512
EXT = TILE + PATCH
MODES = 4
RING = 16
PLANES = 2 * MODES + 1
ROWS = PATCH // RING
PAIR = 2
CHUNKS = 5
ROUTES = 3
DIRECT = PATCH - ROUTES * 8 * CHUNKS
GROUP = 4
FIRST = 16
EARLY = 24
REST = TILE - PATCH
INSIDE = TILE - PATCH

VMEM_SPEC = pl.BlockSpec(memory_space=pltpu.VMEM)
SMEM_SPEC = pl.BlockSpec(memory_space=pltpu.SMEM)
ANY_SPEC = pl.BlockSpec(memory_space=pl.ANY)


def left_table():
    indices = np.arange(PATCH)
    angles = (indices[:, None] * indices[None, :] % PATCH) * (2.0 * math.pi / PATCH)
    cosine = np.cos(angles) / math.sqrt(PATCH)
    sine = -np.sin(angles) / math.sqrt(PATCH)
    whole = np.block([[cosine, -sine], [sine, cosine]])
    return whole.astype(np.float32).astype(ml_dtypes.bfloat16)


def plan_kernel(pos_ref, count_ref, meta_ref):
    count = count_ref[0, 0]
    slots = []
    inner_count, upper_count = jnp.int32(0), jnp.int32(0)
    for s in range(pos_ref.shape[1]):
        row, at = pos_ref[0, s], pos_ref[1, s]
        live = s < count
        upper = live & (row <= INSIDE)
        inner = upper & (at <= INSIDE)
        slots.append((row, at, live, upper, inner))
        inner_count = inner_count + jnp.where(inner, 1, 0)
        upper_count = upper_count + jnp.where(upper, 1, 0)
    low, middle, high = jnp.int32(0), inner_count, upper_count
    for s, (row, at, live, upper, inner) in enumerate(slots):
        outer = upper & jnp.logical_not(inner)
        place = jnp.where(inner, low, jnp.where(outer, middle, jnp.where(live, high, s)))
        meta_ref[0, place] = row
        meta_ref[1, place] = at
        meta_ref[3, place] = s
        low = low + jnp.where(inner, 1, 0)
        middle = middle + jnp.where(outer, 1, 0)
        high = high + jnp.where(live & jnp.logical_not(upper), 1, 0)
    for line in (0, 1, 3):
        meta_ref[line, pos_ref.shape[1]] = 0
    meta_ref[2, 0] = count
    meta_ref[2, 1] = inner_count
    meta_ref[2, 2] = upper_count


def plan(positions, slot_counts):
    return pl.pallas_call(
        plan_kernel,
        out_shape=jax.ShapeDtypeStruct((8, PATCH), jnp.int32),
        in_specs=[SMEM_SPEC] * 2,
        out_specs=SMEM_SPEC,
        name="plan",
    )(positions, slot_counts)


def lanes_of():
    return lax.broadcasted_iota(jnp.int32, (PATCH, PATCH), 1)


def both_sides(left, stacked, right_side):
    half = jnp.dot(left, stacked, preferred_element_type=F32).astype(BF16)
    lanes = [slice(PATCH * m, PATCH * (m + 1)) for m in range(MODES)]
    turned = jnp.concatenate(
        [jnp.concatenate([half[:PATCH, at], half[PATCH:, at]], 1) for at in lanes], 0
    )
    return jnp.dot(turned, right_side, preferred_element_type=F32)


def stack(re, im):
    return jnp.concatenate([jnp.concatenate(re, 1), jnp.concatenate(im, 1)], 0)


def parts(values, m):
    rows = slice(PATCH * m, PATCH * (m + 1))
    return values[rows, :PATCH], values[rows, PATCH:]


def solve(slots, ext, last, probe_ref, lt, rt, amp_ref, pg_ref):
    lane = lanes_of()
    patches_of, waves = [], []
    for s, row, at, live in slots:
        ct, shift = lax.shift_right_logical(at, 7), lax.bitwise_and(at, 127)
        back = lax.bitwise_and(PATCH - shift, 127)
        beside = jnp.minimum(ct + 1, last)
        rows = pl.ds(row, PATCH)
        patch = []
        for p in range(2):
            joined = jnp.where(lane >= shift, ext[p, ct, rows, :], ext[p, beside, rows, :])
            patch.append(pltpu.roll(joined, back, 1))
        patches_of.append(patch)
        re, im = [], []
        for m in range(MODES):
            pr, pi = probe_ref[0, m], probe_ref[1, m]
            re.append((pr * patch[0] - pi * patch[1]).astype(BF16))
            im.append((pr * patch[1] + pi * patch[0]).astype(BF16))
        waves.append(stack(re, im))
    fars = [both_sides(lt, wave, rt) for wave in waves]
    residuals = []
    for (s, row, at, live), far in zip(slots, fars):
        intensity = jnp.zeros((PATCH, PATCH), F32)
        for m in range(MODES):
            fr, fi = parts(far, m)
            intensity = intensity + fr * fr + fi * fi
        measured = amp_ref[s].astype(F32)
        factor = (measured * lax.rsqrt(jnp.maximum(intensity, 1.0)) - 1.0) * live
        re, im = [], []
        for m in range(MODES):
            fr, fi = parts(far, m)
            re.append((fr * factor).astype(BF16))
            im.append((fi * factor).astype(BF16))
        residuals.append(stack(re, im))
    updates = [both_sides(rt, residual, lt) for residual in residuals]
    for m in range(MODES):
        sum_re, sum_im = pg_ref[m], pg_ref[MODES + m]
        for patch, update in zip(patches_of, updates):
            ur, ui = parts(update, m)
            sum_re = sum_re + patch[0] * ur + patch[1] * ui
            sum_im = sum_im + patch[0] * ui - patch[1] * ur
        pg_ref[m] = sum_re
        pg_ref[MODES + m] = sum_im
    lit = pg_ref[2 * MODES]
    for (s, row, at, live), patch in zip(slots, patches_of):
        lit = lit + live * (patch[0] * patch[0] + patch[1] * patch[1])
    pg_ref[2 * MODES] = lit
    grads = []
    for update in updates:
        grad_re = jnp.zeros((PATCH, PATCH), F32)
        grad_im = grad_re
        for m in range(MODES):
            pr, pi = probe_ref[0, m], probe_ref[1, m]
            ur, ui = parts(update, m)
            grad_re = grad_re + pr * ur + pi * ui
            grad_im = grad_im + pr * ui - pi * ur
        grads.append((grad_re, grad_im))
    return grads


def remote(source, dest, sent, got, target):
    return pltpu.make_async_remote_copy(
        source, dest, sent, got, device_id=target, device_id_type=MESH
    )


def greet(barrier, target):
    pl.semaphore_signal(barrier, inc=1, device_id=target, device_id_type=MESH)


def halo_in_kernel(
    obj, meta, meta_ref, probe, left_side, right_side, amp,
    right, lower, diag, meta_above, meta_left, meta_diag, early, pg_ref,
    ext, wide_ext, amp_ref, probe_ref, lt_ref, rt_ref, early_ref, passing, fetched, stored,
    sent, got, sent_to, got_to, sent_on, got_on,
):
    w = lax.axis_index("wide")
    c = lax.axis_index("col")
    y, k = lax.rem(w, 4), lax.div(w, 4)
    above, below = lax.rem(w + 15, 16), lax.rem(w + 1, 16)
    before, after = lax.rem(c + 15, 16), lax.rem(c + 1, 16)
    far_send, far_get = (y == 0) & (k > 0), (y == 3) & (k < 3)
    relays = (y > 0) & (k > 0)
    route = jnp.maximum(y - 1, 0)
    onward_to = lax.rem(w + 15 - y, 16)
    barrier = pltpu.get_barrier_semaphore()
    for target in (
        (w, after), (below, c), (below, after), (w, before), (above, c), (above, before)
    ):
        greet(barrier, target)
    pl.when(relays & (y > 1))(lambda: greet(barrier, (lax.rem(w + 16 - y, 16), c)))

    @pl.when(far_get)
    def _():
        for r in range(ROUTES):
            greet(barrier, (lax.rem(w + 2 + r, 16), c))

    inward = [
        pltpu.make_async_copy(source, dest, fetched.at[10 + j])
        for j, (source, dest) in enumerate(
            ((amp, amp_ref), (probe, probe_ref), (left_side, lt_ref), (right_side, rt_ref))
        )
    ]
    for ct in range(4):
        inward.append(pltpu.make_async_copy(
            obj.at[:, :, pl.ds(PATCH * ct, PATCH)], ext.at[:, ct], fetched.at[ct]
        ))
    beside = [
        pltpu.make_async_copy(
            obj.at[:, :, pl.ds(PATCH * ct, PATCH)], wide_ext.at[:, ct], fetched.at[5 + ct]
        )
        for ct in range(4)
    ]
    for copy in inward + beside:
        copy.start()
    pl.semaphore_wait(barrier, 6 + jnp.where(far_send, 2, jnp.where(relays, 1, 0)))

    def strip(first, rows):
        return pl.ds(first, rows)

    def to_relay(r, j):
        at = strip(DIRECT + 8 * (r * CHUNKS + j), 8)
        return remote(
            obj.at[:, at, :], passing.at[j], sent_to.at[r * CHUNKS + j], got_to.at[j],
            (lax.rem(w + r + 1, 16), c),
        )

    def onward(r, j):
        start = pl.multiple_of(DIRECT + 8 * (r * CHUNKS + j), 8)
        return remote(
            passing.at[j], lower.at[:, strip(start, 8), :],
            sent_on.at[j], got_on.at[r * CHUNKS + j], (onward_to, c),
        )

    @pl.when(far_send)
    def _():
        for j in range(CHUNKS):
            for r in reversed(range(ROUTES)):
                to_relay(r, j).start()

    ups, downs = w > 0, w < 15
    lefts, rights = c > 0, c < 15
    near_send = ups & jnp.logical_not(far_send)
    near_get = downs & jnp.logical_not(far_get)
    top = pl.ds(0, PATCH)
    some, rest = strip(0, DIRECT), strip(DIRECT, PATCH - DIRECT)
    plain = (
        (meta, meta_above, (below, c), downs, ups),
        (meta, meta_left, (w, after), rights, lefts),
        (meta, meta_diag, (below, after), downs & rights, ups & lefts),
        (obj.at[:, some, :], lower.at[:, some, :], (above, c), ups, downs),
        (obj.at[:, rest, :], lower.at[:, rest, :], (above, c), near_send, near_get),
        (obj.at[:, top, top], diag, (above, before), ups & lefts, downs & rights),
        (obj.at[:, :, top], wide_ext.at[:, 4], (w, before), lefts, rights),
    )
    made = []
    for j, (source, dest, target, sends, gets) in enumerate(plain):
        copy = remote(source, dest, sent.at[j], got.at[j], target)
        pl.when(sends)(copy.start)
        made.append((copy, sends, gets))

    pg_ref[...] = jnp.zeros(pg_ref.shape, F32)
    inner = meta_ref[2, 1]
    for copy in inward:
        copy.wait()
    lt = lt_ref[...]
    rt = rt_ref[...]

    def put(index):
        pair = pl.ds(index * GROUP, GROUP)
        return pltpu.make_async_copy(early_ref.at[pair], early.at[pair], stored.at[index])

    def solve_some(index, first_slot, live_slots, tiles, last, columns):
        slots = []
        for u in range(GROUP):
            j = first_slot + u
            row, at = jnp.minimum(meta_ref[0, j], INSIDE), jnp.minimum(meta_ref[1, j], columns)
            slots.append((meta_ref[3, j], row, at, (j < live_slots).astype(F32)))
        grads = solve(slots, tiles, last, probe_ref, lt, rt, amp_ref, pg_ref)
        for u, (grad_re, grad_im) in enumerate(grads):
            early_ref[index * GROUP + u, 0] = grad_re
            early_ref[index * GROUP + u, 1] = grad_im
        put(index).start()

        for half in range(2):
            @pl.when(relays & (2 * index + half < CHUNKS))
            def _(j=2 * index + half):
                to_relay(0, j).wait_recv()
                onward(route, j).start()

    def first_step(index, carry):
        solve_some(index, index * GROUP, inner, ext, 3, INSIDE)
        return carry

    lax.fori_loop(0, FIRST // GROUP, first_step, 0)
    for copy in beside:
        copy.wait()
    pl.when(rights)(made[-1][0].wait_recv)

    @pl.when(c == 15)
    def _():
        wide_ext[:, 4] = jnp.zeros((2, TILE, PATCH), F32)

    keep = pltpu.make_async_copy(wide_ext.at[:, 4], right, fetched.at[9])
    keep.start()
    base = jnp.minimum(inner, FIRST)
    upper = meta_ref[2, 2]

    def next_step(index, carry):
        solve_some(index, base + index * GROUP - FIRST, upper, wide_ext, 4, TILE - 1)
        return carry

    lax.fori_loop(FIRST // GROUP, EARLY // GROUP, next_step, 0)
    keep.wait()
    for index in range(EARLY // GROUP):
        put(index).wait()
    for copy, sends, gets in made[:-1]:
        pl.when(gets)(copy.wait_recv)
        pl.when(sends)(copy.wait_send)
    pl.when(lefts)(made[-1][0].wait_send)

    @pl.when(far_get)
    def _():
        for r in range(ROUTES):
            for j in range(CHUNKS):
                onward(r, j).wait_recv()

    @pl.when(relays)
    def _():
        for j in range(CHUNKS):
            onward(0, j).wait_send()

    @pl.when(far_send)
    def _():
        for r in range(ROUTES):
            for j in range(CHUNKS):
                to_relay(r, j).wait_send()


def halo_in(obj, meta, probe, tables, amp):
    note = jax.ShapeDtypeStruct(meta.shape, meta.dtype)
    made = pl.pallas_call(
        halo_in_kernel,
        out_shape=[
            jax.ShapeDtypeStruct((2, TILE, PATCH), F32),
            jax.ShapeDtypeStruct((2, PATCH, TILE), F32),
            jax.ShapeDtypeStruct((2, PATCH, PATCH), F32),
            note,
            note,
            note,
            jax.ShapeDtypeStruct((EARLY, 2, PATCH, PATCH), F32),
            jax.ShapeDtypeStruct((PLANES, PATCH, PATCH), F32),
        ],
        in_specs=[ANY_SPEC] * 2 + [SMEM_SPEC] + [ANY_SPEC] * 4,
        out_specs=[ANY_SPEC] * 7 + [VMEM_SPEC],
        scratch_shapes=[
            pltpu.VMEM((2, 4, TILE, PATCH), F32),
            pltpu.VMEM((2, 5, TILE, PATCH), F32),
            pltpu.VMEM(amp.shape, amp.dtype),
            pltpu.VMEM(probe.shape, F32),
            pltpu.VMEM(tables[0].shape, BF16),
            pltpu.VMEM(tables[0].shape, BF16),
            pltpu.VMEM((EARLY, 2, PATCH, PATCH), F32),
            pltpu.VMEM((CHUNKS, 2, 8, TILE), F32),
            pltpu.SemaphoreType.DMA((14,)),
            pltpu.SemaphoreType.DMA((EARLY // GROUP,)),
        ]
        + [pltpu.SemaphoreType.DMA((7,))] * 2
        + [pltpu.SemaphoreType.DMA((ROUTES * CHUNKS,)), pltpu.SemaphoreType.DMA((CHUNKS,))]
        + [pltpu.SemaphoreType.DMA((CHUNKS,)), pltpu.SemaphoreType.DMA((ROUTES * CHUNKS,))],
        compiler_params=pltpu.CompilerParams(
            collective_id=1, has_side_effects=True, vmem_limit_bytes=56 * 2**20
        ),
        name="halo_in",
    )(obj, meta, meta, probe, *tables, amp)
    return made[:6], made[6], made[7]


def patches_kernel(
    meta, meta_above, meta_left, meta_diag, probe, left_side, right_side,
    early_pg, amp, early, obj, right, lower, diag,
    pre, grad, weight, pg,
    meta_ref, above_ref, left_ref, diag_ref, probe_ref, lt_ref, rt_ref, pg_ref, amp_ref, early_ref,
    ext, grad_ref, spread, inner_ref, sems, stored,
):
    copies = []

    def fetch(source, dest):
        copy = pltpu.make_async_copy(source, dest, sems.at[len(copies)])
        copy.start()
        copies.append(copy)

    fetch(probe, probe_ref)
    fetch(meta, meta_ref)
    fetch(meta_above, above_ref)
    fetch(meta_left, left_ref)
    fetch(meta_diag, diag_ref)
    at_first = len(copies)
    fetch(early, early_ref)
    fetch(left_side, lt_ref)
    fetch(right_side, rt_ref)
    fetch(early_pg, pg_ref)
    fetch(amp, amp_ref)
    for ct in range(4):
        lanes = pl.ds(PATCH * ct, PATCH)
        fetch(obj.at[:, :, lanes], ext.at[:, ct, pl.ds(0, TILE), :])
        fetch(lower.at[:, :, lanes], ext.at[:, ct, pl.ds(TILE, PATCH), :])
    fetch(right, ext.at[:, 4, pl.ds(0, TILE), :])
    fetch(diag, ext.at[:, 4, pl.ds(TILE, PATCH), :])
    grad_ref[...] = jnp.zeros(grad_ref.shape, F32)
    spread[...] = jnp.zeros(spread.shape, F32)
    for copy in copies[:at_first]:
        copy.wait()
    w = lax.axis_index("wide")
    c = lax.axis_index("col")
    lane = lanes_of()
    count = meta_ref[2, 0]
    base = jnp.minimum(meta_ref[2, 1], FIRST)
    done = jnp.minimum(meta_ref[2, 2], base + EARLY - FIRST)
    power = jnp.sum(probe_ref[...] * probe_ref[...], axis=(0, 1))

    def scatter(ref, row, at, value):
        ct, shift = lax.shift_right_logical(at, 7), lax.bitwise_and(at, 127)
        turned = pltpu.roll(value, shift, 1)
        first = lane >= shift
        zero = jnp.zeros_like(turned)
        rows = pl.ds(row, PATCH)
        ref[ct, rows, :] += jnp.where(first, turned, zero)
        ref[ct + 1, rows, :] += jnp.where(first, zero, turned)

    for ref, there, down, side in (
        (meta_ref, None, 0, 0),
        (above_ref, w > 0, TILE, 0),
        (left_ref, c > 0, 0, TILE),
        (diag_ref, (w > 0) & (c > 0), TILE, TILE),
    ):
        live_there = ref[2, 0] if there is None else jnp.where(there, ref[2, 0], 0)

        def weigh(index, carry, ref=ref, down=down, side=side, live_there=live_there):
            for s in [4 * index + u for u in range(4)]:
                row, at = ref[0, s] + (PATCH - down), ref[1, s] + (PATCH - side)
                live = s < live_there
                if down or side:
                    touches = live
                    if down:
                        touches = touches & (row > 0)
                    if side:
                        touches = touches & (at > 0)
                    pl.when(touches)(functools.partial(scatter, spread, row, at, power))
                else:
                    scatter(spread, row, at, power * live.astype(F32))
            return carry

        lax.fori_loop(0, (live_there + 3) // 4, weigh, 0)
    weights_out = pltpu.make_async_copy(
        spread.at[pl.ds(1, 4), pl.ds(PATCH, TILE), :], weight, stored.at[0]
    )
    weights_out.start()
    copies[at_first].wait()

    def place(index, carry):
        for j in [4 * index + u for u in range(4)]:
            held = jnp.minimum(jnp.where(j < base, j, j - base + FIRST), EARLY - 1)
            for p in range(2):
                value = jnp.where(j < done, early_ref[held, p], 0.0)
                scatter(grad_ref.at[p], meta_ref[0, j], meta_ref[1, j], value)
        return carry

    lax.fori_loop(0, (done + 3) // 4, place, 0)
    for copy in copies[at_first + 1 :]:
        copy.wait()

    @pl.when(w == 15)
    def _():
        ext[:, :, TILE:, :] = jnp.zeros((2, 5, PATCH, PATCH), F32)

    @pl.when(c == 15)
    def _():
        ext[:, 4, :, :] = jnp.zeros((2, EXT, PATCH), F32)

    lt = lt_ref[...]
    rt = rt_ref[...]

    def steps(first_slot, size, number):
        def step(index, carry):
            slots = []
            for u in range(size):
                j = first_slot + index * size + u
                live = (j < count).astype(F32)
                slots.append((meta_ref[3, j], meta_ref[0, j], meta_ref[1, j], live))
            grads = solve(slots, ext, 4, probe_ref, lt, rt, amp_ref, pg_ref)
            for (s, row, at, live), (grad_re, grad_im) in zip(slots, grads):
                scatter(grad_ref.at[0], row, at, grad_re)
                scatter(grad_ref.at[1], row, at, grad_im)
            return carry

        lax.fori_loop(0, number, step, 0)

    whole = (count - done) // GROUP
    left_over = done + whole * GROUP
    steps(done, GROUP, whole)
    steps(left_over, PAIR, (count - left_over + PAIR - 1) // PAIR)
    outward = [weights_out]
    low, top, between = pl.ds(TILE, PATCH), pl.ds(0, PATCH), pl.ds(PATCH, REST)
    for source, dest in (
        (pg_ref, pg),
        (grad_ref.at[:, :, low, :], grad.at[:, :, low, :]),
        (grad_ref.at[:, 4, pl.ds(0, TILE), :], grad.at[:, 4, pl.ds(0, TILE), :]),
        (grad_ref.at[:, pl.ds(0, 4), top, :], grad.at[:, pl.ds(0, 4), top, :]),
        (grad_ref.at[:, 0, between, :], grad.at[:, 0, between, :]),
    ):
        copy = pltpu.make_async_copy(source, dest, stored.at[len(outward)])
        copy.start()
        outward.append(copy)
    inside = slice(PATCH, TILE)
    for ct in range(1, 4):
        scale = spread[ct + 1, PATCH + PATCH : PATCH + TILE, :] + 1.0
        lanes = slice(PATCH * (ct - 1), PATCH * ct)
        for p in range(2):
            inner_ref[p, :, lanes] = ext[p, ct, inside, :] + grad_ref[p, ct, inside, :] / scale
    copy = pltpu.make_async_copy(
        inner_ref, pre.at[:, between, between], stored.at[len(outward)]
    )
    copy.start()
    for copy in outward + [copy]:
        copy.wait()


def patches(metas, probe, tables, amp, early, early_pg, obj, right, lower, diag):
    return pl.pallas_call(
        patches_kernel,
        out_shape=[
            jax.ShapeDtypeStruct((2, TILE, TILE), F32),
            jax.ShapeDtypeStruct((2, 5, EXT, PATCH), F32),
            jax.ShapeDtypeStruct((4, TILE, PATCH), F32),
            jax.ShapeDtypeStruct((PLANES, PATCH, PATCH), F32),
        ],
        in_specs=[ANY_SPEC] * 14,
        out_specs=[ANY_SPEC] * 4,
        scratch_shapes=[pltpu.SMEM(metas[0].shape, jnp.int32)] * 4
        + [
            pltpu.VMEM(probe.shape, F32),
            pltpu.VMEM(tables[0].shape, BF16),
            pltpu.VMEM(tables[0].shape, BF16),
            pltpu.VMEM((PLANES, PATCH, PATCH), F32),
            pltpu.VMEM(amp.shape, amp.dtype),
            pltpu.VMEM(early.shape, early.dtype),
            pltpu.VMEM((2, 5, EXT, PATCH), F32),
            pltpu.VMEM((2, 5, EXT, PATCH), F32),
            pltpu.VMEM((6, EXT + PATCH, PATCH), F32),
            pltpu.VMEM((2, REST, REST), F32),
            pltpu.SemaphoreType.DMA((20,)),
            pltpu.SemaphoreType.DMA((8,)),
        ],
        compiler_params=pltpu.CompilerParams(vmem_limit_bytes=56 * 2**20),
        name="patches",
    )(*metas, probe, *tables, early_pg, amp, early, obj, right, lower, diag)


def exchange_kernel(
    pg_far, grad, total, from_above, from_left, from_diag,
    pg, loaded, buf0, red0, buf1, red1, buf2, buf3, own, res, passing,
    s0, r0, s1, r1, s2, r2, s3, r3, s4, r4, s5, r5, s6, r6, sh, rh, sent_to, got_to, sent_on, got_on,
):
    w = lax.axis_index("wide")
    c = lax.axis_index("col")
    y, k = lax.rem(w, 4), lax.div(w, 4)
    core, chip = lax.rem(c, 2), lax.div(c, 2)
    sibling = (w, 2 * chip + 1 - core)
    above, below = lax.rem(w + 15, 16), lax.rem(w + 1, 16)
    before, after = lax.rem(c + 15, 16), lax.rem(c + 1, 16)
    far_send, far_get = (y == 3) & (k < 3), (y == 0) & (k > 0)
    relays = (y < 3) & (k < 3)
    route = jnp.maximum(2 - y, 0)
    onward_to = lax.rem(w + 4 - y, 16)

    def rows(index, half):
        return pl.ds(pl.multiple_of(index * ROWS + half * (PATCH // 2), ROWS), ROWS)

    def planes(index):
        return pl.ds(index * 3, 3)

    chips = [(w, lax.rem(chip + d, 8) * 2 + core) for d in range(1, 8)]
    along_y = [(k * 4 + lax.rem(y + d, 4), c) for d in range(1, 4)]
    along_z = [(lax.rem(w + 4 * d, 16), c) for d in range(1, 4)]
    barrier = pltpu.get_barrier_semaphore()
    for target in [sibling] + chips + along_y + along_z:
        greet(barrier, target)
    for target in ((w, before), (above, c), (above, before)):
        greet(barrier, target)

    @pl.when(far_get)
    def _():
        for r in range(ROUTES):
            greet(barrier, (lax.rem(w + 12 + r, 16), c))

    load = pltpu.make_async_copy(pg_far, pg, loaded)
    load.start()
    pl.semaphore_wait(barrier, 17 + jnp.where(relays, 1, 0))

    zeroth = []
    for d in range(1, 9):
        p = lax.rem(chip + d, 8)
        copy = remote(pg_far.at[:, rows(p, 1 - core), :], buf0.at[d - 1], s0.at[d - 1], r0.at[d - 1], sibling)
        copy.start()
        zeroth.append(copy)

    def to_relay(r, j):
        at = TILE + DIRECT + 8 * (r * CHUNKS + j)
        return remote(
            grad.at[:, pl.ds(0, 4), pl.ds(at, 8), :], passing.at[j],
            sent_to.at[r * CHUNKS + j], got_to.at[j], (lax.rem(w + 15 - r, 16), c),
        )

    def onward(r, j):
        at = pl.multiple_of(DIRECT + 8 * (r * CHUNKS + j), 8)
        return remote(
            passing.at[j], from_above.at[:, :, pl.ds(at, 8), :],
            sent_on.at[j], got_on.at[r * CHUNKS + j], (onward_to, c),
        )

    def pass_on(chunks):
        @pl.when(relays)
        def _():
            for j in chunks:
                to_relay(0, j).wait_recv()
                onward(route, j).start()

    ups, downs = w > 0, w < 15
    lefts, rights = c > 0, c < 15
    near_send = downs & jnp.logical_not(far_send)
    near_get = ups & jnp.logical_not(far_get)
    strips = []

    def post(source, dest, target, sends, gets):
        copy = remote(source, dest, sh.at[len(strips)], rh.at[len(strips)], target)
        pl.when(sends)(copy.start)
        strips.append((copy, sends, gets))

    def post_rows(first, size, sends, gets):
        post(
            grad.at[:, pl.ds(0, 4), pl.ds(TILE + first, size), :],
            from_above.at[:, :, pl.ds(first, size), :], (below, c), sends, gets,
        )

    def post_columns(first, size):
        at = pl.ds(first, size)
        post(grad.at[:, 4, at, :], from_left.at[:, at, :], (w, after), rights, lefts)

    @pl.when(far_send)
    def _():
        for j in range(CHUNKS):
            for r in reversed(range(ROUTES)):
                to_relay(r, j).start()

    post_rows(DIRECT, 16, near_send, near_get)
    load.wait()
    first = []
    for d in range(1, 8):
        p = lax.rem(chip + d, 8)
        zeroth[d - 1].wait_recv()
        red0[d - 1] = pg[:, rows(p, core), :] + buf0[d - 1]
        copy = remote(red0.at[d - 1], buf1.at[d], s1.at[d], r1.at[d], chips[d - 1])
        copy.start()
        first.append(copy)
    zeroth[7].wait_recv()
    acc = pg[:, rows(chip, core), :] + buf0[7]

    post_rows(DIRECT + 16, 32, near_send, near_get)
    post(
        grad.at[:, 4, pl.ds(TILE, PATCH), :], from_diag, (below, after),
        downs & rights, ups & lefts,
    )
    pass_on(range(2))
    for d in range(1, 8):
        first[d - 1].wait_recv()
        acc = acc + buf1[d]
    red1[pl.ds(0, PLANES)] = acc
    red1[pl.ds(PLANES, 3)] = jnp.zeros((3, ROWS, PATCH), F32)
    second = []
    for d in range(1, 4):
        copy = remote(
            red1.at[planes(lax.rem(y + d, 4))], buf2.at[d], s2.at[d], r2.at[d], along_y[d - 1]
        )
        copy.start()
        second.append(copy)
    pass_on(range(2, CHUNKS))
    post_columns(0, 256)
    acc = red1[planes(y)]
    for d in range(1, 4):
        second[d - 1].wait_recv()
        acc = acc + buf2[d]
    buf3[k] = acc
    third = []
    for d in range(1, 4):
        copy = remote(buf3.at[k], buf3.at[k], s3.at[d], r3.at[d], along_z[d - 1])
        copy.start()
        third.append(copy)
    post_columns(256, 256)
    for d in range(1, 4):
        p = lax.rem(k + 4 - d, 4)
        remote(buf3.at[p], buf3.at[p], s3.at[d], r3.at[d], along_z[d - 1]).wait_recv()
    own[planes(y)] = buf3[0] + buf3[1] + buf3[2] + buf3[3]
    fourth = []
    for d in range(1, 4):
        copy = remote(own.at[planes(y)], own.at[planes(y)], s4.at[d], r4.at[d], along_y[d - 1])
        copy.start()
        fourth.append(copy)
    for d in range(1, 4):
        p = planes(lax.rem(y + 4 - d, 4))
        remote(own.at[p], own.at[p], s4.at[d], r4.at[d], along_y[d - 1]).wait_recv()
    lit = own[2 * MODES]
    res[...] = own[pl.ds(0, 2 * MODES)] / jnp.sqrt(lit + 1.0)[None]

    mine = rows(chip, core)
    fifth, sixth = [], []
    for d in range(1, 8):
        copy = remote(res, total.at[:, mine, :], s5.at[d], r5.at[d], chips[d - 1])
        copy.start()
        fifth.append(copy)
    copy = remote(res, total.at[:, mine, :], s6.at[0], r6.at[0], sibling)
    copy.start()
    sixth.append(copy)
    total[:, mine, :] = res[...]
    post_rows(DIRECT + 48, 72, near_send, near_get)
    post_rows(0, DIRECT, downs, ups)
    for d in range(1, 8):
        at = rows(lax.rem(chip + 8 - d, 8), core)
        remote(res, total.at[:, at, :], s5.at[d], r5.at[d], chips[d - 1]).wait_recv()
        copy = remote(total.at[:, at, :], total.at[:, at, :], s6.at[d], r6.at[d], sibling)
        copy.start()
        sixth.append(copy)
    for copy in zeroth + first + second + third + fourth + fifth:
        copy.wait_send()
    for d in range(8):
        at = rows(lax.rem(chip + 8 - d, 8), 1 - core)
        remote(res, total.at[:, at, :], s6.at[d], r6.at[d], sibling).wait_recv()
    for copy in sixth:
        copy.wait_send()
    for copy, sends, gets in strips:
        pl.when(gets)(copy.wait_recv)
        pl.when(sends)(copy.wait_send)

    @pl.when(far_get)
    def _():
        for r in range(ROUTES):
            for j in range(CHUNKS):
                onward(r, j).wait_recv()

    @pl.when(relays)
    def _():
        for j in range(CHUNKS):
            onward(0, j).wait_send()

    @pl.when(far_send)
    def _():
        for r in range(ROUTES):
            for j in range(CHUNKS):
                to_relay(r, j).wait_send()


def exchange(pg, grad):
    eight = pltpu.SemaphoreType.DMA((8,))
    four = pltpu.SemaphoreType.DMA((4,))
    many = pltpu.SemaphoreType.DMA((ROUTES * CHUNKS,))
    few = pltpu.SemaphoreType.DMA((CHUNKS,))
    return pl.pallas_call(
        exchange_kernel,
        out_shape=[
            jax.ShapeDtypeStruct((2 * MODES, PATCH, PATCH), F32),
            jax.ShapeDtypeStruct((2, 4, PATCH, PATCH), F32),
            jax.ShapeDtypeStruct((2, TILE, PATCH), F32),
            jax.ShapeDtypeStruct((2, PATCH, PATCH), F32),
        ],
        in_specs=[ANY_SPEC] * 2,
        out_specs=[VMEM_SPEC] + [ANY_SPEC] * 3,
        scratch_shapes=[
            pltpu.VMEM((PLANES, PATCH, PATCH), F32),
            pltpu.SemaphoreType.DMA,
            pltpu.VMEM((8, PLANES, ROWS, PATCH), F32),
            pltpu.VMEM((8, PLANES, ROWS, PATCH), F32),
            pltpu.VMEM((8, PLANES, ROWS, PATCH), F32),
            pltpu.VMEM((12, ROWS, PATCH), F32),
            pltpu.VMEM((4, 3, ROWS, PATCH), F32),
            pltpu.VMEM((4, 3, ROWS, PATCH), F32),
            pltpu.VMEM((12, ROWS, PATCH), F32),
            pltpu.VMEM((2 * MODES, ROWS, PATCH), F32),
            pltpu.VMEM((CHUNKS, 2, 4, 8, PATCH), F32),
        ]
        + [eight] * 4
        + [four] * 6
        + [eight] * 4
        + [eight] * 2
        + [many, few, few, many],
        compiler_params=pltpu.CompilerParams(
            collective_id=2, has_side_effects=True, vmem_limit_bytes=56 * 2**20
        ),
        name="exchange",
    )(pg, grad)


def finish_kernel(
    pre, obj, grad, weight, total, from_above, from_left, from_diag, new, direction,
    obj_top, obj_left, grad_top, grad_left, weight_top, weight_left, above, left, corner,
    new_top, new_left, held, sems, stored,
):
    del pre
    top, between, tiles = pl.ds(0, PATCH), pl.ds(PATCH, REST), pl.ds(0, 4)
    copies = []
    for source, dest in (
        (obj.at[:, between, top], obj_left),
        (grad.at[:, 0, between, :], grad_left),
        (weight.at[0, between, :], weight_left),
        (from_left, left),
        (total, held),
        (obj.at[:, top, :], obj_top),
        (grad.at[:, tiles, top, :], grad_top),
        (weight.at[:, top, :], weight_top),
        (from_above, above),
        (from_diag, corner),
    ):
        copy = pltpu.make_async_copy(source, dest, sems.at[len(copies)])
        copy.start()
        copies.append(copy)
    got_above, got_left = lax.axis_index("wide") > 0, lax.axis_index("col") > 0
    for copy in copies[:4]:
        copy.wait()
    scale = weight_left[...] + 1.0
    for p in range(2):
        sums = grad_left[p] + jnp.where(got_left, left[p, PATCH:], 0.0)
        new_left[p] = obj_left[p] + sums / scale
    left_out = pltpu.make_async_copy(new_left, new.at[:, between, top], stored.at[1])
    left_out.start()
    copies[4].wait()
    whole = pltpu.make_async_copy(held, direction, stored.at[0])
    whole.start()
    for copy in copies[5:]:
        copy.wait()
    for ct in range(4):
        lanes = slice(PATCH * ct, PATCH * (ct + 1))
        scale = weight_top[ct] + 1.0
        for p in range(2):
            sums = grad_top[p, ct] + jnp.where(got_above, above[p, ct], 0.0)
            if ct == 0:
                sums = sums + jnp.where(got_left, left[p, :PATCH], 0.0)
                sums = sums + jnp.where(got_above & got_left, corner[p], 0.0)
            new_top[p, :, lanes] = obj_top[p, :, lanes] + sums / scale
    top_out = pltpu.make_async_copy(new_top, new.at[:, top, :], stored.at[2])
    top_out.start()
    for copy in (whole, left_out, top_out):
        copy.wait()


def finish(pre, obj, grad, weight, total, from_above, from_left, from_diag):
    return pl.pallas_call(
        finish_kernel,
        out_shape=[
            jax.ShapeDtypeStruct((2, TILE, TILE), F32),
            jax.ShapeDtypeStruct((2 * MODES, PATCH, PATCH), F32),
        ],
        in_specs=[ANY_SPEC] * 8,
        out_specs=[ANY_SPEC] * 2,
        input_output_aliases={0: 0},
        scratch_shapes=[
            pltpu.VMEM((2, PATCH, TILE), F32),
            pltpu.VMEM((2, REST, PATCH), F32),
            pltpu.VMEM((2, 4, PATCH, PATCH), F32),
            pltpu.VMEM((2, REST, PATCH), F32),
            pltpu.VMEM((4, PATCH, PATCH), F32),
            pltpu.VMEM((REST, PATCH), F32),
            pltpu.VMEM((2, 4, PATCH, PATCH), F32),
            pltpu.VMEM((2, TILE, PATCH), F32),
            pltpu.VMEM((2, PATCH, PATCH), F32),
            pltpu.VMEM((2, PATCH, TILE), F32),
            pltpu.VMEM((2, REST, PATCH), F32),
            pltpu.VMEM((2 * MODES, PATCH, PATCH), F32),
            pltpu.SemaphoreType.DMA((10,)),
            pltpu.SemaphoreType.DMA((3,)),
        ],
        compiler_params=pltpu.CompilerParams(vmem_limit_bytes=56 * 2**20),
        name="finish",
    )(pre, obj, grad, weight, total, from_above, from_left, from_diag)


def local(object_field, probe_modes, amplitude, positions, slot_counts):
    slots = positions.shape[2]
    amp = amplitude.reshape(slots, PATCH, PATCH)
    table = left_table()
    tables = (jnp.asarray(table), jnp.asarray(table.T))
    meta = plan(positions.reshape(slots, 2).T, slot_counts)
    (right, lower, diag, *others), early, early_pg = halo_in(
        object_field, meta, probe_modes, tables, amp
    )
    pre, grad, weight, pg = patches(
        (meta, *others), probe_modes, tables, amp, early, early_pg,
        object_field, right, lower, diag,
    )
    total, from_above, from_left, from_diag = exchange(pg, grad)
    new_object, direction = finish(
        pre, object_field, grad, weight, total, from_above, from_left, from_diag
    )
    return new_object, direction.reshape(probe_modes.shape)


def solution(mesh):
    placed = (
        P(None, "wide", "col"),
        P(),
        P("wide", "col", None, None, None),
        P("wide", "col", None, None),
        P("wide", "col"),
    )
    return jax.shard_map(
        local, mesh=mesh, in_specs=placed, out_specs=(P(None, "wide", "col"), P()), check_vma=False
    )
```
